32 devices in a mesh: section: 2 (over x), dp: 16 (over z, y, core).
Axes of the slice: x: 2, y: 2, z: 4, core: 2. Of those that a mesh axis runs over, the one named last changes fastest.
Arguments:
- center_input: bfloat16 [4, 512, 2, 300], P(None, 'dp'), may hold values from -6 to 6
- edge_input: bfloat16 [4, 512, 100, 300], P(None, 'dp'), may hold values from -6 to 6
- leaf_count: int32 [4, 512, 2], P(None, 'dp'), may hold values from 1 to 100, as said below
- leaf_mask: int32 [4, 512, 2, 100], P(None, 'dp'), may hold values 0 or 1
- w_query: bfloat16 [2, 300, 300], P('section'), may hold values from -0.375 to 0.375
- w_key: bfloat16 [2, 300, 300], P('section'), may hold values from -0.375 to 0.375
- w_value: bfloat16 [2, 300, 300], P('section'), may hold values from -0.375 to 0.375
- w_out: bfloat16 [2, 300, 300], P('section'), may hold values from -1.5 to 1.5
- gain_attn: float32 [2, 300], P('section'), may hold values from 0.1 to 1.9
- bias_attn: float32 [2, 300], P('section'), may hold values from -3 to 3
- w_up: bfloat16 [2, 300, 1200], P('section'), may hold values from -0.375 to 0.375
- w_down: bfloat16 [2, 1200, 300], P('section'), may hold values from -0.1875 to 0.1875
- gain_ffn: float32 [2, 300], P('section'), may hold values from 0.1 to 1.9
- bias_ffn: float32 [2, 300], P('section'), may hold values from -3 to 3
- w_edge: bfloat16 [2, 300, 300], P('section'), may hold values from -0.375 to 0.375
- center_cot: bfloat16 [4, 512, 2, 300], P(None, 'dp'), may hold values from -6 to 6
- edge_cot: bfloat16 [4, 512, 100, 300], P(None, 'dp'), may hold values from -6 to 6
Outputs:
- center_act: bfloat16 [2, 4, 512, 2, 300], P('section', None, 'dp')
- edge_act: bfloat16 [2, 4, 512, 100, 300], P('section', None, 'dp')
- center_grad: bfloat16 [2, 4, 512, 2, 300], P('section', None, 'dp')
- edge_grad: bfloat16 [2, 4, 512, 100, 300], P('section', None, 'dp')
- grad_query: float32 [2, 300, 300], P('section')
- grad_key: float32 [2, 300, 300], P('section')
- grad_value: float32 [2, 300, 300], P('section')
- grad_out: float32 [2, 300, 300], P('section')
- grad_gain_attn: float32 [2, 300], P('section')
- grad_bias_attn: float32 [2, 300], P('section')
- grad_up: float32 [2, 300, 1200], P('section')
- grad_down: float32 [2, 1200, 300], P('section')
- grad_gain_ffn: float32 [2, 300], P('section')
- grad_bias_ffn: float32 [2, 300], P('section')
- grad_edge: float32 [2, 300, 300], P('section')
- center_stats: float32 [2, 2, 300], P('section')
The draws below stay inside these ranges and needn't reach their ends.
Inputs may be any that keep to these rules, and one draw needn't show every extreme that they name: leaf_count[m, p, 0] is the pair's leaf count, at least 10 and at least 1; leaf_count[m, p, 1] keeps half of those leaves or more, rounded up; some pair has all 100 leaves.
All inputs are finite; a program needn't handle non-finite values. No bound on the sum of `leaf_mask` on one device may be relied on, other than what follows from the above.
Results may differ from the reference program's by a relative error of at most 0.02.
Values may be sent and summed in bfloat16 or wider, within the bound.
No kernel may reach another device: no remote copies, remote signals or barrier semaphores. Data moves between devices by JAX's collectives and lax.ppermute only.
A program may use at most 256 MiB of HBM per device.

```python
import math
import jax
import jax.numpy as jnp
from jax import lax

D = 300
FF = 1200
HEADS = 12
HEAD = 25
LEAVES = 100
MICRO = 4
PAIRS = 512


def draw_leaf_count(key, part):
    key = jax.random.fold_in(key, 7)
    key_full, key_cut, key_place = jax.random.split(key, 3)
    fewest = max(1, LEAVES // 10)
    complete = jax.random.randint(key_full, (MICRO * PAIRS,), fewest, LEAVES + 1)
    position = jax.random.randint(key_place, (), 0, MICRO * PAIRS)
    complete = jnp.where(jnp.arange(MICRO * PAIRS) == position, LEAVES, complete)
    halves = (complete + 1) // 2
    cutter = jax.random.randint(key_cut, (MICRO * PAIRS,), 0, 1 << 20)
    truncated = halves + cutter % (complete - halves + 1)
    return jnp.stack([complete, truncated], axis=-1).reshape(MICRO, PAIRS, 2).astype(jnp.int32)


def place_ends(result, stream_key, least, top_value):
    shape = result.shape
    place = [jax.random.randint(jax.random.fold_in(stream_key, axis), (), 0, shape[axis]) for axis in range(len(shape))]
    result = result.at[tuple(place)].set(least)
    longest = shape.index(max(shape))
    place[longest] = (place[longest] + 1) % shape[longest]
    return result.at[tuple(place)].set(top_value)


def level_of(rng, extent, cuts, least, high):
    gain = 1.0
    for axis_at, parts in cuts:
        heights = jax.random.uniform(jax.random.fold_in(jax.random.fold_in(rng, 6), axis_at), (parts,), jnp.float32, least / len(cuts), high / len(cuts))
        gain = gain * jnp.repeat(jnp.exp(heights), extent[axis_at] // parts).reshape((-1,) + (1,) * (len(extent) - 1 - axis_at))
    return gain


def gaussian(own_key, shape, width, bound, pieces=(), held_as=jnp.bfloat16):
    drawn = width * jax.random.normal(own_key, shape, jnp.float32)
    if pieces:
        drawn = drawn * level_of(own_key, shape, pieces, -0.22, 0.18)
    return jnp.clip(drawn, -bound, bound).astype(held_as)


def setup_inputs(seed: int = 0) -> dict:
    key_of = jax.random.split(jax.random.key(seed), 18)
    center_input = gaussian(key_of[0], (MICRO, PAIRS, 2, D), 1.0, 6.0, ((1, 16),))
    edge_input = gaussian(key_of[1], (MICRO, PAIRS, LEAVES, D), 1.0, 6.0, ((1, 16),))
    leaf_count = draw_leaf_count(jax.random.fold_in(key_of[17], 71), 0)
    leaf_mask = place_ends((jax.random.randint(key_of[3], (MICRO, PAIRS, 2, LEAVES), 0, 16) < 15).astype(jnp.int32), jax.random.fold_in(key_of[3], 1), 0, 1)
    w_query = gaussian(key_of[4], (2, D, D), D ** -0.5, 0.375, ((0, 2),))
    w_key = gaussian(key_of[5], (2, D, D), D ** -0.5, 0.375, ((0, 2),))
    w_value = gaussian(key_of[6], (2, D, D), D ** -0.5, 0.375, ((0, 2),))
    w_out = gaussian(key_of[7], (2, D, D), (D // 16) ** -0.5, 1.5, ((0, 2),))
    gain_attn = jnp.clip(1.0 + 0.18 * jax.random.normal(key_of[8], (2, D), jnp.float32), 0.1, 1.9)
    bias_attn = gaussian(key_of[9], (2, D), 0.5, 3.0, ((0, 2),), jnp.float32)
    w_up = gaussian(key_of[10], (2, D, FF), D ** -0.5, 0.375, ((0, 2),))
    w_down = gaussian(key_of[11], (2, FF, D), FF ** -0.5, 0.1875, ((0, 2),))
    gain_ffn = jnp.clip(1.0 + 0.18 * jax.random.normal(key_of[12], (2, D), jnp.float32), 0.1, 1.9)
    bias_ffn = gaussian(key_of[13], (2, D), 0.5, 3.0, ((0, 2),), jnp.float32)
    w_edge = gaussian(key_of[14], (2, D, D), D ** -0.5, 0.375, ((0, 2),))
    center_cot = gaussian(key_of[15], (MICRO, PAIRS, 2, D), 1.0, 6.0, ((1, 16),))
    edge_cot = gaussian(key_of[16], (MICRO, PAIRS, LEAVES, D), 1.0, 6.0, ((1, 16),))
    return {"center_input": center_input, "edge_input": edge_input, "leaf_count": leaf_count, "leaf_mask": leaf_mask, "w_query": w_query, "w_key": w_key, "w_value": w_value, "w_out": w_out, "gain_attn": gain_attn, "bias_attn": bias_attn, "w_up": w_up, "w_down": w_down, "gain_ffn": gain_ffn, "bias_ffn": bias_ffn, "w_edge": w_edge, "center_cot": center_cot, "edge_cot": edge_cot}


@jax.custom_vjp
def low(v):
    return lax.optimization_barrier(v.astype(jnp.bfloat16)).astype(jnp.float32)

@jax.custom_vjp
def low_back(v):
    return v

def low_keep(v):
    return (low(v), None)

def low_pass(kept, grad):
    return (grad,)

def back_keep(v):
    return (v, None)

def back_low(kept, grad):
    return (low(grad),)
low.defvjp(low_keep, low_pass)
low_back.defvjp(back_keep, back_low)
norm_eps = 1e-05

def product(pattern, left_arg, right_arg):
    return jnp.einsum(pattern, left_arg, right_arg, precision=lax.Precision.HIGHEST)

def normalize(values):
    centred = values - lax.optimization_barrier(jnp.mean(values, axis=-1, keepdims=True))
    return centred * lax.rsqrt(lax.optimization_barrier(jnp.mean(centred * centred, axis=-1, keepdims=True)) + norm_eps)

def both_ways(values):
    return low(low_back(values))

def star_layer(center, edges, live_leaves, w_query, w_key, w_value, w_out, gain_attn, bias_attn, w_up, w_down, gain_ffn, bias_ffn, w_edge):
    pair_count = edges.shape[0]
    leaves = edges.shape[1]
    model_width = edges.shape[2]
    score_scale = 1.0 / math.sqrt(HEAD)
    center_keep = low_back(center)
    edge_keep = low_back(edges)
    center_low = low(center_keep)
    edge_low = low(edge_keep)
    queries = both_ways(product('pvd,de->pve', center_low, w_query)).reshape(pair_count, 2, HEADS, HEAD)
    key_self = both_ways(product('pvd,de->pve', center_low, w_key)).reshape(pair_count, 2, HEADS, HEAD)
    value_self = both_ways(product('pvd,de->pve', center_low, w_value)).reshape(pair_count, 2, HEADS, HEAD)
    key_leaf = both_ways(product('pld,de->ple', edge_low, w_key)).reshape(pair_count, leaves, HEADS, HEAD)
    value_leaf = both_ways(product('pld,de->ple', edge_low, w_value)).reshape(pair_count, leaves, HEADS, HEAD)
    score_self = low_back(lax.optimization_barrier(jnp.sum(queries * key_self, axis=-1)) * score_scale)
    score_leaf = low_back(product('pvhd,plhd->pvhl', queries, key_leaf) * score_scale)
    live_heads = live_leaves[:, :, None, :]
    score_top = jnp.maximum(score_self, lax.optimization_barrier(jnp.max(jnp.where(live_heads, score_leaf, score_self[..., None]), axis=-1)))
    weight_self = jnp.exp(score_self - score_top)
    weight_leaf = jnp.where(live_heads, jnp.exp(score_leaf - score_top[..., None]), 0.0)
    weight_total = weight_self + lax.optimization_barrier(jnp.sum(weight_leaf, axis=-1))
    prob_self = low(weight_self / weight_total)
    prob_leaf = low(weight_leaf / weight_total[..., None])
    attended = prob_self[..., None] * value_self + product('pvhl,plhd->pvhd', prob_leaf, value_leaf)
    attended = both_ways(attended.reshape(pair_count, 2, model_width))
    branch = low_back(product('pvd,de->pve', attended, w_out))
    first_norm = normalize(center_keep + branch) * gain_attn + bias_attn
    hidden = low_back(product('pvd,df->pvf', low(first_norm), w_up))
    branch_ffn = low_back(product('pvf,fd->pvd', low(jax.nn.gelu(hidden)), w_down))
    new_center = low(normalize(first_norm + branch_ffn) * gain_ffn + bias_ffn)
    new_edges = low(product('pld,de->ple', edge_low, w_edge))
    return (new_center, new_edges)

def reference(center_input, edge_input, leaf_count, leaf_mask, w_query, w_key, w_value, w_out, gain_attn, bias_attn, w_up, w_down, gain_ffn, bias_ffn, w_edge, center_cot, edge_cot):
    float_weights = [weight.astype(jnp.float32) for weight in (w_query, w_key, w_value, w_out, gain_attn, bias_attn, w_up, w_down, gain_ffn, bias_ffn, w_edge)]
    layer_params = [tuple((weight[layer_index] for weight in float_weights)) for layer_index in range(2)]
    grad_totals = [[jnp.zeros_like(weight) for weight in params] for params in layer_params]
    leaf_slots = jnp.arange(LEAVES, dtype=jnp.int32)
    center_lists = [[], []]
    edge_lists = [[], []]
    back_centers = [[], []]
    back_edges = [[], []]
    for micro_index in range(MICRO):
        live_leaves = (leaf_slots[None, None, :] < leaf_count[micro_index][..., None]) & (leaf_mask[micro_index] == 1)

        def one_layer(center, edges, *params):
            return star_layer(center, edges, live_leaves, *params)
        out_one, pull_one = jax.vjp(one_layer, center_input[micro_index].astype(jnp.float32), edge_input[micro_index].astype(jnp.float32), *layer_params[0])
        out_two, pull_two = jax.vjp(one_layer, out_one[0], out_one[1], *layer_params[1])
        back_two = pull_two((center_cot[micro_index].astype(jnp.float32), edge_cot[micro_index].astype(jnp.float32)))
        back_one = pull_one((back_two[0], back_two[1]))
        for layer_index, outputs, backs in ((0, out_one, back_one), (1, out_two, back_two)):
            center_lists[layer_index].append(outputs[0])
            edge_lists[layer_index].append(outputs[1])
            back_centers[layer_index].append(backs[0])
            back_edges[layer_index].append(backs[1])
            grad_totals[layer_index] = [total + term for total, term in zip(grad_totals[layer_index], backs[2:])]
    center_act = jnp.stack([jnp.stack(center_lists[0]), jnp.stack(center_lists[1])])
    edge_act = jnp.stack([jnp.stack(edge_lists[0]), jnp.stack(edge_lists[1])])
    center_grad = jnp.stack([jnp.stack(back_centers[0]), jnp.stack(back_centers[1])])
    edge_grad = jnp.stack([jnp.stack(back_edges[0]), jnp.stack(back_edges[1])])
    center_count = MICRO * PAIRS * 2
    means = lax.optimization_barrier(jnp.sum(center_act, axis=(1, 2, 3))) / center_count
    squares = lax.optimization_barrier(jnp.sum(center_act * center_act, axis=(1, 2, 3))) / center_count
    center_stats = jnp.stack([means, squares - means * means], axis=1)
    stacked = [jnp.stack([grad_totals[0][index], grad_totals[1][index]]) for index in range(11)]
    return (center_act.astype(jnp.bfloat16), edge_act.astype(jnp.bfloat16), center_grad.astype(jnp.bfloat16), edge_grad.astype(jnp.bfloat16), stacked[0], stacked[1], stacked[2], stacked[3], stacked[4], stacked[5], stacked[6], stacked[7], stacked[8], stacked[9], stacked[10], center_stats)
```

```python
import functools
import math

import jax
import jax.numpy as jnp
import numpy as np
from jax import lax
from jax.experimental import pallas as pl
from jax.experimental.pallas import tpu as pltpu
from jax.sharding import PartitionSpec as P

HEADS = 12
EPS = 1e-05
BIG = 1e30
GROUP = 8
HALF = 2 * GROUP
LANES = 128
ROWS = 304
VMEM = 56 * 1024 * 1024

F32 = jnp.float32
BF16 = jnp.bfloat16


def mm(a, b):
    return lax.dot_general(a, b, (((1,), (0,)), ((), ())), preferred_element_type=F32)


def mm_nt(a, b):
    return lax.dot_general(a, b, (((1,), (1,)), ((), ())), preferred_element_type=F32)


def mm_tn(a, b):
    return lax.dot_general(a, b, (((0,), (0,)), ((), ())), preferred_element_type=F32)


def tiles_of(width):
    return -(-width // LANES)


def constants(width):
    rows = HEADS * HALF
    head = np.arange(rows) // HALF
    pair = (np.arange(rows) % HALF) // 2
    slot = np.arange(rows) % HALF
    head_width = width // HEADS
    own = (np.arange(width)[None, :] // head_width == head[:, None]).astype(np.float32)
    base = width - (tiles_of(width) - 1) * LANES
    bias = np.zeros((rows, LANES), np.float32)
    for p in range(GROUP):
        bias[:, base + p] = np.where(pair == p, 0.0, -BIG)
    for s in range(HALF):
        bias[:, base + GROUP + s] = np.where(slot == s, -BIG, 0.0)
    one_hot = np.zeros((GROUP, LANES), np.float32)
    for p in range(GROUP):
        one_hot[p, base + p] = 1.0
    center = np.zeros((HALF, LANES), np.float32)
    for r in range(HALF):
        center[r, base + r // 2] = 1.0
        for s in range(HALF):
            center[r, base + GROUP + s] = float(s % 2 != r % 2)
    return (
        jnp.asarray(own, BF16),
        jnp.asarray(bias, BF16),
        jnp.asarray(one_hot, F32),
        jnp.asarray(center, BF16),
    )


def normalize(values):
    centred = values - jnp.mean(values, axis=-1, keepdims=True)
    inverse = lax.rsqrt(jnp.mean(centred * centred, axis=-1, keepdims=True) + EPS)
    return centred * inverse, inverse


def norm_back(grad, normed, inverse):
    return inverse * (
        grad
        - jnp.mean(grad, axis=-1, keepdims=True)
        - normed * jnp.mean(grad * normed, axis=-1, keepdims=True)
    )


GELU_C = math.sqrt(2.0 / math.pi)


def gelu_parts(x):
    square = x * x
    t = jnp.tanh(GELU_C * x * (1.0 + 0.044715 * square))
    return square, t


def expand(rows16, own):
    return jnp.concatenate([rows16] * HEADS, axis=0) * own


def fold_heads(values, own):
    masked = values * own.astype(F32)
    return jnp.sum(masked.reshape(HEADS, HALF, values.shape[-1]), axis=0)


def build_x(x_ref, slot, e_f32, dead_ref, one_hot_ref, featc_ref, c_rows, width):
    leaves = e_f32.shape[0]
    edge_rows = leaves * GROUP
    last = (tiles_of(width) - 1) * LANES
    feature = dead_ref[0, slot][:, None, :] + one_hot_ref[...][None, :, :]
    x_ref[slot, 0:edge_rows, last : last + LANES] = feature.reshape(edge_rows, LANES).astype(BF16)
    part = e_f32[:, slot * GROUP : (slot + 1) * GROUP, :].reshape(edge_rows, width)
    x_ref[slot, 0:edge_rows, 0:width] = part.astype(BF16)
    x_ref[slot, edge_rows : edge_rows + HALF, last : last + LANES] = featc_ref[...]
    x_ref[slot, edge_rows : edge_rows + HALF, 0:width] = c_rows


def probabilities(x, keys):
    scores = mm_nt(x, keys)
    top = jnp.max(scores, axis=0, keepdims=True)
    weights = jnp.exp(scores - top)
    total = jnp.sum(weights, axis=0, keepdims=True)
    return weights * (1.0 / total)


def forward_kernel(
    width,
    active_ref,
    e_ref,
    dead_ref,
    c_ref,
    wq_ref,
    wk_ref,
    wv_ref,
    wo_ref,
    gain1_ref,
    bias1_ref,
    wup_ref,
    wdt_ref,
    gain2_ref,
    bias2_ref,
    own_ref,
    qbias_ref,
    one_hot_ref,
    featc_ref,
    newc_ref,
    x_ref,
    p_ref,
    pe_ref,
    att_ref,
    q_ref,
    stat_ref,
    keys_s,
):
    step = pl.program_id(0)
    scale = 1.0 / math.sqrt(width // HEADS)
    last = (tiles_of(width) - 1) * LANES

    @pl.when(active_ref[0] == 1)
    def _():
        @pl.when(step == 0)
        def _():
            q_ref[...] = mm(c_ref[...], wq_ref[...]).astype(BF16)
            keys_s[:, last : last + LANES] = qbias_ref[...]

        own = own_ref[...]
        e_f32 = e_ref[0].astype(F32)
        for slot in range(2):
            row = pl.multiple_of((step * 2 + slot) * HALF, HALF)
            build_x(
                x_ref, slot, e_f32, dead_ref, one_hot_ref, featc_ref,
                c_ref[pl.ds(row, HALF), :], width,
            )
            q_all = expand(q_ref[pl.ds(row, HALF), :], own)
            keys_s[:, 0:width] = (mm_nt(q_all, wk_ref[...]) * scale).astype(BF16)
            probs = probabilities(x_ref[slot], keys_s[...]).astype(BF16)
            p_ref[slot] = probs
            pe = mm_tn(probs, x_ref[slot])[:, 0:width].astype(BF16)
            pe_ref[slot] = pe
            att = fold_heads(mm(pe, wv_ref[...]), own)
            att_ref[pl.ds(row, HALF), :] = att.astype(BF16)

        @pl.when(step == pl.num_programs(0) - 1)
        def _():
            residual = c_ref[...].astype(F32) + mm(att_ref[...], wo_ref[...])
            z1, unused = normalize(residual)
            first = z1 * gain1_ref[...] + bias1_ref[...]
            hidden = mm(first.astype(BF16), wup_ref[...])
            unused, t = gelu_parts(hidden)
            gelu = (0.5 * hidden * (1.0 + t)).astype(BF16)
            z2, unused = normalize(first + mm_nt(gelu, wdt_ref[...]))
            new = (z2 * gain2_ref[...] + bias2_ref[...]).astype(BF16)
            newc_ref[...] = new
            new = new.astype(F32)
            stat_ref[0:1, :] = jnp.sum(new, axis=0, keepdims=True)
            stat_ref[1:2, :] = jnp.sum(new * new, axis=0, keepdims=True)


def whole(shape):
    zeros = (0,) * len(shape)
    return pl.BlockSpec(shape, lambda i, *unused: zeros)


def edge_spec(leaves, width):
    return pl.BlockSpec(
        (1, leaves, HALF, width),
        lambda i, active: ((i // 2) * active[0], 0, (i % 2) * active[0], 0),
    )


def step_spec(shape):
    return pl.BlockSpec(shape, lambda i, active: (i * active[0],) + (0,) * (len(shape) - 1))


def dead_spec(leaves):
    return pl.BlockSpec((1, 2, leaves, LANES), lambda i, active: (i * active[0], 0, 0, 0))


def run_forward(active, edges, dead, center, params, consts):
    micro, leaves, pairs, width = edges.shape
    steps = micro * pairs // HALF
    x_rows = leaves * GROUP + HALF
    pad = tiles_of(width) * LANES
    cols = HEADS * HALF
    ff = params["up"].shape[1]
    count = center.shape[0]
    operands = [
        center,
        params["query"], params["key"], params["value"], params["out"],
        params["gain1"], params["bias1"], params["up"], params["down_t"],
        params["gain2"], params["bias2"],
        *consts,
    ]
    return pl.pallas_call(
        functools.partial(forward_kernel, width),
        grid_spec=pltpu.PrefetchScalarGridSpec(
            num_scalar_prefetch=1,
            grid=(steps,),
            in_specs=[edge_spec(leaves, width), dead_spec(leaves)] + [whole(o.shape) for o in operands],
            out_specs=[
                whole((count, width)),
                step_spec((2, x_rows, pad)),
                step_spec((2, x_rows, cols)),
                step_spec((2, cols, width)),
                whole((count, width)),
                whole((count, width)),
                whole((2, width)),
            ],
            scratch_shapes=[pltpu.VMEM((cols, pad), BF16)],
        ),
        out_shape=[
            jax.ShapeDtypeStruct((count, width), BF16),
            jax.ShapeDtypeStruct((2 * steps, x_rows, pad), BF16),
            jax.ShapeDtypeStruct((2 * steps, x_rows, cols), BF16),
            jax.ShapeDtypeStruct((2 * steps, cols, width), BF16),
            jax.ShapeDtypeStruct((count, width), BF16),
            jax.ShapeDtypeStruct((count, width), BF16),
            jax.ShapeDtypeStruct((2, width), F32),
        ],
        compiler_params=pltpu.CompilerParams(vmem_limit_bytes=VMEM),
        name="layer_forward",
    )(active, edges, dead, *operands)


def pack_tiles(packed_ref, first_tile, matrix, width):
    rows = matrix.shape[0]
    for tile in range(tiles_of(width)):
        lanes = min(LANES, width - tile * LANES)
        packed_ref[first_tile + tile, 0:rows, 0:lanes] = matrix[
            :, tile * LANES : tile * LANES + lanes
        ].astype(BF16)


def backward_kernel(
    width,
    active_ref,
    x_ref,
    p_ref,
    pe_ref,
    c_ref,
    q_ref,
    att_ref,
    dc_ref,
    wq_ref,
    wk_ref,
    wv_ref,
    wo_ref,
    gain1_ref,
    bias1_ref,
    wup_ref,
    wdt_ref,
    gain2_ref,
    bias2_ref,
    own_ref,
    cback_ref,
    da_ref,
    ds_ref,
    packed_ref,
    keys_s,
    dvals_s,
    dwk_s,
    dwv_s,
    dq_s,
    dr_s,
):
    step = pl.program_id(0)
    scale = 1.0 / math.sqrt(width // HEADS)
    last = (tiles_of(width) - 1) * LANES
    tiles = tiles_of(width)
    ff_tiles = tiles_of(wup_ref.shape[1])

    @pl.when(active_ref[0] == 1)
    def _():
        @pl.when(step == 0)
        def _():
            packed_ref[...] = jnp.zeros_like(packed_ref)
            dwk_s[...] = jnp.zeros_like(dwk_s)
            dwv_s[...] = jnp.zeros_like(dwv_s)
            keys_s[:, last : last + LANES] = jnp.zeros((keys_s.shape[0], LANES), BF16)
            dvals_s[:, last : last + LANES] = jnp.zeros((keys_s.shape[0], LANES), BF16)
            att = att_ref[...]
            z1, inverse1 = normalize(c_ref[...].astype(F32) + mm(att, wo_ref[...]))
            first = z1 * gain1_ref[...] + bias1_ref[...]
            first_low = first.astype(BF16)
            hidden = mm(first_low, wup_ref[...])
            square, t = gelu_parts(hidden)
            gelu = (0.5 * hidden * (1.0 + t)).astype(BF16)
            z2, inverse2 = normalize(first + mm_nt(gelu, wdt_ref[...]))
            dc = dc_ref[...].astype(F32)
            dgain2 = jnp.sum(dc * z2, axis=0, keepdims=True)
            dbias2 = jnp.sum(dc, axis=0, keepdims=True)
            dr2 = norm_back(dc * gain2_ref[...], z2, inverse2)
            df = dr2.astype(BF16)
            pack_tiles(packed_ref, 4 * tiles + ff_tiles, mm_tn(df, gelu), wup_ref.shape[1])
            slope = 0.5 * (1.0 + t) + 0.5 * hidden * (1.0 - t * t) * GELU_C * (
                1.0 + 3.0 * 0.044715 * square
            )
            dh = (mm(df, wdt_ref[...]) * slope).astype(BF16)
            pack_tiles(packed_ref, 4 * tiles, mm_tn(first_low, dh), wup_ref.shape[1])
            dfirst = dr2 + mm_nt(dh, wup_ref[...])
            dgain1 = jnp.sum(dfirst * z1, axis=0, keepdims=True)
            dbias1 = jnp.sum(dfirst, axis=0, keepdims=True)
            dr1 = norm_back(dfirst * gain1_ref[...], z1, inverse1)
            dr_s[...] = dr1
            do = dr1.astype(BF16)
            pack_tiles(packed_ref, 3 * tiles, mm_tn(att, do), width)
            da_ref[...] = mm_nt(do, wo_ref[...]).astype(BF16)
            vector_tile = 4 * tiles + 2 * ff_tiles
            for index, vector in enumerate((dgain1, dbias1, dgain2, dbias2)):
                for tile in range(tiles):
                    lanes = min(LANES, width - tile * LANES)
                    spot = 16 * (index * tiles + tile)
                    packed_ref[vector_tile, spot : spot + 16, 0:lanes] = jnp.broadcast_to(
                        vector[:, tile * LANES : tile * LANES + lanes], (16, lanes)
                    ).astype(BF16)

        own = own_ref[...]
        for slot in range(2):
            row = pl.multiple_of((step * 2 + slot) * HALF, HALF)
            x = x_ref[slot]
            q_all = expand(q_ref[pl.ds(row, HALF), :], own)
            da_all = expand(da_ref[pl.ds(row, HALF), :], own)
            keys_s[:, 0:width] = (mm_nt(q_all, wk_ref[...]) * scale).astype(BF16)
            dvals_s[:, 0:width] = mm_nt(da_all, wv_ref[...]).astype(BF16)
            dprobs = mm_nt(x, dvals_s[...])
            probs_low = p_ref[slot]
            probs = probs_low.astype(F32)
            inner = jnp.sum(probs * dprobs, axis=0, keepdims=True)
            dscores = (probs * (dprobs - inner)).astype(BF16)
            ds_ref[slot] = dscores
            dse = mm_tn(dscores, x)[:, 0:width].astype(BF16)
            dwk_s[...] += mm_tn(dse, q_all)
            dwv_s[...] += mm_tn(pe_ref[slot], da_all)
            dq = fold_heads(mm(dse, wk_ref[...]), own) * scale
            dq_s[pl.ds(row, HALF), :] = dq.astype(BF16)
            edge_rows = x.shape[0] - HALF
            dr_s[pl.ds(row, HALF), :] += mm(
                dscores[edge_rows:, :], keys_s[:, 0:width]
            ) + mm(probs_low[edge_rows:, :], dvals_s[:, 0:width])

        @pl.when(step == pl.num_programs(0) - 1)
        def _():
            dq_all = dq_s[...]
            pack_tiles(packed_ref, 0, mm_tn(c_ref[...], dq_all), width)
            pack_tiles(packed_ref, tiles, dwk_s[...] * scale, width)
            pack_tiles(packed_ref, 2 * tiles, dwv_s[...], width)
            cback_ref[...] = (dr_s[...] + mm_nt(dq_all, wq_ref[...])).astype(BF16)


def run_backward(active, x, p, pe, center, q, att, dc, params, consts):
    groups, x_rows, pad = x.shape
    steps = groups // 2
    cols = p.shape[-1]
    count, width = center.shape
    ff = params["up"].shape[1]
    tiles = 4 * tiles_of(width) + 2 * tiles_of(ff) + 1
    operands = [
        center, q, att, dc,
        params["query"], params["key"], params["value"], params["out"],
        params["gain1"], params["bias1"], params["up"], params["down_t"],
        params["gain2"], params["bias2"],
        consts[0],
    ]
    return pl.pallas_call(
        functools.partial(backward_kernel, width),
        grid_spec=pltpu.PrefetchScalarGridSpec(
            num_scalar_prefetch=1,
            grid=(steps,),
            in_specs=[
                step_spec((2, x_rows, pad)),
                step_spec((2, x_rows, cols)),
                step_spec((2, cols, width)),
            ]
            + [whole(o.shape) for o in operands],
            out_specs=[
                whole((count, width)),
                whole((count, width)),
                step_spec((2, x_rows, cols)),
                whole((tiles, ROWS, LANES)),
            ],
            scratch_shapes=[
                pltpu.VMEM((cols, pad), BF16),
                pltpu.VMEM((cols, pad), BF16),
                pltpu.VMEM((width, width), F32),
                pltpu.VMEM((width, width), F32),
                pltpu.VMEM((count, width), BF16),
                pltpu.VMEM((count, width), F32),
            ],
        ),
        out_shape=[
            jax.ShapeDtypeStruct((count, width), BF16),
            jax.ShapeDtypeStruct((count, width), BF16),
            jax.ShapeDtypeStruct((groups, x_rows, cols), BF16),
            jax.ShapeDtypeStruct((tiles, ROWS, LANES), BF16),
        ],
        compiler_params=pltpu.CompilerParams(vmem_limit_bytes=VMEM),
        name="layer_backward",
    )(active, x, p, pe, *operands)


def edge_forward_kernel(late_ref, e_ref, w0_ref, w1_ref, mid_ref, out_ref):
    unused, leaves, pairs, width = e_ref.shape
    rows = e_ref[0].reshape(leaves * pairs, width)
    mid = mm(rows, w0_ref[...]).astype(BF16)
    mid_ref[0] = mid.reshape(leaves, pairs, width)

    @pl.when(late_ref[0] == 1)
    def _():
        out_ref[0] = mm(mid, w1_ref[...]).astype(BF16).reshape(leaves, pairs, width)

    @pl.when(late_ref[0] == 0)
    def _():
        out_ref[0] = mid.reshape(leaves, pairs, width)


def run_edge_forward(late, edges, w0, w1):
    micro, leaves, pairs, width = edges.shape
    cut = 4 if leaves % 4 == 0 else 1
    block = pl.BlockSpec(
        (1, leaves // cut, pairs, width), lambda i, late: (i // cut, i % cut, 0, 0)
    )
    return pl.pallas_call(
        edge_forward_kernel,
        grid_spec=pltpu.PrefetchScalarGridSpec(
            num_scalar_prefetch=1,
            grid=(micro * cut,),
            in_specs=[block, whole(w0.shape), whole(w1.shape)],
            out_specs=[block, block],
        ),
        out_shape=[jax.ShapeDtypeStruct(edges.shape, BF16)] * 2,
        compiler_params=pltpu.CompilerParams(vmem_limit_bytes=VMEM),
        name="edge_forward",
    )(late, edges, w0, w1)


def edge_backward_kernel(
    width,
    late_ref,
    e0_ref,
    e1_ref,
    cot_ref,
    dead_ref,
    x0_ref,
    p0_ref,
    ds0_ref,
    c1_ref,
    q1_ref,
    da1_ref,
    q0_ref,
    da0_ref,
    wk1_ref,
    wv1_ref,
    we1_ref,
    wk0_ref,
    wv0_ref,
    we0_ref,
    own_ref,
    qbias_ref,
    one_hot_ref,
    featc_ref,
    out_ref,
    packed_ref,
    x_s,
    keys_s,
    dvals_s,
    both_s,
    dwe_s,
):
    step = pl.program_id(0)
    scale = 1.0 / math.sqrt(width // HEADS)
    last = (tiles_of(width) - 1) * LANES
    leaves = e1_ref.shape[1]
    edge_rows = leaves * GROUP
    cols = keys_s.shape[0]
    own = own_ref[...]

    @pl.when(step == 0)
    def _():
        keys_s[:, last : last + LANES] = qbias_ref[...]
        dvals_s[:, last : last + LANES] = jnp.zeros((cols, LANES), BF16)
        dwe_s[...] = jnp.zeros_like(dwe_s)
        packed_ref[...] = jnp.zeros_like(packed_ref)

    def joined(parts):
        shaped = [part.reshape(leaves, GROUP, width) for part in parts]
        return jnp.concatenate(shaped, axis=1).reshape(leaves * HALF, width)

    e_f32 = e1_ref[0].astype(F32)
    parts = []
    for slot in range(2):
        row = pl.multiple_of((step * 2 + slot) * HALF, HALF)
        build_x(
            x_s, slot, e_f32, dead_ref, one_hot_ref, featc_ref,
            c1_ref[pl.ds(row, HALF), :], width,
        )
        x = x_s[slot]
        q_all = expand(q1_ref[pl.ds(row, HALF), :], own)
        da_all = expand(da1_ref[pl.ds(row, HALF), :], own)
        keys_s[:, 0:width] = (mm_nt(q_all, wk1_ref[...]) * scale).astype(BF16)
        dvals_s[:, 0:width] = mm_nt(da_all, wv1_ref[...]).astype(BF16)
        probs = probabilities(x, keys_s[...])
        dprobs = mm_nt(x, dvals_s[...])
        inner = jnp.sum(probs * dprobs, axis=0, keepdims=True)
        dscores = (probs * (dprobs - inner)).astype(BF16)
        parts.append(
            mm(dscores[0:edge_rows], keys_s[:, 0:width])
            + mm(probs.astype(BF16)[0:edge_rows], dvals_s[:, 0:width])
        )
    cot = cot_ref[0].reshape(leaves * HALF, width)
    late_grad = (joined(parts) + mm_nt(cot, we1_ref[...])).astype(BF16)

    @pl.when(late_ref[0] == 1)
    def _():
        out_ref[0] = late_grad.reshape(leaves, HALF, width)
        dwe_s[...] += mm_tn(e1_ref[0].reshape(leaves * HALF, width), cot)

    @pl.when(late_ref[0] == 0)
    def _():
        pieces = []
        for slot in range(2):
            row = pl.multiple_of((step * 2 + slot) * HALF, HALF)
            q_all = expand(q0_ref[pl.ds(row, HALF), :], own)
            da_all = expand(da0_ref[pl.ds(row, HALF), :], own)
            keys = (mm_nt(q_all, wk0_ref[...]) * scale).astype(BF16)
            dvals = mm_nt(da_all, wv0_ref[...]).astype(BF16)
            pieces.append(
                mm(ds0_ref[slot, 0:edge_rows, :], keys) + mm(p0_ref[slot, 0:edge_rows, :], dvals)
            )
        early_grad = joined(pieces) + mm_nt(late_grad, we0_ref[...])
        out_ref[0] = early_grad.astype(BF16).reshape(leaves, HALF, width)
        dwe_s[...] += mm_tn(e0_ref[0].reshape(leaves * HALF, width), late_grad)

    @pl.when(step == pl.num_programs(0) - 1)
    def _():
        pack_tiles(packed_ref, 0, dwe_s[...], width)


def run_edge_backward(late, e0, e1, cot, dead, x0, p0, ds0, rows, weights, consts):
    micro, leaves, pairs, width = e1.shape
    steps = micro * pairs // HALF
    groups, x_rows, pad = x0.shape
    cols = p0.shape[-1]
    block = pl.BlockSpec((1, leaves, HALF, width), lambda i, late: (i // 2, 0, i % 2, 0))
    own_block = pl.BlockSpec(
        (1, leaves, HALF, width), lambda i, late: ((i // 2) * (1 - late[0]), 0, (i % 2) * (1 - late[0]), 0)
    )
    early = lambda shape: pl.BlockSpec(
        shape, lambda i, late: (i * (1 - late[0]),) + (0,) * (len(shape) - 1)
    )
    operands = [*rows, *weights, *consts]
    tiles = tiles_of(width)
    return pl.pallas_call(
        functools.partial(edge_backward_kernel, width),
        grid_spec=pltpu.PrefetchScalarGridSpec(
            num_scalar_prefetch=1,
            grid=(steps,),
            in_specs=[
                own_block,
                block,
                block,
                pl.BlockSpec((1, 2, leaves, LANES), lambda i, late: (i, 0, 0, 0)),
                early((2, x_rows, pad)),
                early((2, x_rows, cols)),
                early((2, x_rows, cols)),
            ]
            + [whole(o.shape) for o in operands],
            out_specs=[block, whole((tiles, ROWS, LANES))],
            scratch_shapes=[
                pltpu.VMEM((2, x_rows, pad), BF16),
                pltpu.VMEM((cols, pad), BF16),
                pltpu.VMEM((cols, pad), BF16),
                pltpu.VMEM((16, LANES), BF16),
                pltpu.VMEM((width, width), F32),
            ],
        ),
        out_shape=[
            jax.ShapeDtypeStruct(e1.shape, BF16),
            jax.ShapeDtypeStruct((tiles, ROWS, LANES), BF16),
        ],
        compiler_params=pltpu.CompilerParams(vmem_limit_bytes=VMEM),
        name="edge_backward",
    )(late, e0, e1, cot, dead, x0, p0, ds0, *operands)


def swapped(array, axis, bit):
    devices = lax.axis_size(axis)
    return lax.ppermute(array, axis, [(i, i ^ bit) for i in range(devices)])


def sum_over(blocks, axis, order):
    me = lax.axis_index(axis)
    held = blocks.astype(F32)
    for bit in order:
        upper = (me // bit) % 2 == 1
        half = held.shape[0] // 2
        low, high = held[:half], held[half:]
        sent = jnp.where(upper, low, high).astype(BF16)
        held = jnp.where(upper, high, low) + swapped(sent, axis, bit).astype(F32)
    held = held.astype(BF16)
    for bit in order[::-1]:
        upper = (me // bit) % 2 == 1
        other = swapped(held, axis, bit)
        held = jnp.concatenate([jnp.where(upper, other, held), jnp.where(upper, held, other)])
    return held


def reduce_packed(packed, axis):
    devices = lax.axis_size(axis)
    bits = [1 << k for k in range(devices.bit_length() - 1)]
    tiles, rows, lanes = packed.shape
    blocks = packed.reshape(tiles * rows // 16, 16, lanes)
    count = blocks.shape[0]
    total = -(-count // (2 * devices)) * 2 * devices
    blocks = jnp.pad(blocks, ((0, total - count), (0, 0), (0, 0)))
    half = total // 2
    first = sum_over(blocks[:half], axis, bits)
    second = sum_over(blocks[half:], axis, bits[:1] + bits[2:] + bits[1:2])
    return jnp.concatenate([first, second])[:count].reshape(tiles, rows, lanes)


def sum_small(array, axis):
    devices = lax.axis_size(axis)
    for k in range(devices.bit_length() - 1):
        array = array + swapped(array, axis, 1 << k)
    return array


def shards(
    center_input,
    edge_input,
    leaf_count,
    leaf_mask,
    w_query,
    w_key,
    w_value,
    w_out,
    gain_attn,
    bias_attn,
    w_up,
    w_down,
    gain_ffn,
    bias_ffn,
    w_edge,
    center_cot,
    edge_cot,
):
    micro, pairs, leaves, width = edge_input.shape
    ff = w_up.shape[-1]
    section = lax.axis_index("section")
    first_section = section == 0
    late = jnp.where(first_section, 0, 1).astype(jnp.int32).reshape(1)
    early = 1 - late
    consts = constants(width)
    params = {
        "query": w_query[0], "key": w_key[0], "value": w_value[0], "out": w_out[0],
        "gain1": gain_attn, "bias1": bias_attn,
        "up": w_up[0], "down_t": jnp.transpose(w_down[0]),
        "gain2": gain_ffn, "bias2": bias_ffn,
    }
    edges0 = jnp.transpose(edge_input, (0, 2, 1, 3))
    cot = jnp.transpose(edge_cot, (0, 2, 1, 3))
    center0 = center_input.reshape(micro * pairs * 2, width)
    center_cot_rows = center_cot.reshape(micro * pairs * 2, width)

    slots = jnp.arange(leaves, dtype=jnp.int32)
    dead = jnp.where((slots < leaf_count[..., None]) & (leaf_mask == 1), 0.0, 1.0)
    dead = dead.reshape(micro * pairs // HALF, 2, HALF, leaves).transpose(0, 1, 3, 2)
    base = width - (tiles_of(width) - 1) * LANES + GROUP
    dead = jnp.pad(dead, ((0, 0), (0, 0), (0, 0), (base, LANES - base - HALF)))

    both = [(0, 1), (1, 0)]
    edge_other = lax.ppermute(w_edge[0], "section", both)
    w_key_other = lax.ppermute(w_key[0], "section", both)
    w_value_other = lax.ppermute(w_value[0], "section", both)

    def pick(at_first, at_second):
        return jnp.where(first_section, at_first, at_second)

    edge0, edge1 = pick(w_edge[0], edge_other), pick(edge_other, w_edge[0])

    new0, x0, p0, pe0, att0, q0, stat0 = run_forward(early, edges0, dead, center0, params, consts)
    center1 = lax.ppermute(new0, "section", [(0, 1)])
    edges1, edge_out = run_edge_forward(late, edges0, edge0, edge1)
    new1, x1, p1, pe1, att1, q1, stat1 = run_forward(late, edges1, dead, center1, params, consts)
    back1, da1, ds1, packed1 = run_backward(
        late, x1, p1, pe1, center1, q1, att1, center_cot_rows, params, consts
    )
    back1_other = lax.ppermute(back1, "section", [(1, 0)])
    q1_other = lax.ppermute(q1, "section", [(1, 0)])
    da1_other = lax.ppermute(da1, "section", [(1, 0)])
    back0, da0, ds0, packed0 = run_backward(
        early, x0, p0, pe0, center0, q0, att0, back1_other, params, consts
    )
    edge_back, packed_edge = run_edge_backward(
        late, edges0, edges1, cot, dead, x0, p0, ds0,
        (pick(new0, center1), pick(q1_other, q1), pick(da1_other, da1), q0, da0),
        (
            pick(w_key_other, w_key[0]), pick(w_value_other, w_value[0]), edge1,
            w_key[0], w_value[0], edge0,
        ),
        consts,
    )
    stats = sum_small(pick(stat0, stat1), "dp")
    packed = reduce_packed(jnp.concatenate([pick(packed0, packed1), packed_edge]), "dp").astype(F32)

    tiles, ff_tiles = tiles_of(width), tiles_of(ff)

    def matrix(first_tile, columns):
        span = packed[first_tile : first_tile + tiles_of(columns)]
        return jnp.transpose(span, (1, 0, 2)).reshape(ROWS, -1)[:width, :columns][None]

    vectors = packed[4 * tiles + 2 * ff_tiles]

    def vector(index):
        return jnp.concatenate(
            [vectors[16 * (index * tiles + t)] for t in range(tiles)]
        )[:width][None]

    edge_tile = 4 * tiles + 2 * ff_tiles + 1
    total = micro * pairs * 2 * lax.axis_size("dp")
    means = stats[0] / total
    variances = stats[1] / total - means * means
    shape = (1, micro, pairs, 2, width)
    return (
        pick(new0, new1).reshape(shape),
        jnp.transpose(edge_out, (0, 2, 1, 3))[None],
        pick(back0, back1).reshape(shape),
        jnp.transpose(edge_back, (0, 2, 1, 3))[None],
        matrix(0, width),
        matrix(tiles, width),
        matrix(2 * tiles, width),
        matrix(3 * tiles, width),
        vector(0),
        vector(1),
        matrix(4 * tiles, ff),
        jnp.transpose(matrix(4 * tiles + ff_tiles, ff), (0, 2, 1)),
        vector(2),
        vector(3),
        matrix(edge_tile, width),
        jnp.stack([means, variances])[None],
    )


def solution(mesh):
    data4 = P(None, "dp", None, None)
    square = P("section", None, None)
    row = P("section", None)
    acts = P("section", None, "dp", None, None)
    return jax.shard_map(
        shards,
        mesh=mesh,
        in_specs=(
            data4, data4, P(None, "dp", None), data4,
            square, square, square, square, row, row, square, square, row, row, square,
            data4, data4,
        ),
        out_specs=(
            acts, acts, acts, acts,
            square, square, square, square, row, row, square, square, row, row, square,
            square,
        ),
        check_vma=False,
    )
```

```python
import functools
import math

import jax
import jax.numpy as jnp
import numpy as np
from jax import lax
from jax.experimental import pallas as pl
from jax.experimental.pallas import tpu as pltpu
from jax.sharding import PartitionSpec as P

HEADS = 12
EPS = 1e-05
BIG = 1e30
GROUP = 8
HALF = 2 * GROUP
LANES = 128
ROWS = 304
VMEM = 56 * 1024 * 1024

F32 = jnp.float32
BF16 = jnp.bfloat16


def mm(a, b):
    return lax.dot_general(a, b, (((1,), (0,)), ((), ())), preferred_element_type=F32)


def mm_nt(a, b):
    return lax.dot_general(a, b, (((1,), (1,)), ((), ())), preferred_element_type=F32)


def mm_tn(a, b):
    return lax.dot_general(a, b, (((0,), (0,)), ((), ())), preferred_element_type=F32)


def tiles_of(width):
    return -(-width // LANES)


def constants(width):
    rows = HEADS * HALF
    head = np.arange(rows) // HALF
    pair = (np.arange(rows) % HALF) // 2
    slot = np.arange(rows) % HALF
    head_width = width // HEADS
    own = (np.arange(width)[None, :] // head_width == head[:, None]).astype(np.float32)
    base = width - (tiles_of(width) - 1) * LANES
    bias = np.zeros((rows, LANES), np.float32)
    for p in range(GROUP):
        bias[:, base + p] = np.where(pair == p, 0.0, -BIG)
    for s in range(HALF):
        bias[:, base + GROUP + s] = np.where(slot == s, -BIG, 0.0)
    one_hot = np.zeros((GROUP, LANES), np.float32)
    for p in range(GROUP):
        one_hot[p, base + p] = 1.0
    center = np.zeros((HALF, LANES), np.float32)
    for r in range(HALF):
        center[r, base + r // 2] = 1.0
        for s in range(HALF):
            center[r, base + GROUP + s] = float(s % 2 != r % 2)
    return (
        jnp.asarray(own, BF16),
        jnp.asarray(bias, BF16),
        jnp.asarray(one_hot, F32),
        jnp.asarray(center, BF16),
    )


def normalize(values):
    centred = values - jnp.mean(values, axis=-1, keepdims=True)
    inverse = lax.rsqrt(jnp.mean(centred * centred, axis=-1, keepdims=True) + EPS)
    return centred * inverse, inverse


def norm_back(grad, normed, inverse):
    return inverse * (
        grad
        - jnp.mean(grad, axis=-1, keepdims=True)
        - normed * jnp.mean(grad * normed, axis=-1, keepdims=True)
    )


GELU_C = math.sqrt(2.0 / math.pi)


def gelu_parts(x):
    square = x * x
    t = jnp.tanh(GELU_C * x * (1.0 + 0.044715 * square))
    return square, t


def expand(rows16, own):
    return jnp.concatenate([rows16] * HEADS, axis=0) * own


def fold_heads(values, own):
    masked = values * own.astype(F32)
    return jnp.sum(masked.reshape(HEADS, HALF, values.shape[-1]), axis=0)


def build_x(x_ref, slot, e_f32, dead_ref, one_hot_ref, featc_ref, c_rows, width):
    leaves = e_f32.shape[0]
    edge_rows = leaves * GROUP
    last = (tiles_of(width) - 1) * LANES
    feature = dead_ref[0, slot][:, None, :] + one_hot_ref[...][None, :, :]
    x_ref[slot, 0:edge_rows, last : last + LANES] = feature.reshape(edge_rows, LANES).astype(BF16)
    part = e_f32[:, slot * GROUP : (slot + 1) * GROUP, :].reshape(edge_rows, width)
    x_ref[slot, 0:edge_rows, 0:width] = part.astype(BF16)
    x_ref[slot, edge_rows : edge_rows + HALF, last : last + LANES] = featc_ref[...]
    x_ref[slot, edge_rows : edge_rows + HALF, 0:width] = c_rows


def column_rows(columns):
    rows = columns[0].shape[0]
    lane = lax.broadcasted_iota(jnp.int32, (rows, LANES), 1)
    tile = jnp.zeros((rows, LANES), F32)
    for index, column in enumerate(columns):
        tile = jnp.where(lane == index, column, tile)
    return jnp.transpose(tile)[0 : len(columns)]


def forward_kernel(
    width,
    deps,
    active_ref,
    e_ref,
    dead_ref,
    c_ref,
    wq_ref,
    wk_ref,
    wv_ref,
    wo_ref,
    gain1_ref,
    bias1_ref,
    wup_ref,
    wdt_ref,
    gain2_ref,
    bias2_ref,
    own_ref,
    qbias_ref,
    one_hot_ref,
    featc_ref,
    *rest,
):
    newc_ref, x_ref, p_ref, pe_ref, att_ref, q_ref, lse_ref, stat_ref, keys_s = rest[deps:]
    step = pl.program_id(0)
    scale = 1.0 / math.sqrt(width // HEADS)
    last = (tiles_of(width) - 1) * LANES
    slots = x_ref.shape[0]
    cols = HEADS * HALF

    @pl.when(active_ref[0] == 1)
    def _():
        @pl.when(step == 0)
        def _():
            q_ref[...] = mm(c_ref[...], wq_ref[...]).astype(BF16)
            for slot in range(slots):
                keys_s[slot, :, last : last + LANES] = qbias_ref[...]

        own = own_ref[...]
        base = pl.multiple_of(step * slots * HALF, slots * HALF)
        q_rows = q_ref[pl.ds(base, slots * HALF), :]
        q_all = jnp.concatenate(
            [expand(q_rows[s * HALF : (s + 1) * HALF], own) for s in range(slots)], axis=0
        )
        keys = (mm_nt(q_all, wk_ref[...]) * scale).astype(BF16)
        c_rows = c_ref[pl.ds(base, slots * HALF), :]
        e_f32 = e_ref[0].astype(F32)
        for slot in range(slots):
            keys_s[slot, :, 0:width] = keys[slot * cols : (slot + 1) * cols]
            build_x(
                x_ref, slot, e_f32, dead_ref, one_hot_ref, featc_ref,
                c_rows[slot * HALF : (slot + 1) * HALF], width,
            )
        scores = [mm_nt(keys_s[slot], x_ref[slot]) for slot in range(slots)]
        probs, logs = [], []
        for slot in range(slots):
            top = jnp.max(scores[slot], axis=1, keepdims=True)
            weights = jnp.exp(scores[slot] - top)
            total = jnp.sum(weights, axis=1, keepdims=True)
            probs.append((weights * (1.0 / total)).astype(BF16))
            logs.append(top + jnp.log(total))
        pes = []
        for slot in range(slots):
            p_ref[slot] = probs[slot]
            pe = mm(probs[slot], x_ref[slot])[:, 0:width].astype(BF16)
            pe_ref[slot] = pe
            pes.append(pe)
        lse_ref[0] = column_rows(logs)
        att = mm(jnp.concatenate(pes, axis=0), wv_ref[...])
        att = jnp.concatenate(
            [fold_heads(att[s * cols : (s + 1) * cols], own) for s in range(slots)], axis=0
        )
        att_ref[pl.ds(base, slots * HALF), :] = att.astype(BF16)

        @pl.when(step == pl.num_programs(0) - 1)
        def _():
            residual = c_ref[...].astype(F32) + mm(att_ref[...], wo_ref[...])
            z1, unused = normalize(residual)
            first = z1 * gain1_ref[...] + bias1_ref[...]
            hidden = mm(first.astype(BF16), wup_ref[...])
            unused, t = gelu_parts(hidden)
            gelu = (0.5 * hidden * (1.0 + t)).astype(BF16)
            z2, unused = normalize(first + mm_nt(gelu, wdt_ref[...]))
            new = (z2 * gain2_ref[...] + bias2_ref[...]).astype(BF16)
            newc_ref[...] = new
            new = new.astype(F32)
            stat_ref[0:1, :] = jnp.sum(new, axis=0, keepdims=True)
            stat_ref[1:2, :] = jnp.sum(new * new, axis=0, keepdims=True)


def whole(shape):
    zeros = (0,) * len(shape)
    return pl.BlockSpec(shape, lambda i, *unused: zeros)


def step_spec(shape, of=1):
    rest = (0,) * (len(shape) - 1)
    return pl.BlockSpec(shape, lambda i, flag: (i * (flag[0] == of).astype(jnp.int32),) + rest)


def run_forward(active, edges, dead, center, params, consts, deps=()):
    micro, leaves, pairs, width = edges.shape
    slots = pairs // GROUP
    groups = micro * slots
    x_rows = leaves * GROUP + HALF
    pad = tiles_of(width) * LANES
    cols = HEADS * HALF
    count = center.shape[0]
    operands = [
        center,
        params["query"], params["key"], params["value"], params["out"],
        params["gain1"], params["bias1"], params["up"], params["down_t"],
        params["gain2"], params["bias2"],
        *consts,
    ]
    return pl.pallas_call(
        functools.partial(forward_kernel, width, len(deps)),
        grid_spec=pltpu.PrefetchScalarGridSpec(
            num_scalar_prefetch=1,
            grid=(micro,),
            in_specs=[
                step_spec((1, leaves, pairs, width)),
                step_spec((1, slots, leaves, LANES)),
            ]
            + [whole(o.shape) for o in operands]
            + [pl.BlockSpec(memory_space=pl.ANY)] * len(deps),
            out_specs=[
                whole((count, width)),
                step_spec((slots, x_rows, pad)),
                step_spec((slots, cols, x_rows)),
                step_spec((slots, cols, width)),
                whole((count, width)),
                whole((count, width)),
                step_spec((1, slots, cols)),
                whole((2, width)),
            ],
            scratch_shapes=[pltpu.VMEM((slots, cols, pad), BF16)],
        ),
        out_shape=[
            jax.ShapeDtypeStruct((count, width), BF16),
            jax.ShapeDtypeStruct((groups, x_rows, pad), BF16),
            jax.ShapeDtypeStruct((groups, cols, x_rows), BF16),
            jax.ShapeDtypeStruct((groups, cols, width), BF16),
            jax.ShapeDtypeStruct((count, width), BF16),
            jax.ShapeDtypeStruct((count, width), BF16),
            jax.ShapeDtypeStruct((micro, slots, cols), F32),
            jax.ShapeDtypeStruct((2, width), F32),
        ],
        compiler_params=pltpu.CompilerParams(vmem_limit_bytes=VMEM),
        cost_estimate=cost(19e-6),
        name="layer_forward",
    )(active, edges, dead, *operands, *deps)


def blocks_for(devices, width, ff):
    count = (packed_tiles(width, ff) + tiles_of(width)) * (ROWS // 16)
    return -(-count // devices) * devices


def packed_tiles(width, ff):
    return 4 * (width // LANES) + 2 * (ff // LANES) + 3


def placement(width, ff):
    full, wide = width // LANES, ff // LANES
    rest = 4 * full + 2 * wide
    narrow, broad = width - full * LANES, ff - wide * LANES
    return (
        (0, width, (rest, 0)),
        (full, width, (rest, narrow)),
        (2 * full, width, (rest + 1, 0)),
        (3 * full, width, (rest + 1, narrow)),
        (4 * full, ff, (rest + 2, 0)),
        (4 * full + wide, ff, (rest + 2, broad)),
        (rest + 3, width, (rest + 3 + full, 0)),
    )


SPOT = 64


def sums_fit(devices, width):
    return width % LANES <= SPOT and 4 * devices <= LANES - SPOT


def put_tile(packed_ref, tile, matrix):
    rows, lanes = matrix.shape
    full = matrix
    if rows < ROWS:
        full = jnp.concatenate([matrix, jnp.zeros((ROWS - rows, lanes), F32)], axis=0)
    if lanes < LANES:
        full = jnp.concatenate([full, jnp.zeros((ROWS, LANES - lanes), F32)], axis=1)
    per = ROWS // 16
    packed_ref[tile * per : (tile + 1) * per] = full.astype(BF16).reshape(per, 16, LANES)


def put_matrix(packed_ref, first_tile, matrix):
    full = matrix.shape[1] // LANES
    for tile in range(full):
        put_tile(packed_ref, first_tile + tile, matrix[:, tile * LANES : (tile + 1) * LANES])
    return matrix[:, full * LANES :]


def backward_kernel(
    width,
    deps,
    olds,
    active_ref,
    x_ref,
    p_ref,
    pe_ref,
    c_ref,
    q_ref,
    att_ref,
    dc_ref,
    wq_ref,
    wk_ref,
    wv_ref,
    wo_ref,
    gain1_ref,
    bias1_ref,
    wup_ref,
    wdt_ref,
    gain2_ref,
    bias2_ref,
    own_ref,
    *rest,
):
    old_refs, rest = rest[deps : deps + olds], rest[deps + olds :]
    rows_ref, inner_ref, ds_ref, packed_out_ref, sent_ref, *rest = rest
    count = c_ref.shape[0]
    cback_ref, da_ref = rows_ref.at[0:count], rows_ref.at[count:]
    packed_ref, packed_sem, dvals_s, dwk_s, dwv_s, dwo_s, vec_s, dq_s, dr_s = rest
    step = pl.program_id(0)
    scale = 1.0 / math.sqrt(width // HEADS)
    last = (tiles_of(width) - 1) * LANES
    places = placement(width, wup_ref.shape[1])
    slots, x_rows, pad = x_ref.shape
    edge_rows = x_rows - HALF
    cols = HEADS * HALF

    @pl.when(active_ref[0] == 1)
    def _():
        @pl.when(step == 0)
        def _():
            dwk_s[...] = jnp.zeros_like(dwk_s)
            dwv_s[...] = jnp.zeros_like(dwv_s)
            for slot in range(slots):
                dvals_s[slot, :, last : last + LANES] = jnp.zeros((cols, LANES), BF16)
            att = att_ref[...]
            z1, inverse1 = normalize(c_ref[...].astype(F32) + mm(att, wo_ref[...]))
            first = z1 * gain1_ref[...] + bias1_ref[...]
            first_low = first.astype(BF16)
            hidden = mm(first_low, wup_ref[...])
            square, t = gelu_parts(hidden)
            gelu = (0.5 * hidden * (1.0 + t)).astype(BF16)
            z2, inverse2 = normalize(first + mm_nt(gelu, wdt_ref[...]))
            dc = dc_ref[0:count, :].astype(F32)
            dgain2 = jnp.sum(dc * z2, axis=0, keepdims=True)
            dbias2 = jnp.sum(dc, axis=0, keepdims=True)
            dr2 = norm_back(dc * gain2_ref[...], z2, inverse2)
            df = dr2.astype(BF16)
            down_rest = put_matrix(packed_ref, places[5][0], mm_tn(df, gelu))
            slope = 0.5 * (1.0 + t) + 0.5 * hidden * (1.0 - t * t) * GELU_C * (
                1.0 + 3.0 * 0.044715 * square
            )
            dh = (mm(df, wdt_ref[...]) * slope).astype(BF16)
            up_rest = put_matrix(packed_ref, places[4][0], mm_tn(first_low, dh))
            put_tile(packed_ref, places[4][2][0], jnp.concatenate([up_rest, down_rest], axis=1))
            dfirst = dr2 + mm_nt(dh, wup_ref[...])
            dgain1 = jnp.sum(dfirst * z1, axis=0, keepdims=True)
            dbias1 = jnp.sum(dfirst, axis=0, keepdims=True)
            dr1 = norm_back(dfirst * gain1_ref[...], z1, inverse1)
            dr_s[...] = dr1
            do = dr1.astype(BF16)
            dwo_s[...] = mm_tn(att, do)
            da_ref[...] = mm_nt(do, wo_ref[...]).astype(BF16)
            for index, vector in enumerate((dgain1, dbias1, dgain2, dbias2)):
                vec_s[index : index + 1, :] = vector

        own = own_ref[...]
        base = pl.multiple_of(step * slots * HALF, slots * HALF)

        def all_heads(ref):
            rows = ref[pl.ds(base, slots * HALF), :]
            return jnp.concatenate(
                [expand(rows[s * HALF : (s + 1) * HALF], own) for s in range(slots)], axis=0
            )

        q_all, da_all = all_heads(q_ref), all_heads(da_ref)
        keys = (mm_nt(q_all, wk_ref[...]) * scale).astype(BF16)
        dvals = mm_nt(da_all, wv_ref[...]).astype(BF16)
        for slot in range(slots):
            dvals_s[slot, :, 0:width] = dvals[slot * cols : (slot + 1) * cols]
        dprobs = [mm_nt(dvals_s[slot], x_ref[slot]) for slot in range(slots)]
        dscores, inners = [], []
        for slot in range(slots):
            probs = p_ref[slot].astype(F32)
            inner = jnp.sum(probs * dprobs[slot], axis=1, keepdims=True)
            dscores.append((probs * (dprobs[slot] - inner)).astype(BF16))
            ds_ref[slot] = dscores[slot]
            inners.append(inner)
        inner_ref[0] = column_rows(inners)
        dses, parts = [], []
        for slot in range(slots):
            dses.append(mm(dscores[slot], x_ref[slot])[:, 0:width].astype(BF16))
            span = slice(slot * cols, (slot + 1) * cols)
            parts.append(
                mm_tn(dscores[slot][:, edge_rows:], keys[span])
                + mm_tn(p_ref[slot, :, edge_rows:], dvals[span])
            )
        dse = jnp.concatenate(dses, axis=0)
        pe = pe_ref[...].reshape(slots * cols, width)
        dwk_s[...] += mm_tn(dse, q_all)
        dwv_s[...] += mm_tn(pe, da_all)
        dq = mm(dse, wk_ref[...])
        dq = jnp.concatenate(
            [fold_heads(dq[s * cols : (s + 1) * cols], own) for s in range(slots)], axis=0
        )
        dq_s[pl.ds(base, slots * HALF), :] = (dq * scale).astype(BF16)
        dr_s[pl.ds(base, slots * HALF), :] += jnp.concatenate(parts, axis=0)

        @pl.when(step == pl.num_programs(0) - 1)
        def _():
            dq_all = dq_s[...]
            dwq = jnp.concatenate([mm_tn(c_ref[...], dq_all), vec_s[...]], axis=0)
            query_rest = put_matrix(packed_ref, places[0][0], dwq)
            key_rest = put_matrix(packed_ref, places[1][0], dwk_s[...] * scale)
            key_rest = jnp.concatenate([key_rest, jnp.zeros((4, key_rest.shape[1]), F32)], axis=0)
            put_tile(packed_ref, places[0][2][0], jnp.concatenate([query_rest, key_rest], axis=1))
            value_rest = put_matrix(packed_ref, places[2][0], dwv_s[...])
            out_rest = put_matrix(packed_ref, places[3][0], dwo_s[...])
            put_tile(packed_ref, places[2][2][0], jnp.concatenate([value_rest, out_rest], axis=1))
            copy = pltpu.make_async_copy(packed_ref, packed_out_ref, packed_sem.at[0])
            copy.start()
            size = sent_ref.shape[0]
            start = pl.multiple_of((1 - active_ref[1]) * size, size)
            copy_half = pltpu.make_async_copy(
                packed_ref.at[pl.ds(start, size)], sent_ref, packed_sem.at[1]
            )
            copy_half.start()
            cback_ref[...] = (dr_s[...] + mm_nt(dq_all, wq_ref[...])).astype(BF16)
            copy.wait()
            copy_half.wait()

    if old_refs:

        @pl.when(active_ref[0] == 0)
        def _():
            for new_ref, old_ref in zip((rows_ref, inner_ref), old_refs):
                new_ref[...] = old_ref[...]


def run_backward(active, x, p, pe, center, q, att, dc, params, consts, micro, blocks, old, deps=()):
    groups, x_rows, pad = x.shape
    slots = groups // micro
    cols = p.shape[1]
    count, width = center.shape
    ff = params["up"].shape[1]
    operands = [
        center, q, att, dc,
        params["query"], params["key"], params["value"], params["out"],
        params["gain1"], params["bias1"], params["up"], params["down_t"],
        params["gain2"], params["bias2"],
        consts[0],
    ]
    inner_spec = pl.BlockSpec((1, slots, cols), lambda i, flag: (i, 0, 0))
    inputs = [x, p, pe, *operands, *deps, *old]
    return pl.pallas_call(
        functools.partial(backward_kernel, width, len(deps), len(old)),
        grid_spec=pltpu.PrefetchScalarGridSpec(
            num_scalar_prefetch=1,
            grid=(micro,),
            in_specs=[
                step_spec((slots, x_rows, pad)),
                step_spec((slots, cols, x_rows)),
                step_spec((slots, cols, width)),
            ]
            + [whole(o.shape) for o in operands]
            + [pl.BlockSpec(memory_space=pl.ANY)] * len(deps)
            + ([whole((2 * count, width)), inner_spec] if old else [])
            + ([pl.BlockSpec(memory_space=pl.ANY)] * 2 if old else []),
            out_specs=[
                whole((2 * count, width)),
                inner_spec,
                step_spec((slots, cols, x_rows)),
                pl.BlockSpec(memory_space=pl.ANY),
                pl.BlockSpec(memory_space=pl.ANY),
            ],
            scratch_shapes=[
                pltpu.VMEM((blocks, 16, LANES), BF16),
                pltpu.SemaphoreType.DMA((2,)),
                pltpu.VMEM((slots, cols, pad), BF16),
                pltpu.VMEM((width, width), F32),
                pltpu.VMEM((width, width), F32),
                pltpu.VMEM((width, width), F32),
                pltpu.VMEM((4, width), F32),
                pltpu.VMEM((count, width), BF16),
                pltpu.VMEM((count, width), F32),
            ],
        ),
        out_shape=[
            jax.ShapeDtypeStruct((2 * count, width), BF16),
            jax.ShapeDtypeStruct((micro, slots, cols), F32),
            jax.ShapeDtypeStruct((groups, cols, x_rows), BF16),
            jax.ShapeDtypeStruct((blocks, 16, LANES), BF16),
            jax.ShapeDtypeStruct((blocks // 2, 16, LANES), BF16),
        ],
        compiler_params=pltpu.CompilerParams(vmem_limit_bytes=VMEM),
        cost_estimate=cost(25e-6),
        input_output_aliases={len(inputs) - 1: 3, len(inputs): 4} if old else {},
        name="layer_backward",
    )(active, *inputs)


def edge_forward_kernel(e_ref, w_ref, dep_ref, out_ref):
    unused, leaves, pairs, width = e_ref.shape
    rows = e_ref[0].reshape(leaves * pairs, width)
    out_ref[0] = mm(rows, w_ref[...]).astype(BF16).reshape(leaves, pairs, width)


def run_edge_forward(edges, weight, dep):
    micro, leaves, pairs, width = edges.shape
    cut = 2 if leaves % 2 == 0 else 1
    block = pl.BlockSpec((1, leaves // cut, pairs, width), lambda i: (i // cut, i % cut, 0, 0))
    return pl.pallas_call(
        edge_forward_kernel,
        grid=(micro * cut,),
        in_specs=[block, whole(weight.shape), pl.BlockSpec(memory_space=pl.ANY)],
        out_specs=block,
        out_shape=jax.ShapeDtypeStruct(edges.shape, BF16),
        compiler_params=pltpu.CompilerParams(vmem_limit_bytes=VMEM),
        cost_estimate=cost(13e-6),
        name="edge_forward",
    )(edges, weight, dep)


def edge_weight_kernel(
    width, e_ref, cot_ref, p_ref, ds_ref, q_ref, rows_ref, wk_ref, wv_ref, own_ref,
    dep_ref, out_ref, cross_ref,
):
    step = pl.program_id(0)
    scale = 1.0 / math.sqrt(width // HEADS)
    slots = p_ref.shape[0]
    leaves = e_ref.shape[1]
    edge_rows = leaves * GROUP

    @pl.when(step == 0)
    def _():
        out_ref[...] = jnp.zeros_like(out_ref)
        cross_ref[...] = jnp.zeros_like(cross_ref)

    flat = (leaves * slots * GROUP, width)
    cross_ref[...] += mm_tn(e_ref[0].reshape(flat), cot_ref[0].reshape(flat))
    own = own_ref[...]
    base = pl.multiple_of(step * slots * HALF, slots * HALF)

    def all_heads(ref):
        rows = ref[pl.ds(base, slots * HALF), :]
        return jnp.concatenate(
            [expand(rows[s * HALF : (s + 1) * HALF], own) for s in range(slots)], axis=0
        )

    keys = (mm_nt(all_heads(q_ref), wk_ref[...]) * scale).astype(BF16)
    dvals = mm_nt(all_heads(rows_ref.at[q_ref.shape[0] :]), wv_ref[...]).astype(BF16)
    e_f32 = e_ref[0].astype(F32)
    dses, pes = [], []
    for slot in range(slots):
        part = e_f32[:, slot * GROUP : (slot + 1) * GROUP, :].reshape(edge_rows, width)
        part = part.astype(BF16)
        dses.append(mm(ds_ref[slot, :, 0:edge_rows], part).astype(BF16))
        pes.append(mm(p_ref[slot, :, 0:edge_rows], part).astype(BF16))
    out_ref[...] += mm_tn(jnp.concatenate(dses, axis=0), keys) + mm_tn(
        jnp.concatenate(pes, axis=0), dvals
    )


def run_edge_weight(edges, cot, p, ds, q, rows, w_key, w_value, consts, dep):
    micro, leaves, pairs, width = edges.shape
    groups, cols, x_rows = p.shape
    slots = groups // micro
    operands = [q, rows, w_key, w_value, consts[0]]

    def all_steps(shape):
        return pl.BlockSpec(shape, lambda i: (i,) + (0,) * (len(shape) - 1))

    return pl.pallas_call(
        functools.partial(edge_weight_kernel, width),
        grid_spec=pltpu.PrefetchScalarGridSpec(
            num_scalar_prefetch=0,
            grid=(micro,),
            in_specs=[
                all_steps((1, leaves, pairs, width)),
                all_steps((1, leaves, pairs, width)),
                all_steps((slots, cols, x_rows)),
                all_steps((slots, cols, x_rows)),
            ]
            + [whole(o.shape) for o in operands]
            + [pl.BlockSpec(memory_space=pl.ANY)],
            out_specs=[whole((width, width))] * 2,
        ),
        out_shape=[jax.ShapeDtypeStruct((width, width), F32)] * 2,
        compiler_params=pltpu.CompilerParams(vmem_limit_bytes=VMEM),
        cost_estimate=cost(24e-6),
        name="edge_weight",
    )(edges, cot, p, ds, *operands, dep)


def edge_backward_kernel(
    width,
    first,
    deps,
    late_ref,
    e1_ref,
    cot_ref,
    x0_ref,
    x1_ref,
    q_ref,
    rows_ref,
    lse_ref,
    inner_ref,
    c1_ref,
    rows1_ref,
    weights1_ref,
    sums_ref,
    wk_ref,
    wv_ref,
    w0_ref,
    wc_ref,
    we_ref,
    own_ref,
    qbias_ref,
    *rest,
):
    out_ref, act_ref, both_s, sum_s, joint_s, act_s, act_sem = rest[deps:]
    step = pl.program_id(0)
    scale = 1.0 / math.sqrt(width // HEADS)
    last = (tiles_of(width) - 1) * LANES
    leaves = cot_ref.shape[1]
    edge_rows = leaves * GROUP
    cols = HEADS * HALF
    own = own_ref[...]

    @pl.when(step == 0)
    def _():
        for slot in range(2):
            for layer in range(2):
                both_s[slot, layer, :, last : last + LANES] = qbias_ref[...]
                both_s[slot, 2 + layer, :, last : last + LANES] = jnp.zeros((cols, LANES), BF16)

    base = pl.multiple_of((first + step) * HALF * 2, HALF * 2)
    half = ((first + step) % (lse_ref.shape[1] // 2)) * 2

    def set_layer(layer, q_rows, da_rows, w_key, w_value):
        def all_heads(rows):
            return jnp.concatenate([expand(rows[0:HALF], own), expand(rows[HALF:], own)], axis=0)

        keys = (mm_nt(all_heads(q_rows), w_key) * scale).astype(BF16)
        dvals = mm_nt(all_heads(da_rows), w_value).astype(BF16)
        for slot in range(2):
            span = slice(slot * cols, (slot + 1) * cols)
            both_s[slot, layer, :, 0:width] = keys[span]
            both_s[slot, 2 + layer, :, 0:width] = dvals[span]

    def attention_part(x_ref, layers):
        parts = []
        count = layers * cols
        pad = both_s.shape[-1]
        for slot in range(2):
            x = x_ref[slot, 0:edge_rows, :]
            lse = lse_ref[0, pl.ds(half + slot, 1), :]
            inner = inner_ref[0, pl.ds(half + slot, 1), :]
            if layers == 2:
                lse = jnp.concatenate([lse, sums_ref[0, 0, pl.ds(half + slot, 1), :]], axis=1)
                inner = jnp.concatenate([inner, sums_ref[1, 0, pl.ds(half + slot, 1), :]], axis=1)
            if layers == 2:
                both = both_s[slot].reshape(2 * count, pad)
                product = mm_nt(x, both)
                probs = jnp.exp(product[:, 0:count] - lse)
                dscores = probs * (product[:, count:] - inner)
                part = mm(
                    jnp.concatenate([dscores.astype(BF16), probs.astype(BF16)], axis=1), both
                )
            else:
                keys, dvals = both_s[slot, 0], both_s[slot, 2]
                probs = jnp.exp(mm_nt(x, keys) - lse)
                dscores = probs * (mm_nt(x, dvals) - inner)
                part = mm(dscores.astype(BF16), keys) + mm(probs.astype(BF16), dvals)
            parts.append(part[:, 0:width])
        return parts

    def joined(parts):
        shaped = [part.reshape(leaves, GROUP, width) for part in parts]
        return jnp.concatenate(shaped, axis=1).reshape(leaves * HALF, width)

    cot = cot_ref[0].reshape(leaves * HALF, width)
    sum_s[...] = mm_nt(cot, wc_ref[...])
    own_rows = pl.ds(base, 2 * HALF)
    count = q_ref.shape[0]
    da_rows = pl.ds(count + base, 2 * HALF)
    set_layer(0, q_ref[own_rows, :], rows_ref[da_rows, :], wk_ref[...], wv_ref[...])

    @pl.when(late_ref[0] == 1)
    def _():
        grad = sum_s[...] + joined(attention_part(x1_ref, 1))
        out_ref[0] = grad.astype(BF16).reshape(leaves, HALF, width)
        act = mm(e1_ref[0].reshape(leaves * HALF, width), we_ref[...])
        act_s[...] = act.astype(BF16).reshape(leaves, HALF, width)
        per = act_ref.shape[2] // HALF
        micro = (first + step) // per
        pair = pl.multiple_of((first + step) % per * HALF, HALF)
        copy = pltpu.make_async_copy(
            act_s, act_ref.at[micro, :, pl.ds(pair, HALF), :], act_sem
        )
        copy.start()
        copy.wait()

    @pl.when(late_ref[0] == 0)
    def _():
        @pl.when(step == 0)
        def _():
            for index in range(2):
                at = (1 + index) * width
                joint_s[index] = mm(w0_ref[...], weights1_ref[at : at + width, :]).astype(BF16)

        q1 = mm(c1_ref[own_rows, :], weights1_ref[0:width, :]).astype(BF16)
        set_layer(1, q1, rows1_ref[da_rows, :], joint_s[0], joint_s[1])
        grad = sum_s[...] + joined(attention_part(x0_ref, 2))
        out_ref[0] = grad.astype(BF16).reshape(leaves, HALF, width)


def run_edge_backward(
    late, first, steps, so_far, e1, cot, x0, x1, rows, weights, consts, deps
):
    micro, leaves, pairs, width = cot.shape
    per = pairs // HALF
    groups, x_rows, pad = x0.shape
    cols = HEADS * HALF
    slots = groups // micro
    block = pl.BlockSpec(
        (1, leaves, HALF, width), lambda i, late: ((first + i) // per, 0, (first + i) % per, 0)
    )
    row_spec = pl.BlockSpec((1, slots, cols), lambda i, late: ((first + i) // per, 0, 0))
    sums_spec = pl.BlockSpec((2, 1, slots, cols), lambda i, late: (0, (first + i) // per, 0, 0))
    late_block = pl.BlockSpec(
        (1, leaves, HALF, width),
        lambda i, late: (
            (first + i) // per * late[0] + first // per * (1 - late[0]), 0,
            (first + i) % per * late[0], 0,
        ),
    )

    def x_spec(of):
        return pl.BlockSpec(
            (2, x_rows, pad),
            lambda i, late: ((first + i) * (late[0] == of).astype(jnp.int32), 0, 0),
        )

    operands = [*weights, consts[0], consts[1]]
    extra = list(deps) + ([] if so_far is None else [so_far])
    inputs = [e1, cot, x0, x1, *rows, *operands, *extra]
    aliases = {1: 1} if so_far is None else {1: 1, len(inputs): 0}
    return pl.pallas_call(
        functools.partial(edge_backward_kernel, width, first, len(extra)),
        grid_spec=pltpu.PrefetchScalarGridSpec(
            num_scalar_prefetch=1,
            grid=(steps,),
            in_specs=[late_block, block, x_spec(0), x_spec(1)]
            + [whole(rows[0].shape), whole(rows[1].shape), row_spec, row_spec]
            + [whole(rows[4].shape), whole(rows[5].shape), whole(rows[6].shape), sums_spec]
            + [whole(o.shape) for o in operands]
            + [pl.BlockSpec(memory_space=pl.ANY)] * len(extra),
            out_specs=[block, pl.BlockSpec(memory_space=pl.ANY)],
            scratch_shapes=[
                pltpu.VMEM((2, 4, cols, pad), BF16),
                pltpu.VMEM((leaves * HALF, width), F32),
                pltpu.VMEM((2, width, width), BF16),
                pltpu.VMEM((leaves, HALF, width), BF16),
                pltpu.SemaphoreType.DMA(()),
            ],
        ),
        out_shape=[jax.ShapeDtypeStruct(cot.shape, BF16)] * 2,
        input_output_aliases=aliases,
        compiler_params=pltpu.CompilerParams(vmem_limit_bytes=VMEM),
        cost_estimate=cost(7e-6 * steps),
        name="edge_backward",
    )(late, *inputs)


def cost(seconds):
    return pl.CostEstimate(flops=int(seconds * 1e9), bytes_accessed=0, transcendentals=0)


def split_kernel(parts, recv_count, deps, edge_at, digit_ref, *refs):
    held_ref, *refs = refs
    recv_refs, refs = refs[:recv_count], refs[recv_count:]
    if edge_at is not None:
        edge_ref, edge_recv_ref, *refs = refs
    refs = refs[deps:]
    keep_ref, *refs = refs
    send_refs, refs = refs[: parts - 1], refs[parts - 1 :]
    total = held_ref[...].astype(F32)
    for recv_ref in recv_refs:
        total = total + recv_ref[...].astype(F32)
    if parts == 1:
        keep_ref[...] = total.astype(keep_ref.dtype)
        return
    total_ref = refs[0]
    total_ref[...] = total
    if edge_at is not None:

        @pl.when(digit_ref[1] == 1)
        def _():
            span = slice(edge_at, edge_at + edge_ref.shape[0])
            total_ref[span] = edge_ref[...].astype(F32) + edge_recv_ref[...].astype(F32)

    size = held_ref.shape[0] // parts
    digit = digit_ref[0]

    def part(other):
        start = pl.multiple_of((digit ^ other) * size, size)
        return total_ref[pl.ds(start, size)]

    keep_ref[...] = part(0).astype(keep_ref.dtype)
    for index, send_ref in enumerate(send_refs):
        send_ref[...] = part(index + 1).astype(BF16)


def run_split(held, received, parts, digits, keep_type, edges=(), edge_at=None, deps=()):
    count = held.shape[0] // 2 if edges else held.shape[0]
    size = count // parts
    inputs = [held, *received, *edges]

    def spec(array):
        return whole(array.shape)

    held_spec = pl.BlockSpec((count, 16, LANES), lambda i, digits: (digits[1], 0, 0))
    out_shape = [jax.ShapeDtypeStruct((size, 16, LANES), keep_type)]
    out_shape += [jax.ShapeDtypeStruct((size, 16, LANES), BF16)] * (parts - 1)
    return pl.pallas_call(
        functools.partial(split_kernel, parts, len(received), len(deps), edge_at),
        grid_spec=pltpu.PrefetchScalarGridSpec(
            num_scalar_prefetch=1,
            grid=(1,),
            in_specs=[held_spec if edges else spec(held)]
            + [spec(array) for array in inputs[1:]]
            + [pl.BlockSpec(memory_space=pl.ANY)] * len(deps),
            out_specs=[spec(array) for array in out_shape],
            scratch_shapes=[pltpu.VMEM((count, 16, LANES), F32)],
        ),
        out_shape=out_shape,
        compiler_params=pltpu.CompilerParams(vmem_limit_bytes=VMEM),
        cost_estimate=cost(2e-6),
        name="split_gradients",
    )(digits, *inputs, *deps)


def join_kernel(count, deps, *refs):
    out_ref = refs[count + deps]
    size = refs[0].shape[0]
    for index in range(count):
        out_ref[index * size : (index + 1) * size] = refs[index][...]


def run_join(pieces, deps=()):
    size = pieces[0].shape[0]
    spec = pl.BlockSpec(memory_space=pltpu.VMEM)
    return pl.pallas_call(
        functools.partial(join_kernel, len(pieces), len(deps)),
        in_specs=[spec] * len(pieces) + [pl.BlockSpec(memory_space=pl.ANY)] * len(deps),
        out_specs=spec,
        out_shape=jax.ShapeDtypeStruct((size * len(pieces), 16, LANES), BF16),
        compiler_params=pltpu.CompilerParams(vmem_limit_bytes=VMEM),
        cost_estimate=cost(1e-6),
        name="join_gradients",
    )(*pieces, *deps)


def edge_tiles_kernel(late_ref, early_ref, late_edge_ref, sums_ref, dep_ref, out_ref):
    width = early_ref.shape[0]
    full = width // LANES
    edge = jnp.where(late_ref[0] == 1, late_edge_ref[...], early_ref[...].astype(F32))
    over = put_matrix(out_ref, 0, edge)
    lane = lax.broadcasted_iota(jnp.int32, (LANES, width), 0) - SPOT - 4 * late_ref[1]
    table = jnp.zeros((LANES, width), F32)
    for index in range(2):
        row = sums_ref[index : index + 1, :]
        high = row.astype(BF16).astype(F32)
        table = jnp.where(lane == index, high, table)
        table = jnp.where(lane == 2 + index, row - high, table)
    columns = jnp.transpose(table)
    gap = jnp.zeros((width, LANES - over.shape[1]), F32)
    put_tile(out_ref, full, jnp.concatenate([over, gap], axis=1) + columns)


def run_edge_tiles(late_me, early_edge, late_edge, sums, dep):
    width = late_edge.shape[0]
    per = ROWS // 16
    vmem = pl.BlockSpec(memory_space=pltpu.VMEM)
    return pl.pallas_call(
        edge_tiles_kernel,
        in_specs=[pl.BlockSpec(memory_space=pltpu.SMEM), vmem, vmem, vmem]
        + [pl.BlockSpec(memory_space=pl.ANY)],
        out_shape=jax.ShapeDtypeStruct((tiles_of(width) * per, 16, LANES), BF16),
        compiler_params=pltpu.CompilerParams(vmem_limit_bytes=VMEM),
        cost_estimate=cost(2e-6),
        name="edge_tiles",
    )(late_me, early_edge, late_edge, sums, dep)


def stages_of(devices):
    bits = devices.bit_length() - 1
    stages = [(0, 1)]
    if (bits - 1) % 2:
        stages.append((1, 1))
    at = sum(width for unused, width in stages)
    while at < bits:
        stages.append((at, 2))
        at += 2
    return stages


def unpack_kernel(width, ff, me_ref, own_ref, other_ref, *refs):
    *outs, vector_ref, sums_ref, total_ref = refs
    half, per = own_ref.shape[0], own_ref.shape[1]
    me = me_ref[0]
    for index in range(half):
        for source, base in ((own_ref, 0), (other_ref, half)):
            start = pl.multiple_of((me ^ (base + index)) * per, per)
            total_ref[pl.ds(start, per)] = source[index]
    rows = ROWS // 16

    def tile_at(tile):
        return total_ref[tile * rows : (tile + 1) * rows].reshape(ROWS, LANES).astype(F32)

    for (first, columns, (spot, lane)), ref in zip(placement(width, ff), outs):
        full = columns // LANES
        for tile in range(full):
            values = tile_at(first + tile)
            ref[:, 0, tile * LANES : (tile + 1) * LANES] = values[0:width]
            if first == 0:
                vector_ref[:, tile * LANES : (tile + 1) * LANES] = values[width : width + 4]
        values = tile_at(spot)[:, lane : lane + columns - full * LANES]
        ref[:, 0, full * LANES : columns] = values[0:width]
        if first == 0:
            vector_ref[:, full * LANES : columns] = values[width : width + 4]
    last = tile_at(placement(width, ff)[6][2][0])[0:width].astype(BF16)
    lane = lax.broadcasted_iota(jnp.int32, (LANES, LANES), 0)
    kind = lax.broadcasted_iota(jnp.int32, (LANES, LANES), 1)
    chosen = (lane >= SPOT) & (lane % 2 == kind)
    sums_ref[...] = mm(last, chosen.astype(F32).astype(BF16))


def run_unpack(me, own, other, width, ff):
    square = jax.ShapeDtypeStruct((width, 1, width), F32)
    wide = jax.ShapeDtypeStruct((width, 1, ff), F32)
    count = own.shape[0] * own.shape[1] * 2
    spec = pl.BlockSpec(memory_space=pltpu.VMEM)
    return pl.pallas_call(
        functools.partial(unpack_kernel, width, ff),
        in_specs=[pl.BlockSpec(memory_space=pltpu.SMEM), spec, spec],
        out_shape=[square] * 4 + [wide] * 2 + [
            square, jax.ShapeDtypeStruct((4, width), F32), jax.ShapeDtypeStruct((width, LANES), F32)
        ],
        scratch_shapes=[pltpu.VMEM((count, 16, LANES), BF16)],
        compiler_params=pltpu.CompilerParams(vmem_limit_bytes=VMEM),
        name="unpack_gradients",
    )(me, own, other)


def swapped(array, axis, bit):
    devices = lax.axis_size(axis)
    return lax.ppermute(array, axis, [(i, i ^ bit) for i in range(devices)])


def sum_small(array, axis):
    devices = lax.axis_size(axis)
    for k in range(devices.bit_length() - 1):
        array = array + swapped(array, axis, 1 << k)
    return array


def shards(
    center_input,
    edge_input,
    leaf_count,
    leaf_mask,
    w_query,
    w_key,
    w_value,
    w_out,
    gain_attn,
    bias_attn,
    w_up,
    w_down,
    gain_ffn,
    bias_ffn,
    w_edge,
    center_cot,
    edge_cot,
):
    micro, pairs, leaves, width = edge_input.shape
    ff = w_up.shape[-1]
    section = lax.axis_index("section")
    at_first = section == 0
    late = jnp.where(at_first, 0, 1).astype(jnp.int32).reshape(1)
    early = 1 - late
    consts = constants(width)
    params = {
        "query": w_query[0], "key": w_key[0], "value": w_value[0], "out": w_out[0],
        "gain1": gain_attn, "bias1": bias_attn,
        "up": w_up[0], "down_t": jnp.transpose(w_down[0]),
        "gain2": gain_ffn, "bias2": bias_ffn,
    }
    edges0 = jnp.transpose(edge_input, (0, 2, 1, 3))
    cot = jnp.transpose(edge_cot, (0, 2, 1, 3))
    center0 = center_input.reshape(micro * pairs * 2, width)
    center_cot_rows = center_cot.reshape(micro * pairs * 2, width)

    slots = jnp.arange(leaves, dtype=jnp.int32)
    dead = jnp.where((slots < leaf_count[..., None]) & (leaf_mask == 1), 0.0, 1.0)
    dead = dead.reshape(micro, pairs // GROUP, HALF, leaves).transpose(0, 1, 3, 2)
    base = width - (tiles_of(width) - 1) * LANES + GROUP
    dead = jnp.pad(dead, ((0, 0), (0, 0), (0, 0), (base, LANES - base - HALF)))

    both = [(0, 1), (1, 0)]
    edge_other = lax.ppermute(w_edge[0], "section", both)
    weights1 = lax.ppermute(
        jnp.concatenate([w_query[0], w_key[0], w_value[0]]), "section", [(1, 0)]
    )

    def pick(at_first, at_second):
        return jnp.where(section == 0, at_first, at_second)

    def back_to_first(array):
        return lax.ppermute(array, "section", [(1, 0)])

    edge0, edge1 = pick(w_edge[0], edge_other), pick(edge_other, w_edge[0])
    devices = lax.axis_size("dp")
    blocks = blocks_for(devices, width, ff)
    me = lax.axis_index("dp")
    core = (me & 1).astype(jnp.int32).reshape(1)
    late_core, early_core = jnp.concatenate([late, core]), jnp.concatenate([early, core])

    new0, x0, p0, pe0, att0, q0, lse0, stat0 = run_forward(
        early, edges0, dead, center0, params, consts, (edge_other,)
    )
    center1 = lax.ppermute(new0, "section", [(0, 1)])
    edges1 = run_edge_forward(edges0, edge0, weights1)
    joint = mm(edge0, edge1).astype(BF16)
    new1, x1, p1, pe1, att1, q1, lse1, stat1 = run_forward(
        late, edges1, dead, center1, params, consts
    )
    rows1, inner1, ds1, packed1, sent1 = run_backward(
        late_core, x1, p1, pe1, center1, q1, att1, center_cot_rows, params, consts, micro, blocks,
        (),
    )
    rows1_other = back_to_first(rows1)
    sums1_other = back_to_first(jnp.stack([lse1, inner1]))

    def second_section(*operands):
        edges, cot, p, ds, q, rows, w_key, w_value, edge0, edge1, dep = operands
        attended, cross = run_edge_weight(edges, cot, p, ds, q, rows, w_key, w_value, consts, dep)
        cross = cross.astype(BF16)
        return (attended + mm_nt(cross, edge1)).astype(BF16), mm_tn(edge0, cross)

    def first_section(*operands):
        return jnp.zeros((width, width), BF16), jnp.zeros((width, width), F32)

    early_edge, late_edge = lax.cond(
        at_first, first_section, second_section,
        edges0, cot, p1, ds1, q1, rows1, w_key[0], w_value[0], edge0, edge1, rows1_other,
    )
    rows, inner, unused, packed, sent = run_backward(
        early_core, x0, p0, pe0, center0, q0, att0, rows1_other, params, consts, micro, blocks,
        (rows1, inner1, packed1, sent1), (early_edge, sums1_other),
    )
    early_other = back_to_first(early_edge)
    sums = pick(stat0, stat1)
    fits = sums_fit(devices, width)
    spot_of_sums = me if fits else jnp.full((), devices)
    late_me = jnp.concatenate([late, spot_of_sums.astype(jnp.int32).reshape(1)])
    piece_rows = (
        pick(q0, q1), rows, pick(lse0, lse1), inner, new0, rows1_other, weights1, sums1_other
    )
    edge_weights = (w_key[0], w_value[0], edge0, pick(joint, edge1), edge1)
    edge_back, edge_out = None, edges1
    steps, done = micro * pairs // HALF, 0

    def edge_piece(count, *deps):
        nonlocal edge_back, edge_out, done
        count = min(count, steps - done)
        if count:
            edge_back, edge_out = run_edge_backward(
                late, done, count, edge_back, edge_out, cot, x0, x1, piece_rows, edge_weights,
                consts, deps,
            )
            done += count

    stages = stages_of(devices)
    digits = [((me >> at) & ((1 << width_) - 1)).astype(jnp.int32) for at, width_ in stages]
    spot = jnp.zeros((), jnp.int32)
    for digit, (at, width_) in zip(digits, stages):
        spot = (spot << width_) | digit
    received = [swapped(sent, "dp", 1)]
    edge_piece(1, sent, early_edge)
    edge_tiles = run_edge_tiles(late_me, early_other, late_edge, sums, edge_back)
    edges = (edge_tiles, swapped(edge_tiles, "dp", 1))
    edge_at = packed_tiles(width, ff) * (ROWS // 16) - blocks // 2
    held, hidden = packed, (edge_back,)
    for (at, width_), digit in list(zip(stages, digits))[1:]:
        held, *sent = run_split(
            held, received, 1 << width_, jnp.stack([digit, digits[0]]), F32, edges, edge_at, hidden
        )
        received = [swapped(part, "dp", (k + 1) << at) for k, part in enumerate(sent)]
        edge_piece(2, *sent)
        edges, edge_at, hidden = (), None, (edge_back,)
    (piece,) = run_split(held, received, 1, jnp.zeros((2,), jnp.int32), BF16, deps=hidden)
    for index, (at, width_) in list(enumerate(stages))[::-1]:
        received = [swapped(piece, "dp", (k + 1) << at) for k in range((1 << width_) - 1)]
        if index:
            edge_piece(2, piece)
            piece = run_join([piece, *received], (edge_back,))
    per = blocks // devices
    own_half = piece.reshape(devices // 2, per, 16, LANES)
    other_half = received[0].reshape(devices // 2, per, 16, LANES)
    edge_piece(steps)
    *squares, up, down_t, edge_grad, vectors, summed = run_unpack(
        spot.reshape(1), own_half, other_half, width, ff
    )
    stats = summed[:, 0:2].T if fits else sum_small(sums, "dp")

    def matrix(array):
        return jnp.transpose(array, (1, 0, 2))

    total = micro * pairs * 2 * devices
    means = stats[0] / total
    variances = stats[1] / total - means * means
    shape = (1, micro, pairs, 2, width)
    return (
        pick(new0, new1).reshape(shape),
        jnp.transpose(edge_out, (0, 2, 1, 3))[None],
        rows[: new0.shape[0]].reshape(shape),
        jnp.transpose(edge_back, (0, 2, 1, 3))[None],
        *[matrix(square) for square in squares],
        vectors[0:1],
        vectors[1:2],
        matrix(up),
        jnp.transpose(down_t, (1, 2, 0)),
        vectors[2:3],
        vectors[3:4],
        matrix(edge_grad),
        jnp.stack([means, variances])[None],
    )


def solution(mesh):
    data4 = P(None, "dp", None, None)
    square = P("section", None, None)
    row = P("section", None)
    acts = P("section", None, "dp", None, None)
    return jax.shard_map(
        shards,
        mesh=mesh,
        in_specs=(
            data4, data4, P(None, "dp", None), data4,
            square, square, square, square, row, row, square, square, row, row, square,
            data4, data4,
        ),
        out_specs=(
            acts, acts, acts, acts,
            square, square, square, square, row, row, square, square, row, row, square,
            square,
        ),
        check_vma=False,
    )
```

```python
import functools
import math

import jax
import jax.numpy as jnp
import numpy as np
from jax import lax
from jax.experimental import pallas as pl
from jax.experimental.pallas import tpu as pltpu
from jax.sharding import PartitionSpec as P

HEADS = 12
EPS = 1e-05
BIG = 1e30
GROUP = 8
HALF = 2 * GROUP
LANES = 128
ROWS = 304
VMEM = 56 * 1024 * 1024

F32 = jnp.float32
BF16 = jnp.bfloat16


def mm(a, b):
    return lax.dot_general(a, b, (((1,), (0,)), ((), ())), preferred_element_type=F32)


def mm_nt(a, b):
    return lax.dot_general(a, b, (((1,), (1,)), ((), ())), preferred_element_type=F32)


def mm_tn(a, b):
    return lax.dot_general(a, b, (((0,), (0,)), ((), ())), preferred_element_type=F32)


def tiles_of(width):
    return -(-width // LANES)


def dead_lane(width):
    base = width - (tiles_of(width) - 1) * LANES
    return -(-(base + GROUP) // 8) * 8


def constants(width):
    rows = HEADS * HALF
    head = np.arange(rows) // HALF
    pair = (np.arange(rows) % HALF) // 2
    slot = np.arange(rows) % HALF
    head_width = width // HEADS
    own = (np.arange(width)[None, :] // head_width == head[:, None]).astype(np.float32)
    base = width - (tiles_of(width) - 1) * LANES
    dead = dead_lane(width)
    bias = np.zeros((rows, LANES), np.float32)
    for p in range(GROUP):
        bias[:, base + p] = np.where(pair == p, 0.0, -BIG)
    for s in range(HALF):
        bias[:, dead + s] = np.where(slot == s, -BIG, 0.0)
    one_hot = np.zeros((GROUP, LANES), np.float32)
    for p in range(GROUP):
        one_hot[p, base + p] = 1.0
    center = np.zeros((HALF, LANES), np.float32)
    for r in range(HALF):
        center[r, base + r // 2] = 1.0
        for s in range(HALF):
            center[r, dead + s] = float(s % 2 != r % 2)
    return (
        jnp.asarray(own, BF16),
        jnp.asarray(bias, BF16),
        jnp.asarray(one_hot, F32),
        jnp.asarray(center, BF16),
    )


def normalize(values):
    centred = values - jnp.mean(values, axis=-1, keepdims=True)
    inverse = lax.rsqrt(jnp.mean(centred * centred, axis=-1, keepdims=True) + EPS)
    return centred * inverse, inverse


def norm_back(grad, normed, inverse):
    return inverse * (
        grad
        - jnp.mean(grad, axis=-1, keepdims=True)
        - normed * jnp.mean(grad * normed, axis=-1, keepdims=True)
    )


GELU_C = math.sqrt(2.0 / math.pi)


def gelu_parts(x):
    square = x * x
    t = jnp.tanh(GELU_C * x * (1.0 + 0.044715 * square))
    return square, t


def expand(rows16, own):
    return jnp.concatenate([rows16] * HEADS, axis=0) * own


def fold_heads(values, own):
    masked = values * own.astype(F32)
    return jnp.sum(masked.reshape(HEADS, HALF, values.shape[-1]), axis=0)


def build_x(x_ref, slot, e_f32, dead_ref, one_hot_ref, featc_ref, c_rows, width):
    leaves = e_f32.shape[0]
    edge_rows = leaves * GROUP
    last = (tiles_of(width) - 1) * LANES
    place = dead_lane(width)
    rows = [jnp.zeros((place, LANES), F32)]
    rows.append(jnp.concatenate([dead_ref[slot], jnp.zeros((HALF, LANES - leaves), F32)], axis=1))
    rows.append(jnp.zeros((LANES - place - HALF, LANES), F32))
    dead = jnp.transpose(jnp.concatenate(rows, axis=0))[0:leaves]
    feature = dead[:, None, :] + one_hot_ref[...][None, :, :]
    x_ref[slot, 0:edge_rows, last : last + LANES] = feature.reshape(edge_rows, LANES).astype(BF16)
    part = e_f32[:, slot * GROUP : (slot + 1) * GROUP, :].reshape(edge_rows, width)
    x_ref[slot, 0:edge_rows, 0:width] = part.astype(BF16)
    x_ref[slot, edge_rows : edge_rows + HALF, last : last + LANES] = featc_ref[...]
    x_ref[slot, edge_rows : edge_rows + HALF, 0:width] = c_rows


def column_rows(columns):
    rows = columns[0].shape[0]
    lane = lax.broadcasted_iota(jnp.int32, (rows, LANES), 1)
    tile = jnp.zeros((rows, LANES), F32)
    for index, column in enumerate(columns):
        tile = jnp.where(lane == index, column, tile)
    return jnp.transpose(tile)[0 : len(columns)]


def forward_kernel(
    width,
    deps,
    e_ref,
    dead_ref,
    c_ref,
    wq_ref,
    wk_ref,
    wv_ref,
    wo_ref,
    gain1_ref,
    bias1_ref,
    wup_ref,
    wdt_ref,
    gain2_ref,
    bias2_ref,
    own_ref,
    qbias_ref,
    one_hot_ref,
    featc_ref,
    *rest,
):
    newc_ref, x_ref, p_ref, pe_ref, att_ref, q_ref, keys_ref, lse_ref, stat_ref, keys_s = rest[deps:]
    step = pl.program_id(0)
    scale = 1.0 / math.sqrt(width // HEADS)
    last = (tiles_of(width) - 1) * LANES
    slots = x_ref.shape[0]
    cols = HEADS * HALF

    @pl.when(step == 0)
    def _():
        q_ref[...] = mm(c_ref[...], wq_ref[...]).astype(BF16)
        for slot in range(slots):
            keys_s[slot, :, last : last + LANES] = qbias_ref[...]

    own = own_ref[...]
    base = pl.multiple_of(step * slots * HALF, slots * HALF)
    q_rows = q_ref[pl.ds(base, slots * HALF), :]
    q_all = jnp.concatenate(
        [expand(q_rows[s * HALF : (s + 1) * HALF], own) for s in range(slots)], axis=0
    )
    keys = (mm_nt(q_all, wk_ref[...]) * scale).astype(BF16)
    c_rows = c_ref[pl.ds(base, slots * HALF), :]
    e_f32 = e_ref[0].astype(F32)
    for slot in range(slots):
        keys_s[slot, :, 0:width] = keys[slot * cols : (slot + 1) * cols]
        keys_ref[slot] = keys[slot * cols : (slot + 1) * cols]
        build_x(
            x_ref, slot, e_f32, dead_ref, one_hot_ref, featc_ref,
            c_rows[slot * HALF : (slot + 1) * HALF], width,
        )
    scores = [mm_nt(keys_s[slot], x_ref[slot]) for slot in range(slots)]
    probs, logs = [], []
    for slot in range(slots):
        top = jnp.max(scores[slot], axis=1, keepdims=True)
        weights = jnp.exp(scores[slot] - top)
        total = jnp.sum(weights, axis=1, keepdims=True)
        probs.append((weights * (1.0 / total)).astype(BF16))
        logs.append(top + jnp.log(total))
    pes = []
    for slot in range(slots):
        p_ref[slot] = probs[slot]
        pe = mm(probs[slot], x_ref[slot])[:, 0:width].astype(BF16)
        pe_ref[slot] = pe
        pes.append(pe)
    lse_ref[0] = column_rows(logs)
    att = mm(jnp.concatenate(pes, axis=0), wv_ref[...])
    att = jnp.concatenate(
        [fold_heads(att[s * cols : (s + 1) * cols], own) for s in range(slots)], axis=0
    )
    att_ref[pl.ds(base, slots * HALF), :] = att.astype(BF16)

    @pl.when(step == pl.num_programs(0) - 1)
    def _():
        residual = c_ref[...].astype(F32) + mm(att_ref[...], wo_ref[...])
        z1, unused = normalize(residual)
        first = z1 * gain1_ref[...] + bias1_ref[...]
        hidden = mm(first.astype(BF16), wup_ref[...])
        unused, t = gelu_parts(hidden)
        gelu = (0.5 * hidden * (1.0 + t)).astype(BF16)
        z2, unused = normalize(first + mm_nt(gelu, wdt_ref[...]))
        new = (z2 * gain2_ref[...] + bias2_ref[...]).astype(BF16)
        newc_ref[...] = new
        new = new.astype(F32)
        stat_ref[0:1, :] = jnp.sum(new, axis=0, keepdims=True)
        stat_ref[1:2, :] = jnp.sum(new * new, axis=0, keepdims=True)


def whole(shape):
    zeros = (0,) * len(shape)
    return pl.BlockSpec(shape, lambda i, *unused: zeros)


def step_spec(shape, first=0):
    rest = (0,) * (len(shape) - 1)
    return pl.BlockSpec(shape, lambda i, *unused: (first + i,) + rest)


def part_spec(shape, part):
    return pl.BlockSpec(shape, lambda i, *unused: (part, 0))


ANY = pl.BlockSpec(memory_space=pl.ANY)


def run_forward(edges, dead, center, part, params, consts, first, micro, deps=()):
    unused, leaves, pairs, width = edges.shape
    slots = pairs // GROUP
    groups = micro * slots
    x_rows = leaves * GROUP + HALF
    pad = tiles_of(width) * LANES
    cols = HEADS * HALF
    count = groups * HALF
    operands = [
        params["query"], params["key"], params["value"], params["out"],
        params["gain1"], params["bias1"], params["up"], params["down_t"],
        params["gain2"], params["bias2"],
        *consts,
    ]
    return pl.pallas_call(
        functools.partial(forward_kernel, width, len(deps)),
        grid=(micro,),
        in_specs=[
            step_spec((1, leaves, pairs, width), first),
            step_spec((slots, HALF, leaves), first),
            part_spec((count, width), part),
        ]
        + [whole(o.shape) for o in operands]
        + [ANY] * len(deps),
        out_specs=[
            whole((count, width)),
            step_spec((slots, x_rows, pad)),
            step_spec((slots, cols, x_rows)),
            step_spec((slots, cols, width)),
            whole((count, width)),
            whole((count, width)),
            step_spec((slots, cols, width)),
            step_spec((1, slots, cols)),
            whole((2, width)),
        ],
        scratch_shapes=[pltpu.VMEM((slots, cols, pad), BF16)],
        out_shape=[
            jax.ShapeDtypeStruct((count, width), BF16),
            jax.ShapeDtypeStruct((groups, x_rows, pad), BF16),
            jax.ShapeDtypeStruct((groups, cols, x_rows), BF16),
            jax.ShapeDtypeStruct((groups, cols, width), BF16),
            jax.ShapeDtypeStruct((count, width), BF16),
            jax.ShapeDtypeStruct((count, width), BF16),
            jax.ShapeDtypeStruct((groups, cols, width), BF16),
            jax.ShapeDtypeStruct((micro, slots, cols), F32),
            jax.ShapeDtypeStruct((2, width), F32),
        ],
        compiler_params=pltpu.CompilerParams(vmem_limit_bytes=VMEM),
        cost_estimate=cost(10e-6),
        name="layer_forward",
    )(edges, dead, center, *operands, *deps)


def blocks_for(devices, width, ff):
    count = (packed_tiles(width, ff) + tiles_of(width)) * (ROWS // 16)
    return -(-count // devices) * devices


def packed_tiles(width, ff):
    return 4 * (width // LANES) + 2 * (ff // LANES) + 3


def placement(width, ff):
    full, wide = width // LANES, ff // LANES
    rest = 4 * full + 2 * wide
    narrow, broad = width - full * LANES, ff - wide * LANES
    return (
        (0, width, (rest, 0)),
        (full, width, (rest, narrow)),
        (2 * full, width, (rest + 1, 0)),
        (3 * full, width, (rest + 1, narrow)),
        (4 * full, ff, (rest + 2, 0)),
        (4 * full + wide, ff, (rest + 2, broad)),
        (rest + 3, width, (rest + 3 + full, 0)),
    )


SPOT = 64


def sums_fit(devices, width):
    return width % LANES <= SPOT and 4 * devices <= LANES - SPOT


def put_tile(packed_ref, tile, matrix, add=False):
    rows, lanes = matrix.shape
    full = matrix
    if rows < ROWS:
        full = jnp.concatenate([matrix, jnp.zeros((ROWS - rows, lanes), F32)], axis=0)
    if lanes < LANES:
        full = jnp.concatenate([full, jnp.zeros((ROWS, LANES - lanes), F32)], axis=1)
    per = ROWS // 16
    if add:
        full = full + packed_ref[tile * per : (tile + 1) * per].reshape(ROWS, LANES).astype(F32)
    packed_ref[tile * per : (tile + 1) * per] = full.astype(BF16).reshape(per, 16, LANES)


def put_matrix(packed_ref, first_tile, matrix, add=False):
    full = matrix.shape[1] // LANES
    for tile in range(full):
        put_tile(
            packed_ref, first_tile + tile, matrix[:, tile * LANES : (tile + 1) * LANES], add
        )
    return matrix[:, full * LANES :]


def backward_kernel(
    width,
    deps,
    add,
    final,
    core_ref,
    x_ref,
    p_ref,
    pe_ref,
    keys_ref,
    c_ref,
    q_ref,
    att_ref,
    dc_ref,
    wq_ref,
    wk_ref,
    wv_ref,
    wo_ref,
    gain1_ref,
    bias1_ref,
    wup_ref,
    wdt_ref,
    gain2_ref,
    bias2_ref,
    own_ref,
    *rest,
):
    rest = rest[deps:]
    if add:
        before_ref, *rest = rest
    rows_ref, inner_ref, ds_ref, dvals_ref, packed_out_ref, *rest = rest
    if final:
        sent_ref, *rest = rest
    count = c_ref.shape[0]
    cback_ref, da_ref = rows_ref.at[0:count], rows_ref.at[count:]
    packed_ref, packed_sem, dvals_s, dwk_s, dwv_s, dwo_s, vec_s, dq_s, dr_s = rest
    step = pl.program_id(0)
    scale = 1.0 / math.sqrt(width // HEADS)
    last = (tiles_of(width) - 1) * LANES
    places = placement(width, wup_ref.shape[1])
    slots, x_rows, pad = x_ref.shape
    edge_rows = x_rows - HALF
    cols = HEADS * HALF

    @pl.when(step == 0)
    def _():
        if add:
            before = pltpu.make_async_copy(before_ref, packed_ref, packed_sem.at[2])
            before.start()
        dwk_s[...] = jnp.zeros_like(dwk_s)
        dwv_s[...] = jnp.zeros_like(dwv_s)
        for slot in range(slots):
            dvals_s[slot, :, last : last + LANES] = jnp.zeros((cols, LANES), BF16)
        att = att_ref[...]
        z1, inverse1 = normalize(c_ref[...].astype(F32) + mm(att, wo_ref[...]))
        first = z1 * gain1_ref[...] + bias1_ref[...]
        first_low = first.astype(BF16)
        hidden = mm(first_low, wup_ref[...])
        square, t = gelu_parts(hidden)
        gelu = (0.5 * hidden * (1.0 + t)).astype(BF16)
        z2, inverse2 = normalize(first + mm_nt(gelu, wdt_ref[...]))
        dc = dc_ref[0:count, :].astype(F32)
        dgain2 = jnp.sum(dc * z2, axis=0, keepdims=True)
        dbias2 = jnp.sum(dc, axis=0, keepdims=True)
        dr2 = norm_back(dc * gain2_ref[...], z2, inverse2)
        df = dr2.astype(BF16)
        if add:
            before.wait()
        down_rest = put_matrix(packed_ref, places[5][0], mm_tn(df, gelu), add)
        slope = 0.5 * (1.0 + t) + 0.5 * hidden * (1.0 - t * t) * GELU_C * (
            1.0 + 3.0 * 0.044715 * square
        )
        dh = (mm(df, wdt_ref[...]) * slope).astype(BF16)
        up_rest = put_matrix(packed_ref, places[4][0], mm_tn(first_low, dh), add)
        put_tile(packed_ref, places[4][2][0], jnp.concatenate([up_rest, down_rest], axis=1), add)
        dfirst = dr2 + mm_nt(dh, wup_ref[...])
        dgain1 = jnp.sum(dfirst * z1, axis=0, keepdims=True)
        dbias1 = jnp.sum(dfirst, axis=0, keepdims=True)
        dr1 = norm_back(dfirst * gain1_ref[...], z1, inverse1)
        dr_s[...] = dr1
        do = dr1.astype(BF16)
        dwo_s[...] = mm_tn(att, do)
        da_ref[...] = mm_nt(do, wo_ref[...]).astype(BF16)
        for index, vector in enumerate((dgain1, dbias1, dgain2, dbias2)):
            vec_s[index : index + 1, :] = vector

    own = own_ref[...]
    base = pl.multiple_of(step * slots * HALF, slots * HALF)

    def all_heads(ref):
        rows = ref[pl.ds(base, slots * HALF), :]
        return jnp.concatenate(
            [expand(rows[s * HALF : (s + 1) * HALF], own) for s in range(slots)], axis=0
        )

    q_all, da_all = all_heads(q_ref), all_heads(da_ref)
    dvals = mm_nt(da_all, wv_ref[...]).astype(BF16)
    for slot in range(slots):
        dvals_s[slot, :, 0:width] = dvals[slot * cols : (slot + 1) * cols]
        dvals_ref[slot] = dvals[slot * cols : (slot + 1) * cols]
    dprobs = [mm_nt(dvals_s[slot], x_ref[slot]) for slot in range(slots)]
    dscores, inners = [], []
    for slot in range(slots):
        probs = p_ref[slot].astype(F32)
        inner = jnp.sum(probs * dprobs[slot], axis=1, keepdims=True)
        dscores.append((probs * (dprobs[slot] - inner)).astype(BF16))
        ds_ref[slot] = dscores[slot]
        inners.append(inner)
    inner_ref[0] = column_rows(inners)
    dses, parts = [], []
    for slot in range(slots):
        dses.append(mm(dscores[slot], x_ref[slot])[:, 0:width].astype(BF16))
        span = slice(slot * cols, (slot + 1) * cols)
        parts.append(
            mm_tn(dscores[slot][:, edge_rows:], keys_ref[slot])
            + mm_tn(p_ref[slot, :, edge_rows:], dvals[span])
        )
    dse = jnp.concatenate(dses, axis=0)
    pe = pe_ref[...].reshape(slots * cols, width)
    dwk_s[...] += mm_tn(dse, q_all)
    dwv_s[...] += mm_tn(pe, da_all)
    dq = mm(dse, wk_ref[...])
    dq = jnp.concatenate(
        [fold_heads(dq[s * cols : (s + 1) * cols], own) for s in range(slots)], axis=0
    )
    dq_s[pl.ds(base, slots * HALF), :] = (dq * scale).astype(BF16)
    dr_s[pl.ds(base, slots * HALF), :] += jnp.concatenate(parts, axis=0)

    @pl.when(step == pl.num_programs(0) - 1)
    def _():
        dq_all = dq_s[...]
        dwq = jnp.concatenate([mm_tn(c_ref[...], dq_all), vec_s[...]], axis=0)
        query_rest = put_matrix(packed_ref, places[0][0], dwq, add)
        key_rest = put_matrix(packed_ref, places[1][0], dwk_s[...] * scale, add)
        key_rest = jnp.concatenate([key_rest, jnp.zeros((4, key_rest.shape[1]), F32)], axis=0)
        put_tile(
            packed_ref, places[0][2][0], jnp.concatenate([query_rest, key_rest], axis=1), add
        )
        value_rest = put_matrix(packed_ref, places[2][0], dwv_s[...], add)
        out_rest = put_matrix(packed_ref, places[3][0], dwo_s[...], add)
        put_tile(
            packed_ref, places[2][2][0], jnp.concatenate([value_rest, out_rest], axis=1), add
        )
        copy = pltpu.make_async_copy(packed_ref, packed_out_ref, packed_sem.at[0])
        copy.start()
        if final:
            size = sent_ref.shape[0]
            start = pl.multiple_of((1 - core_ref[0]) * size, size)
            copy_half = pltpu.make_async_copy(
                packed_ref.at[pl.ds(start, size)], sent_ref, packed_sem.at[1]
            )
            copy_half.start()
        cback_ref[...] = (dr_s[...] + mm_nt(dq_all, wq_ref[...])).astype(BF16)
        copy.wait()
        if final:
            copy_half.wait()


def run_backward(
    core, x, p, pe, keys, center, q, att, dc, part, dc_part, params, consts, micro, blocks, before, final,
    deps=(),
):
    groups, x_rows, pad = x.shape
    slots = groups // micro
    cols = p.shape[1]
    count, width = q.shape
    operands = [
        q, att, dc,
        params["query"], params["key"], params["value"], params["out"],
        params["gain1"], params["bias1"], params["up"], params["down_t"],
        params["gain2"], params["bias2"],
        consts[0],
    ]
    specs = [whole(o.shape) for o in operands]
    specs[2] = part_spec((count, width), dc_part)
    tail = [*deps] + ([] if before is None else [before])
    half = [jax.ShapeDtypeStruct((blocks // 2, 16, LANES), BF16)] if final else []
    return pl.pallas_call(
        functools.partial(backward_kernel, width, len(deps), before is not None, final),
        grid_spec=pltpu.PrefetchScalarGridSpec(
            num_scalar_prefetch=1,
            grid=(micro,),
            in_specs=[
                step_spec((slots, x_rows, pad)),
                step_spec((slots, cols, x_rows)),
                step_spec((slots, cols, width)),
                step_spec((slots, cols, width)),
                part_spec((count, width), part),
            ]
            + specs
            + [ANY] * len(tail),
            out_specs=[
                whole((2 * count, width)),
                step_spec((1, slots, cols)),
                step_spec((slots, cols, x_rows)),
                step_spec((slots, cols, width)),
                ANY,
            ]
            + [ANY] * len(half),
            scratch_shapes=[
                pltpu.VMEM((blocks, 16, LANES), BF16),
                pltpu.SemaphoreType.DMA((3,)),
                pltpu.VMEM((slots, cols, pad), BF16),
                pltpu.VMEM((width, width), F32),
                pltpu.VMEM((width, width), F32),
                pltpu.VMEM((width, width), F32),
                pltpu.VMEM((4, width), F32),
                pltpu.VMEM((count, width), BF16),
                pltpu.VMEM((count, width), F32),
            ],
        ),
        out_shape=[
            jax.ShapeDtypeStruct((2 * count, width), BF16),
            jax.ShapeDtypeStruct((micro, slots, cols), F32),
            jax.ShapeDtypeStruct((groups, cols, x_rows), BF16),
            jax.ShapeDtypeStruct((groups, cols, width), BF16),
            jax.ShapeDtypeStruct((blocks, 16, LANES), BF16),
        ]
        + half,
        compiler_params=pltpu.CompilerParams(vmem_limit_bytes=VMEM),
        cost_estimate=cost(0.2e-6),
        name="layer_backward",
    )(core, x, p, pe, keys, center, *operands, *tail)


def nothing(like):
    return tuple(
        pl.pallas_call(
            lambda *refs: None, out_specs=[ANY] * len(like), out_shape=list(like), name="nothing"
        )()
    )


def edge_forward_kernel(e_ref, w_ref, dep_ref, out_ref):
    unused, leaves, pairs, width = e_ref.shape
    rows = e_ref[0].reshape(leaves * pairs, width)
    out_ref[0] = mm(rows, w_ref[...]).astype(BF16).reshape(leaves, pairs, width)


def run_edge_forward(edges, weight, dep):
    micro, leaves, pairs, width = edges.shape
    cut = 2 if leaves % 2 == 0 else 1
    block = pl.BlockSpec((1, leaves // cut, pairs, width), lambda i: (i // cut, i % cut, 0, 0))
    return pl.pallas_call(
        edge_forward_kernel,
        grid=(micro * cut,),
        in_specs=[block, whole(weight.shape), pl.BlockSpec(memory_space=pl.ANY)],
        out_specs=block,
        out_shape=jax.ShapeDtypeStruct(edges.shape, BF16),
        compiler_params=pltpu.CompilerParams(vmem_limit_bytes=VMEM),
        cost_estimate=cost(13e-6),
        name="edge_forward",
    )(edges, weight, dep)


def edge_act_kernel(late_ref, e_ref, w_ref, dep_ref, out_ref, in_s, out_s, in_sems, out_sems):
    micro, leaves, pairs, width = e_ref.shape
    cut = 2
    steps, size = micro * cut, leaves // cut

    def part(ref, step):
        return ref.at[lax.div(step, cut), pl.ds(lax.rem(step, cut) * size, size)]

    def fetch(step):
        slot = lax.rem(step, 2)
        return pltpu.make_async_copy(part(e_ref, step), in_s.at[slot], in_sems.at[slot])

    def store(step):
        slot = lax.rem(step, 2)
        return pltpu.make_async_copy(out_s.at[slot], part(out_ref, step), out_sems.at[slot])

    @pl.when(late_ref[0] == 1)
    def _():
        fetch(jnp.int32(0)).start()

        def one_step(step, carry):
            slot = lax.rem(step, 2)

            @pl.when(step + 1 < steps)
            def _():
                fetch(step + 1).start()

            fetch(step).wait()

            @pl.when(step >= 2)
            def _():
                store(step - 2).wait()

            act = mm(in_s[slot].reshape(size * pairs, width), w_ref[...])
            out_s[slot] = act.astype(BF16).reshape(size, pairs, width)
            store(step).start()
            return carry

        lax.fori_loop(0, steps, one_step, 0)
        store(jnp.int32(steps - 2)).wait()
        store(jnp.int32(steps - 1)).wait()


def run_edge_act(late, edges, weight, dep):
    micro, leaves, pairs, width = edges.shape
    blocks = pltpu.VMEM((2, leaves // 2, pairs, width), BF16)
    return pl.pallas_call(
        edge_act_kernel,
        in_specs=[
            pl.BlockSpec(memory_space=pltpu.SMEM), ANY, pl.BlockSpec(memory_space=pltpu.VMEM), ANY
        ],
        out_specs=ANY,
        scratch_shapes=[
            blocks, blocks, pltpu.SemaphoreType.DMA((2,)), pltpu.SemaphoreType.DMA((2,))
        ],
        out_shape=jax.ShapeDtypeStruct(edges.shape, BF16),
        input_output_aliases={1: 0},
        compiler_params=pltpu.CompilerParams(vmem_limit_bytes=VMEM),
        cost_estimate=cost(12e-6),
        name="edge_act",
    )(late, edges, weight, dep)


def edge_weight_kernel(width, e_ref, p_ref, ds_ref, keys_ref, dvals_ref, *rest):
    out_ref = rest[-1]
    slots, cols, unused = p_ref.shape
    leaves = e_ref.shape[1]
    edge_rows = leaves * GROUP

    @pl.when(pl.program_id(0) == 0)
    def _():
        out_ref[...] = jnp.zeros_like(out_ref)

    e_f32 = e_ref[0].astype(F32)
    dses, pes = [], []
    for slot in range(slots):
        part = e_f32[:, slot * GROUP : (slot + 1) * GROUP, :].reshape(edge_rows, width)
        part = part.astype(BF16)
        dses.append(mm(ds_ref[slot, :, 0:edge_rows], part).astype(BF16))
        pes.append(mm(p_ref[slot, :, 0:edge_rows], part).astype(BF16))
    flat = (slots * cols, width)
    out_ref[...] += mm_tn(jnp.concatenate(dses, axis=0), keys_ref[...].reshape(flat)) + mm_tn(
        jnp.concatenate(pes, axis=0), dvals_ref[...].reshape(flat)
    )


def run_edge_weight(edges, p, ds, keys, dvals, *deps):
    micro, leaves, pairs, width = edges.shape
    groups, cols, x_rows = p.shape
    slots = groups // micro
    return pl.pallas_call(
        functools.partial(edge_weight_kernel, width),
        grid=(micro,),
        in_specs=[
            step_spec((1, leaves, pairs, width)),
            step_spec((slots, cols, x_rows)),
            step_spec((slots, cols, x_rows)),
            step_spec((slots, cols, width)),
            step_spec((slots, cols, width)),
        ]
        + [ANY] * len(deps),
        out_specs=whole((width, width)),
        out_shape=jax.ShapeDtypeStruct((width, width), F32),
        compiler_params=pltpu.CompilerParams(vmem_limit_bytes=VMEM),
        cost_estimate=cost(8e-6),
        name="edge_weight",
    )(edges, p, ds, keys, dvals, *deps)


def edge_cross_kernel(e_ref, cot_ref, dep_ref, out_ref, total_ref):
    step = pl.program_id(0)
    unused, leaves, pairs, width = e_ref.shape
    flat = (leaves * pairs, width)

    @pl.when(step == 0)
    def _():
        total_ref[...] = jnp.zeros_like(total_ref)

    total_ref[...] += mm_tn(e_ref[0].reshape(flat), cot_ref[0].reshape(flat))

    @pl.when(step == pl.num_programs(0) - 1)
    def _():
        out_ref[...] = total_ref[...].astype(BF16)


def run_edge_cross(edges, cot, dep):
    micro, leaves, pairs, width = edges.shape
    cut = 2 if leaves % 2 == 0 else 1
    block = pl.BlockSpec((1, leaves // cut, pairs, width), lambda i: (i // cut, i % cut, 0, 0))
    return pl.pallas_call(
        edge_cross_kernel,
        grid=(micro * cut,),
        in_specs=[block, block, ANY],
        out_specs=whole((width, width)),
        out_shape=jax.ShapeDtypeStruct((width, width), BF16),
        scratch_shapes=[pltpu.VMEM((width, width), F32)],
        compiler_params=pltpu.CompilerParams(vmem_limit_bytes=VMEM),
        cost_estimate=cost(8e-6),
        name="edge_cross",
    )(edges, cot, dep)


def edge_backward_kernel(
    width,
    first,
    deps,
    late_ref,
    cot_ref,
    x_ref,
    keys_ref,
    dvals_ref,
    lse_ref,
    inner_ref,
    c1_ref,
    rows1_ref,
    weights1_ref,
    sums_ref,
    w0_ref,
    wc_ref,
    own_ref,
    qbias_ref,
    *rest,
):
    out_ref, both_s, sum_s, joint_s = rest[deps:]
    step = pl.program_id(0)
    scale = 1.0 / math.sqrt(width // HEADS)
    last = (tiles_of(width) - 1) * LANES
    leaves = cot_ref.shape[1]
    edge_rows = leaves * GROUP
    cols = HEADS * HALF

    @pl.when(step == 0)
    def _():
        for slot in range(2):
            for layer in range(2):
                both_s[slot, layer, :, last : last + LANES] = qbias_ref[...]
                both_s[slot, 2 + layer, :, last : last + LANES] = jnp.zeros((cols, LANES), BF16)

    base = pl.multiple_of((first + step) * HALF * 2, HALF * 2)
    half = ((first + step) % (lse_ref.shape[1] // 2)) * 2

    def attention_part(layers):
        parts = []
        count = layers * cols
        pad = both_s.shape[-1]
        for slot in range(2):
            x = x_ref[slot, 0:edge_rows, :]
            lse = lse_ref[0, pl.ds(half + slot, 1), :]
            inner = inner_ref[0, pl.ds(half + slot, 1), :]
            if layers == 2:
                lse = jnp.concatenate([lse, sums_ref[0, 0, pl.ds(half + slot, 1), :]], axis=1)
                inner = jnp.concatenate([inner, sums_ref[1, 0, pl.ds(half + slot, 1), :]], axis=1)
            if layers == 2:
                both = both_s[slot].reshape(2 * count, pad)
                product = mm_nt(x, both)
                probs = jnp.exp(product[:, 0:count] - lse)
                dscores = probs * (product[:, count:] - inner)
                part = mm(
                    jnp.concatenate([dscores.astype(BF16), probs.astype(BF16)], axis=1), both
                )
            else:
                keys, dvals = both_s[slot, 0], both_s[slot, 2]
                probs = jnp.exp(mm_nt(x, keys) - lse)
                dscores = probs * (mm_nt(x, dvals) - inner)
                part = mm(dscores.astype(BF16), keys) + mm(probs.astype(BF16), dvals)
            parts.append(part[:, 0:width])
        return parts

    def joined(parts):
        shaped = [part.reshape(leaves, GROUP, width) for part in parts]
        return jnp.concatenate(shaped, axis=1).reshape(leaves * HALF, width)

    cot = cot_ref[0].reshape(leaves * HALF, width)
    sum_s[...] = mm_nt(cot, wc_ref[...])
    for slot in range(2):
        both_s[slot, 0, :, 0:width] = keys_ref[slot]
        both_s[slot, 2, :, 0:width] = dvals_ref[slot]

    @pl.when(late_ref[0] == 1)
    def _():
        grad = sum_s[...] + joined(attention_part(1))
        out_ref[0] = grad.astype(BF16).reshape(leaves, HALF, width)

    @pl.when(late_ref[0] == 0)
    def _():
        own = own_ref[...]
        stacked = weights1_ref.shape[0] // 4

        @pl.when(step == 0)
        def _():
            for index in range(2):
                at = (2 + index) * stacked
                other = weights1_ref[at : at + width, 0:width]
                joint_s[index] = mm(w0_ref[...], other).astype(BF16)

        def all_heads(rows):
            return jnp.concatenate([expand(rows[0:HALF], own), expand(rows[HALF:], own)], axis=0)

        w_query = weights1_ref[stacked : stacked + width, 0:width]
        q1 = mm(c1_ref[pl.ds(base, 2 * HALF), :], w_query).astype(BF16)
        da1 = rows1_ref[pl.ds(c1_ref.shape[0] + base, 2 * HALF), :]
        keys = (mm_nt(all_heads(q1), joint_s[0]) * scale).astype(BF16)
        dvals = mm_nt(all_heads(da1), joint_s[1]).astype(BF16)
        for slot in range(2):
            span = slice(slot * cols, (slot + 1) * cols)
            both_s[slot, 1, :, 0:width] = keys[span]
            both_s[slot, 3, :, 0:width] = dvals[span]
        grad = sum_s[...] + joined(attention_part(2))
        out_ref[0] = grad.astype(BF16).reshape(leaves, HALF, width)


def run_edge_backward(
    late, first, steps, so_far, cot, x, keys, dvals, lse, inner, other, weights, consts, deps
):
    micro, leaves, pairs, width = cot.shape
    per = pairs // HALF
    groups, x_rows, pad = x.shape
    cols = HEADS * HALF
    slots = pairs // GROUP
    block = pl.BlockSpec(
        (1, leaves, HALF, width), lambda i, late: ((first + i) // per, 0, (first + i) % per, 0)
    )
    row_spec = pl.BlockSpec((1, slots, cols), lambda i, late: ((first + i) // per, 0, 0))
    sums_spec = pl.BlockSpec((2, 1, slots, cols), lambda i, late: (0, (first + i) // per, 0, 0))
    center1, rows1, weights1, sums1 = other
    operands = [*weights, consts[0], consts[1]]
    extra = list(deps) + ([] if so_far is None else [so_far])
    inputs = [cot, x, keys, dvals, lse, inner, center1, rows1, weights1, sums1, *operands, *extra]
    return pl.pallas_call(
        functools.partial(edge_backward_kernel, width, first, len(extra)),
        grid_spec=pltpu.PrefetchScalarGridSpec(
            num_scalar_prefetch=1,
            grid=(steps,),
            in_specs=[
                block,
                step_spec((2, x_rows, pad), first),
                step_spec((2, cols, width), first),
                step_spec((2, cols, width), first),
                row_spec,
                row_spec,
                whole(center1.shape),
                whole(rows1.shape),
                whole(weights1.shape),
                sums_spec,
            ]
            + [whole(o.shape) for o in operands]
            + [ANY] * len(extra),
            out_specs=block,
            scratch_shapes=[
                pltpu.VMEM((2, 4, cols, pad), BF16),
                pltpu.VMEM((leaves * HALF, width), F32),
                pltpu.VMEM((2, width, width), BF16),
            ],
        ),
        out_shape=jax.ShapeDtypeStruct(cot.shape, BF16),
        input_output_aliases={} if so_far is None else {len(inputs): 0},
        compiler_params=pltpu.CompilerParams(vmem_limit_bytes=VMEM),
        cost_estimate=cost(7e-6 * steps),
        name="edge_backward",
    )(late, *inputs)


def cost(seconds):
    return pl.CostEstimate(flops=int(seconds * 1e9), bytes_accessed=0, transcendentals=0)


def split_kernel(parts, recv_count, deps, edge_at, digit_ref, *refs):
    held_ref, *refs = refs
    recv_refs, refs = refs[:recv_count], refs[recv_count:]
    if edge_at is not None:
        edge_ref, edge_recv_ref, *refs = refs
    refs = refs[deps:]
    out_refs = refs
    size = held_ref.shape[0] // parts
    digit = digit_ref[0]
    for other, out_ref in enumerate(out_refs):
        span = pl.ds(pl.multiple_of((digit ^ other) * size, size), size)
        total = held_ref[span].astype(F32)
        for recv_ref in recv_refs:
            total = total + recv_ref[span].astype(F32)
        out_ref[...] = total.astype(BF16)
    if edge_at is not None:
        tiles = edge_ref.shape[0]
        for part in range(parts):
            low = max(edge_at, part * size)
            high = min(edge_at + tiles, (part + 1) * size)
            for other, out_ref in enumerate(out_refs):
                if low < high:

                    @pl.when((digit_ref[1] == 1) & ((digit ^ other) == part))
                    def _(low=low, high=high, part=part, out_ref=out_ref):
                        place = slice(low - part * size, high - part * size)
                        source = slice(low - edge_at, high - edge_at)
                        out_ref[place] = (
                            edge_ref[source].astype(F32) + edge_recv_ref[source].astype(F32)
                        ).astype(BF16)


def run_split(held, received, parts, digits, edges=(), edge_at=None, deps=()):
    count = held.shape[0] // 2 if edges else held.shape[0]
    size = count // parts
    inputs = [held, *received, *edges]

    def spec(array):
        return whole(array.shape)

    held_spec = pl.BlockSpec((count, 16, LANES), lambda i, digits: (digits[1], 0, 0))
    out_shape = [jax.ShapeDtypeStruct((size, 16, LANES), BF16)] * parts
    return pl.pallas_call(
        functools.partial(split_kernel, parts, len(received), len(deps), edge_at),
        grid_spec=pltpu.PrefetchScalarGridSpec(
            num_scalar_prefetch=1,
            grid=(1,),
            in_specs=[held_spec if edges else spec(held)]
            + [spec(array) for array in inputs[1:]]
            + [pl.BlockSpec(memory_space=pl.ANY)] * len(deps),
            out_specs=[spec(array) for array in out_shape],
        ),
        out_shape=out_shape,
        compiler_params=pltpu.CompilerParams(vmem_limit_bytes=VMEM),
        cost_estimate=cost(2e-6),
        name="split_gradients",
    )(digits, *inputs, *deps)


def join_kernel(count, deps, *refs):
    out_ref = refs[count + deps]
    size = refs[0].shape[0]
    for index in range(count):
        out_ref[index * size : (index + 1) * size] = refs[index][...]


def run_join(pieces, deps=()):
    size = pieces[0].shape[0]
    spec = pl.BlockSpec(memory_space=pltpu.VMEM)
    return pl.pallas_call(
        functools.partial(join_kernel, len(pieces), len(deps)),
        in_specs=[spec] * len(pieces) + [pl.BlockSpec(memory_space=pl.ANY)] * len(deps),
        out_specs=spec,
        out_shape=jax.ShapeDtypeStruct((size * len(pieces), 16, LANES), BF16),
        compiler_params=pltpu.CompilerParams(vmem_limit_bytes=VMEM),
        cost_estimate=cost(1e-6),
        name="join_gradients",
    )(*pieces, *deps)


def edge_tiles_kernel(late_ref, early_ref, late_edge_ref, sums_ref, dep_ref, out_ref):
    width = early_ref.shape[0]
    full = width // LANES
    edge = jnp.where(late_ref[0] == 1, late_edge_ref[...], early_ref[...]).astype(F32)
    over = put_matrix(out_ref, 0, edge)
    lane = lax.broadcasted_iota(jnp.int32, (LANES, width), 0) - SPOT - 4 * late_ref[1]
    table = jnp.zeros((LANES, width), F32)
    for index in range(2):
        row = sums_ref[index : index + 1, :]
        high = row.astype(BF16).astype(F32)
        table = jnp.where(lane == index, high, table)
        table = jnp.where(lane == 2 + index, row - high, table)
    columns = jnp.transpose(table)
    gap = jnp.zeros((width, LANES - over.shape[1]), F32)
    put_tile(out_ref, full, jnp.concatenate([over, gap], axis=1) + columns)


def run_edge_tiles(late_me, early_edge, late_edge, sums, dep):
    width = early_edge.shape[0]
    per = ROWS // 16
    vmem = pl.BlockSpec(memory_space=pltpu.VMEM)
    return pl.pallas_call(
        edge_tiles_kernel,
        in_specs=[pl.BlockSpec(memory_space=pltpu.SMEM), vmem, vmem, vmem, ANY],
        out_shape=jax.ShapeDtypeStruct((tiles_of(width) * per, 16, LANES), BF16),
        compiler_params=pltpu.CompilerParams(vmem_limit_bytes=VMEM),
        cost_estimate=cost(2e-6),
        name="edge_tiles",
    )(late_me, early_edge, late_edge, sums, dep)


def stack_kernel(*refs):
    *parts, out_ref = refs
    rows = out_ref.shape[0] // len(parts)
    for index, part in enumerate(parts):
        out_ref[index * rows : index * rows + part.shape[0], 0 : part.shape[1]] = part[...]


def run_stack(arrays):
    rows, width = arrays[0].shape
    vmem = pl.BlockSpec(memory_space=pltpu.VMEM)
    shape = (len(arrays) * -(-rows // 16) * 16, tiles_of(width) * LANES)
    return pl.pallas_call(
        stack_kernel,
        in_specs=[vmem] * len(arrays),
        out_shape=jax.ShapeDtypeStruct(shape, BF16),
        compiler_params=pltpu.CompilerParams(vmem_limit_bytes=VMEM),
        cost_estimate=cost(1e-6),
        name="stack_weights",
    )(*arrays)


def stages_of(devices):
    bits = devices.bit_length() - 1
    stages = [(0, 1)]
    if (bits - 1) % 2:
        stages.append((1, 1))
    at = sum(width for unused, width in stages)
    while at < bits:
        stages.append((at, 2))
        at += 2
    return stages


def unpack_kernel(width, ff, count, rows_summed, me_ref, *refs):
    sources, refs = refs[:count], refs[count:]
    total_ref = refs[-1]
    outs, vector_refs, stats_ref = refs[:7], refs[7:11], refs[11]
    me, at = me_ref[0], 0
    for source in sources:
        many, per = source.shape[0], source.shape[1]
        for index in range(many):
            start = pl.multiple_of((me ^ (at + index)) * per, per)
            total_ref[pl.ds(start, per)] = source[index]
        at += many
    rows = ROWS // 16

    def tile_at(tile):
        return total_ref[tile * rows : (tile + 1) * rows].reshape(ROWS, LANES).astype(F32)

    for (first, columns, (spot, lane)), ref in zip(placement(width, ff), outs):
        full = columns // LANES
        for tile in range(full):
            values = tile_at(first + tile)
            ref[:, 0, tile * LANES : (tile + 1) * LANES] = values[0:width]
            if first == 0:
                for row, vector_ref in enumerate(vector_refs):
                    vector_ref[:, tile * LANES : (tile + 1) * LANES] = values[
                        width + row : width + row + 1
                    ]
        values = tile_at(spot)[:, lane : lane + columns - full * LANES]
        ref[:, 0, full * LANES : columns] = values[0:width]
        if first == 0:
            for row, vector_ref in enumerate(vector_refs):
                vector_ref[:, full * LANES : columns] = values[width + row : width + row + 1]
    last = tile_at(placement(width, ff)[6][2][0])[0:width].astype(BF16)
    kind = lax.broadcasted_iota(jnp.int32, (16, LANES), 0)
    lane = lax.broadcasted_iota(jnp.int32, (16, LANES), 1)
    chosen = (lane >= SPOT) & (lane % 2 == kind)
    sums = mm_nt(chosen.astype(F32).astype(BF16), last) * (1.0 / rows_summed)
    stats_ref[0, 0:1, :] = sums[0:1]
    stats_ref[0, 1:2, :] = sums[1:2] - sums[0:1] * sums[0:1]


def run_unpack(me, pieces, width, ff, rows_summed):
    square = jax.ShapeDtypeStruct((width, 1, width), F32)
    wide = jax.ShapeDtypeStruct((width, 1, ff), F32)
    count = sum(piece.shape[0] * piece.shape[1] for piece in pieces)
    spec = pl.BlockSpec(memory_space=pltpu.VMEM)
    return pl.pallas_call(
        functools.partial(unpack_kernel, width, ff, len(pieces), rows_summed),
        in_specs=[pl.BlockSpec(memory_space=pltpu.SMEM)] + [spec] * len(pieces),
        out_shape=[square] * 4 + [wide] * 2 + [square]
        + [jax.ShapeDtypeStruct((1, width), F32)] * 4
        + [jax.ShapeDtypeStruct((1, 2, width), F32)],
        scratch_shapes=[pltpu.VMEM((count, 16, LANES), BF16)],
        compiler_params=pltpu.CompilerParams(vmem_limit_bytes=VMEM),
        name="unpack_gradients",
    )(me, *pieces)


def swapped(array, axis, bit):
    devices = lax.axis_size(axis)
    return lax.ppermute(array, axis, [(i, i ^ bit) for i in range(devices)])


def sum_small(array, axis):
    devices = lax.axis_size(axis)
    for k in range(devices.bit_length() - 1):
        array = array + swapped(array, axis, 1 << k)
    return array


def shards(
    center_input,
    edge_input,
    leaf_count,
    leaf_mask,
    w_query,
    w_key,
    w_value,
    w_out,
    gain_attn,
    bias_attn,
    w_up,
    w_down,
    gain_ffn,
    bias_ffn,
    w_edge,
    center_cot,
    edge_cot,
):
    micro, pairs, leaves, width = edge_input.shape
    ff = w_up.shape[-1]
    section = lax.axis_index("section")
    at_first = section == 0
    late = jnp.where(at_first, 0, 1).astype(jnp.int32).reshape(1)
    early = 1 - late
    consts = constants(width)
    params = {
        "query": w_query[0], "key": w_key[0], "value": w_value[0], "out": w_out[0],
        "gain1": gain_attn, "bias1": bias_attn,
        "up": w_up[0], "down_t": jnp.transpose(w_down[0]),
        "gain2": gain_ffn, "bias2": bias_ffn,
    }
    edges0 = jnp.transpose(edge_input, (0, 2, 1, 3))
    cot = jnp.transpose(edge_cot, (0, 2, 1, 3))
    center0 = center_input.reshape(micro * pairs * 2, width)

    slots = jnp.arange(leaves, dtype=jnp.int32)
    dead = jnp.where((slots < leaf_count[..., None]) & (leaf_mask == 1), 0.0, 1.0)
    dead = dead.reshape(micro * pairs // GROUP, HALF, leaves)

    def pick(at_first_section, at_second_section):
        return jnp.where(at_first, at_first_section, at_second_section)

    def back_to_first(array):
        return lax.ppermute(array, "section", [(1, 0)])

    def branch(on_first, on_second, *operands):
        def unwritten(run):
            return lambda *o: nothing(jax.eval_shape(run, *o))

        return lax.cond(
            at_first, on_first or unwritten(on_second), on_second or unwritten(on_first), *operands
        )

    edge_first = lax.ppermute(w_edge[0], "section", [(0, 1)])
    late_query, center0, dead = lax.optimization_barrier((w_query[0], center0, dead))
    weights1 = back_to_first(run_stack([w_edge[0], late_query, w_key[0], w_value[0]]))
    edge0 = pick(w_edge[0], edge_first)
    devices = lax.axis_size("dp")
    blocks = blocks_for(devices, width, ff)
    me = lax.axis_index("dp")
    core = (me & 1).astype(jnp.int32).reshape(1)

    def forward(edges, dead, center, dep):
        return tuple(run_forward(edges, dead, center, 0, params, consts, 0, micro, dep))

    def backward(*operands):
        operands, deps = operands[:9], operands[9:]
        return tuple(
            run_backward(*operands, 0, 0, params, consts, micro, blocks, None, True, deps)
        )

    layer0 = branch(forward, None, edges0, dead, center0, ())
    new0, x0, p0, pe0, att0, q0, keys0, lse0, stat0 = layer0
    center1 = lax.ppermute(new0, "section", [(0, 1)])
    edges1 = run_edge_forward(edges0, edge0, new0)
    (cross,) = branch(lambda *o: (run_edge_cross(*o),), None, edges0, cot, edges1)
    weights1, cross = lax.optimization_barrier((weights1, cross))
    edge1 = pick(weights1[:width, :width], w_edge[0])
    joint = pick(mm(edge0, edge1).astype(BF16), edge1)
    cross_other = lax.ppermute(cross, "section", [(0, 1)])
    center_cot_rows, edges1 = lax.optimization_barrier(
        (center_cot.reshape(micro * pairs * 2, width), edges1)
    )

    def kept(edges, dead, center, dep, *layer):
        return layer

    layer1 = branch(
        lambda edges, dead, center, dep, dep2, *layer: layer,
        lambda edges, dead, center, dep, dep2, *layer: forward(edges, dead, center, (dep, dep2)),
        edges1, dead, center1, cross, weights1, *layer0,
    )
    new, x, p1, pe1, att1, q1, keys, lse, stat = layer1
    back1 = branch(
        None, backward, core, x, p1, pe1, keys, center1, q1, att1, center_cot_rows, edges1
    )
    rows1, inner1, ds1, dvals1, packed1, sent1 = back1
    rows1_other = back_to_first(rows1)
    sums1_other = back_to_first(jnp.stack([lse, inner1]))

    def weights_on_second(edges0, cross, edge0, edge1, dep, dep2, p, ds, keys, dvals):
        attended = run_edge_weight(edges0, p, ds, keys, dvals, dep, dep2)
        attended = (attended + mm_nt(cross, edge1)).astype(BF16)
        return attended, mm_tn(edge0, cross).astype(BF16)

    early_edge, late_edge = branch(
        None, weights_on_second, edges0, cross_other, edge0, edge1, rows1_other, sums1_other, p1,
        ds1, keys, dvals1,
    )
    edge_out = run_edge_act(late, edges1, edge1, early_edge)

    def keep(*operands):
        return operands[-5:]

    def first_backward(*operands):
        rows, inner, unused, dvals, packed, sent = backward(*operands[:13])
        return rows, inner, dvals, packed, sent

    rows, inner, dvals, packed, sent = branch(
        first_backward, keep, core, x0, p0, pe0, keys0, center0, q0, att0, rows1_other, early_edge,
        sums1_other, edge_out, joint, rows1, inner1, dvals1, packed1, sent1,
    )
    rows, sent = lax.optimization_barrier((rows, sent))
    early_other = back_to_first(early_edge)
    fits = sums_fit(devices, width)
    spot_of_sums = me if fits else jnp.full((), 2 * devices)
    late_me = jnp.concatenate([late, spot_of_sums.astype(jnp.int32).reshape(1)])
    edge_back = None
    steps, done = micro * pairs // HALF, 0

    def edge_piece(count, *deps):
        nonlocal edge_back, done
        count = min(count, steps - done)
        if count:
            edge_back = run_edge_backward(
                late, done, count, edge_back, cot, x, keys, dvals, lse, inner,
                (new, rows1_other, weights1, sums1_other), (edge0, joint), consts, deps,
            )
            done += count

    stages = stages_of(devices)
    digits = [((me >> at) & ((1 << width_) - 1)).astype(jnp.int32) for at, width_ in stages]
    spot = jnp.zeros((), jnp.int32)
    for digit, (at, width_) in zip(digits, stages):
        spot = (spot << width_) | digit
    received = [swapped(sent, "dp", 1)]
    edge_piece(1, sent, early_edge)
    edge_tiles = run_edge_tiles(late_me, early_other, late_edge, stat, edge_back)
    edges = (edge_tiles, swapped(edge_tiles, "dp", 1))
    edge_at = packed_tiles(width, ff) * (ROWS // 16) - blocks // 2
    held, hidden = packed, (edge_back,)
    for (at, width_), digit in list(zip(stages, digits))[1:]:
        held, *sent = run_split(
            held, received, 1 << width_, jnp.stack([digit, digits[0]]), edges, edge_at, hidden
        )
        received = [swapped(part, "dp", (k + 1) << at) for k, part in enumerate(sent)]
        edge_piece(2, *sent)
        edges, edge_at, hidden = (), None, (edge_back,)
    (piece,) = run_split(held, received, 1, jnp.zeros((2,), jnp.int32), deps=hidden)
    for at, width_ in stages[:1:-1]:
        received = [swapped(piece, "dp", (k + 1) << at) for k in range((1 << width_) - 1)]
        edge_piece(2, piece)
        piece = run_join([piece, *received], (edge_back,))
    at, width_ = stages[1]
    own = [piece] + [swapped(piece, "dp", (k + 1) << at) for k in range((1 << width_) - 1)]
    other = [swapped(piece, "dp", 1)]
    edge_piece(steps, piece)
    *rest, edge_back, rows, new = lax.optimization_barrier((*own[1:], edge_back, rows, new))
    back = rows[: new.shape[0]]
    other += [swapped(part, "dp", 1) for part in rest]
    per = blocks // devices
    pieces = [part.reshape(-1, per, 16, LANES) for part in own + other]
    total = micro * pairs * 2 * devices
    *squares, up, down_t, edge_grad, dgain1, dbias1, dgain2, dbias2, stats = run_unpack(
        spot.reshape(1), pieces, width, ff, total
    )
    if not fits:
        means, squared = sum_small(stat, "dp") / total
        stats = jnp.stack([means, squared - means * means])[None]

    def matrix(array):
        return jnp.transpose(array, (1, 0, 2))

    shape = (1, micro, pairs, 2, width)

    return (
        new.reshape(shape),
        jnp.transpose(edge_out, (0, 2, 1, 3))[None],
        back.reshape(shape),
        jnp.transpose(edge_back, (0, 2, 1, 3))[None],
        *[matrix(square) for square in squares],
        dgain1,
        dbias1,
        matrix(up),
        jnp.transpose(down_t, (1, 2, 0)),
        dgain2,
        dbias2,
        matrix(edge_grad),
        stats,
    )


def solution(mesh):
    data4 = P(None, "dp", None, None)
    square = P("section", None, None)
    row = P("section", None)
    acts = P("section", None, "dp", None, None)
    return jax.shard_map(
        shards,
        mesh=mesh,
        in_specs=(
            data4, data4, P(None, "dp", None), data4,
            square, square, square, square, row, row, square, square, row, row, square,
            data4, data4,
        ),
        out_specs=(
            acts, acts, acts, acts,
            square, square, square, square, row, row, square, square, row, row, square,
            square,
        ),
        check_vma=False,
    )
```

```python
import functools
import math

import jax
import jax.numpy as jnp
import numpy as np
from jax import lax
from jax.experimental import pallas as pl
from jax.experimental.pallas import tpu as pltpu
from jax.sharding import PartitionSpec as P

HEADS = 12
EPS = 1e-05
BIG = 1e30
GROUP = 8
HALF = 2 * GROUP
LANES = 128
ROWS = 304
VMEM = 56 * 1024 * 1024

F32 = jnp.float32
BF16 = jnp.bfloat16


def mm(a, b):
    return lax.dot_general(a, b, (((1,), (0,)), ((), ())), preferred_element_type=F32)


def mm_nt(a, b):
    return lax.dot_general(a, b, (((1,), (1,)), ((), ())), preferred_element_type=F32)


def mm_tn(a, b):
    return lax.dot_general(a, b, (((0,), (0,)), ((), ())), preferred_element_type=F32)


def tiles_of(width):
    return -(-width // LANES)


def dead_lane(width):
    base = width - (tiles_of(width) - 1) * LANES
    return -(-(base + GROUP) // 8) * 8


def constants(width):
    rows = HEADS * HALF
    head = np.arange(rows) // HALF
    pair = (np.arange(rows) % HALF) // 2
    slot = np.arange(rows) % HALF
    head_width = width // HEADS
    own = (np.arange(width)[None, :] // head_width == head[:, None]).astype(np.float32)
    base = width - (tiles_of(width) - 1) * LANES
    dead = dead_lane(width)
    bias = np.zeros((rows, LANES), np.float32)
    for p in range(GROUP):
        bias[:, base + p] = np.where(pair == p, 0.0, -BIG)
    for s in range(HALF):
        bias[:, dead + s] = np.where(slot == s, -BIG, 0.0)
    one_hot = np.zeros((GROUP, LANES), np.float32)
    for p in range(GROUP):
        one_hot[p, base + p] = 1.0
    center = np.zeros((HALF, LANES), np.float32)
    for r in range(HALF):
        center[r, base + r // 2] = 1.0
        for s in range(HALF):
            center[r, dead + s] = float(s % 2 != r % 2)
    return (
        jnp.asarray(own, BF16),
        jnp.asarray(bias, BF16),
        jnp.asarray(one_hot, F32),
        jnp.asarray(center, BF16),
    )


def normalize(values):
    centred = values - jnp.mean(values, axis=-1, keepdims=True)
    inverse = lax.rsqrt(jnp.mean(centred * centred, axis=-1, keepdims=True) + EPS)
    return centred * inverse, inverse


def norm_back(grad, normed, inverse):
    return inverse * (
        grad
        - jnp.mean(grad, axis=-1, keepdims=True)
        - normed * jnp.mean(grad * normed, axis=-1, keepdims=True)
    )


GELU_C = math.sqrt(2.0 / math.pi)


def gelu_parts(x):
    square = x * x
    t = jnp.tanh(GELU_C * x * (1.0 + 0.044715 * square))
    return square, t


def expand(rows16, own):
    return jnp.concatenate([rows16] * HEADS, axis=0) * own


def fold_heads(values, own):
    masked = values * own.astype(F32)
    return jnp.sum(masked.reshape(HEADS, HALF, values.shape[-1]), axis=0)


def build_x(x_ref, slot, e_f32, dead_ref, one_hot_ref, featc_ref, c_rows, width):
    leaves = e_f32.shape[0]
    edge_rows = leaves * GROUP
    last = (tiles_of(width) - 1) * LANES
    place = dead_lane(width)
    rows = [jnp.zeros((place, LANES), F32)]
    rows.append(jnp.concatenate([dead_ref[slot], jnp.zeros((HALF, LANES - leaves), F32)], axis=1))
    rows.append(jnp.zeros((LANES - place - HALF, LANES), F32))
    dead = jnp.transpose(jnp.concatenate(rows, axis=0))[0:leaves]
    feature = dead[:, None, :] + one_hot_ref[...][None, :, :]
    x_ref[slot, 0:edge_rows, last : last + LANES] = feature.reshape(edge_rows, LANES).astype(BF16)
    part = e_f32[:, slot * GROUP : (slot + 1) * GROUP, :].reshape(edge_rows, width)
    x_ref[slot, 0:edge_rows, 0:width] = part.astype(BF16)
    x_ref[slot, edge_rows : edge_rows + HALF, last : last + LANES] = featc_ref[...]
    x_ref[slot, edge_rows : edge_rows + HALF, 0:width] = c_rows


def column_rows(columns):
    rows = columns[0].shape[0]
    lane = lax.broadcasted_iota(jnp.int32, (rows, LANES), 1)
    tile = jnp.zeros((rows, LANES), F32)
    for index, column in enumerate(columns):
        tile = jnp.where(lane == index, column, tile)
    return jnp.transpose(tile)[0 : len(columns)]


def forward_kernel(
    width,
    deps,
    e_ref,
    dead_ref,
    c_ref,
    wq_ref,
    wk_ref,
    wv_ref,
    wo_ref,
    gain1_ref,
    bias1_ref,
    wup_ref,
    wdt_ref,
    gain2_ref,
    bias2_ref,
    own_ref,
    qbias_ref,
    one_hot_ref,
    featc_ref,
    *rest,
):
    newc_ref, x_ref, p_ref, pe_ref, att_ref, q_ref, keys_ref, lse_ref, stat_ref, keys_s = rest[deps:]
    step = pl.program_id(0)
    scale = 1.0 / math.sqrt(width // HEADS)
    last = (tiles_of(width) - 1) * LANES
    slots = x_ref.shape[0]
    cols = HEADS * HALF

    @pl.when(step == 0)
    def _():
        q_ref[...] = mm(c_ref[...], wq_ref[...]).astype(BF16)
        for slot in range(slots):
            keys_s[slot, :, last : last + LANES] = qbias_ref[...]

    own = own_ref[...]
    base = pl.multiple_of(step * slots * HALF, slots * HALF)
    q_rows = q_ref[pl.ds(base, slots * HALF), :]
    q_all = jnp.concatenate(
        [expand(q_rows[s * HALF : (s + 1) * HALF], own) for s in range(slots)], axis=0
    )
    keys = (mm_nt(q_all, wk_ref[...]) * scale).astype(BF16)
    c_rows = c_ref[pl.ds(base, slots * HALF), :]
    e_f32 = e_ref[0].astype(F32)
    for slot in range(slots):
        keys_s[slot, :, 0:width] = keys[slot * cols : (slot + 1) * cols]
        keys_ref[slot] = keys[slot * cols : (slot + 1) * cols]
        build_x(
            x_ref, slot, e_f32, dead_ref, one_hot_ref, featc_ref,
            c_rows[slot * HALF : (slot + 1) * HALF], width,
        )
    scores = [mm_nt(keys_s[slot], x_ref[slot]) for slot in range(slots)]
    probs, logs = [], []
    for slot in range(slots):
        top = jnp.max(scores[slot], axis=1, keepdims=True)
        weights = jnp.exp(scores[slot] - top)
        total = jnp.sum(weights, axis=1, keepdims=True)
        probs.append((weights * (1.0 / total)).astype(BF16))
        logs.append(top + jnp.log(total))
    pes = []
    for slot in range(slots):
        p_ref[slot] = probs[slot]
        pe = mm(probs[slot], x_ref[slot])[:, 0:width].astype(BF16)
        pe_ref[slot] = pe
        pes.append(pe)
    lse_ref[0] = column_rows(logs)
    att = mm(jnp.concatenate(pes, axis=0), wv_ref[...])
    att = jnp.concatenate(
        [fold_heads(att[s * cols : (s + 1) * cols], own) for s in range(slots)], axis=0
    )
    att_ref[pl.ds(base, slots * HALF), :] = att.astype(BF16)

    @pl.when(step == pl.num_programs(0) - 1)
    def _():
        residual = c_ref[...].astype(F32) + mm(att_ref[...], wo_ref[...])
        z1, unused = normalize(residual)
        first = z1 * gain1_ref[...] + bias1_ref[...]
        hidden = mm(first.astype(BF16), wup_ref[...])
        unused, t = gelu_parts(hidden)
        gelu = (0.5 * hidden * (1.0 + t)).astype(BF16)
        z2, unused = normalize(first + mm_nt(gelu, wdt_ref[...]))
        new = (z2 * gain2_ref[...] + bias2_ref[...]).astype(BF16)
        newc_ref[...] = new
        new = new.astype(F32)
        stat_ref[0:1, :] = jnp.sum(new, axis=0, keepdims=True)
        stat_ref[1:2, :] = jnp.sum(new * new, axis=0, keepdims=True)


def whole(shape):
    zeros = (0,) * len(shape)
    return pl.BlockSpec(shape, lambda i, *unused: zeros)


def step_spec(shape, first=0):
    rest = (0,) * (len(shape) - 1)
    return pl.BlockSpec(shape, lambda i, *unused: (first + i,) + rest)


def part_spec(shape, part):
    return pl.BlockSpec(shape, lambda i, *unused: (part, 0))


ANY = pl.BlockSpec(memory_space=pl.ANY)


def run_forward(edges, dead, center, part, params, consts, first, micro, deps=()):
    unused, leaves, pairs, width = edges.shape
    slots = pairs // GROUP
    groups = micro * slots
    x_rows = leaves * GROUP + HALF
    pad = tiles_of(width) * LANES
    cols = HEADS * HALF
    count = groups * HALF
    operands = [
        params["query"], params["key"], params["value"], params["out"],
        params["gain1"], params["bias1"], params["up"], params["down_t"],
        params["gain2"], params["bias2"],
        *consts,
    ]
    return pl.pallas_call(
        functools.partial(forward_kernel, width, len(deps)),
        grid=(micro,),
        in_specs=[
            step_spec((1, leaves, pairs, width), first),
            step_spec((slots, HALF, leaves), first),
            part_spec((count, width), part),
        ]
        + [whole(o.shape) for o in operands]
        + [ANY] * len(deps),
        out_specs=[
            whole((count, width)),
            step_spec((slots, x_rows, pad)),
            step_spec((slots, cols, x_rows)),
            step_spec((slots, cols, width)),
            whole((count, width)),
            whole((count, width)),
            step_spec((slots, cols, width)),
            step_spec((1, slots, cols)),
            whole((2, width)),
        ],
        scratch_shapes=[pltpu.VMEM((slots, cols, pad), BF16)],
        out_shape=[
            jax.ShapeDtypeStruct((count, width), BF16),
            jax.ShapeDtypeStruct((groups, x_rows, pad), BF16),
            jax.ShapeDtypeStruct((groups, cols, x_rows), BF16),
            jax.ShapeDtypeStruct((groups, cols, width), BF16),
            jax.ShapeDtypeStruct((count, width), BF16),
            jax.ShapeDtypeStruct((count, width), BF16),
            jax.ShapeDtypeStruct((groups, cols, width), BF16),
            jax.ShapeDtypeStruct((micro, slots, cols), F32),
            jax.ShapeDtypeStruct((2, width), F32),
        ],
        compiler_params=pltpu.CompilerParams(vmem_limit_bytes=VMEM),
        cost_estimate=cost(10e-6),
        name="layer_forward",
    )(edges, dead, center, *operands, *deps)


def blocks_for(devices, width, ff):
    count = (packed_tiles(width, ff) + tiles_of(width)) * (ROWS // 16)
    return -(-count // devices) * devices


def packed_tiles(width, ff):
    return 4 * (width // LANES) + 2 * (ff // LANES) + 3


def placement(width, ff):
    full, wide = width // LANES, ff // LANES
    rest = 4 * full + 2 * wide
    narrow, broad = width - full * LANES, ff - wide * LANES
    return (
        (0, width, (rest, 0)),
        (full, width, (rest, narrow)),
        (2 * full, width, (rest + 1, 0)),
        (3 * full, width, (rest + 1, narrow)),
        (4 * full, ff, (rest + 2, 0)),
        (4 * full + wide, ff, (rest + 2, broad)),
        (rest + 3, width, (rest + 3 + full, 0)),
    )


SPOT = 64


def sums_fit(devices, width):
    return width % LANES <= SPOT and 4 * devices <= LANES - SPOT


def put_tile(packed_ref, tile, matrix):
    rows, lanes = matrix.shape
    full = matrix
    if rows < ROWS:
        full = jnp.concatenate([matrix, jnp.zeros((ROWS - rows, lanes), F32)], axis=0)
    if lanes < LANES:
        full = jnp.concatenate([full, jnp.zeros((ROWS, LANES - lanes), F32)], axis=1)
    per = ROWS // 16
    packed_ref[tile * per : (tile + 1) * per] = full.astype(BF16).reshape(per, 16, LANES)


def put_matrix(packed_ref, first_tile, matrix):
    full = matrix.shape[1] // LANES
    for tile in range(full):
        put_tile(packed_ref, first_tile + tile, matrix[:, tile * LANES : (tile + 1) * LANES])
    return matrix[:, full * LANES :]


def backward_kernel(
    width,
    deps,
    begin,
    end,
    first,
    core_ref,
    x_ref,
    p_ref,
    pe_ref,
    keys_ref,
    lse_ref,
    c_ref,
    q_ref,
    att_ref,
    dc_ref,
    wq_ref,
    wk_ref,
    wv_ref,
    wo_ref,
    gain1_ref,
    bias1_ref,
    wup_ref,
    wdt_ref,
    gain2_ref,
    bias2_ref,
    own_ref,
    *rest,
):
    rest = rest[deps:]
    if not begin:
        sums_in, vec_in, dq_in, dr_in, da_in, packed_in, *rest = rest
    if end:
        cback_ref, inner_ref, dvals_ref, packed_out_ref, sent_ref, *rest = rest
    else:
        sums_out, vec_out, dq_out, dr_out, inner_ref, dvals_ref, packed_out_ref, *rest = rest
    if begin:
        da_out, *rest = rest
    if begin and end:
        ds_ref, *rest = rest
    packed_ref, packed_sem, dvals_s, dwk_s, dwv_s, dwo_s, vec_s, dq_s, dr_s, da_s = rest
    count = c_ref.shape[0]
    step = pl.program_id(0)
    scale = 1.0 / math.sqrt(width // HEADS)
    last = (tiles_of(width) - 1) * LANES
    places = placement(width, wup_ref.shape[1])
    slots, x_rows, pad = x_ref.shape
    edge_rows = x_rows - HALF
    cols = HEADS * HALF

    @pl.when(step == 0)
    def _():
        for slot in range(slots):
            dvals_s[slot, :, last : last + LANES] = jnp.zeros((cols, LANES), BF16)
        if not begin:
            pltpu.make_async_copy(packed_in, packed_ref, packed_sem.at[0]).start()
            for total_ref, total in zip((dwk_s, dwv_s, dwo_s), (0, 1, 2)):
                total_ref[...] = sums_in[total]
            vec_s[...] = vec_in[...]
            dq_s[...] = dq_in[...]
            dr_s[...] = dr_in[...]
            da_s[...] = da_in[...]
            return
        dwk_s[...] = jnp.zeros_like(dwk_s)
        dwv_s[...] = jnp.zeros_like(dwv_s)
        att = att_ref[...]
        z1, inverse1 = normalize(c_ref[...].astype(F32) + mm(att, wo_ref[...]))
        first = z1 * gain1_ref[...] + bias1_ref[...]
        first_low = first.astype(BF16)
        hidden = mm(first_low, wup_ref[...])
        square, t = gelu_parts(hidden)
        gelu = (0.5 * hidden * (1.0 + t)).astype(BF16)
        z2, inverse2 = normalize(first + mm_nt(gelu, wdt_ref[...]))
        dc = dc_ref[0:count, :].astype(F32)
        dgain2 = jnp.sum(dc * z2, axis=0, keepdims=True)
        dbias2 = jnp.sum(dc, axis=0, keepdims=True)
        dr2 = norm_back(dc * gain2_ref[...], z2, inverse2)
        df = dr2.astype(BF16)
        down_rest = put_matrix(packed_ref, places[5][0], mm_tn(df, gelu))
        slope = 0.5 * (1.0 + t) + 0.5 * hidden * (1.0 - t * t) * GELU_C * (
            1.0 + 3.0 * 0.044715 * square
        )
        dh = (mm(df, wdt_ref[...]) * slope).astype(BF16)
        up_rest = put_matrix(packed_ref, places[4][0], mm_tn(first_low, dh))
        put_tile(packed_ref, places[4][2][0], jnp.concatenate([up_rest, down_rest], axis=1))
        dfirst = dr2 + mm_nt(dh, wup_ref[...])
        dgain1 = jnp.sum(dfirst * z1, axis=0, keepdims=True)
        dbias1 = jnp.sum(dfirst, axis=0, keepdims=True)
        dr1 = norm_back(dfirst * gain1_ref[...], z1, inverse1)
        dr_s[...] = dr1
        do = dr1.astype(BF16)
        dwo_s[...] = mm_tn(att, do)
        da_s[...] = mm_nt(do, wo_ref[...]).astype(BF16)
        da_out[...] = da_s[...]
        for index, vector in enumerate((dgain1, dbias1, dgain2, dbias2)):
            vec_s[index : index + 1, :] = vector
        if not end:
            pltpu.make_async_copy(packed_ref, packed_out_ref, packed_sem.at[0]).start()

    own = own_ref[...]
    base = pl.multiple_of((first + step) * slots * HALF, slots * HALF)

    def all_heads(ref):
        rows = ref[pl.ds(base, slots * HALF), :]
        return jnp.concatenate(
            [expand(rows[s * HALF : (s + 1) * HALF], own) for s in range(slots)], axis=0
        )

    q_all, da_all = all_heads(q_ref), all_heads(da_s)
    dvals = mm_nt(da_all, wv_ref[...]).astype(BF16)
    for slot in range(slots):
        dvals_s[slot, :, 0:width] = dvals[slot * cols : (slot + 1) * cols]
        dvals_ref[slot] = dvals[slot * cols : (slot + 1) * cols]
    dprobs = [mm_nt(dvals_s[slot], x_ref[slot]) for slot in range(slots)]
    dscores, inners = [], []
    for slot in range(slots):
        probs = p_ref[slot].astype(F32)
        inner = jnp.sum(probs * dprobs[slot], axis=1, keepdims=True)
        dscores.append((probs * (dprobs[slot] - inner)).astype(BF16))
        if begin and end:
            ds_ref[slot] = dscores[slot]
        inners.append(inner)
    inner_ref[0, 0] = lse_ref[0]
    inner_ref[1, 0] = column_rows(inners)
    dses, parts = [], []
    for slot in range(slots):
        dses.append(mm(dscores[slot], x_ref[slot])[:, 0:width].astype(BF16))
        span = slice(slot * cols, (slot + 1) * cols)
        parts.append(
            mm_tn(dscores[slot][:, edge_rows:], keys_ref[slot])
            + mm_tn(p_ref[slot, :, edge_rows:], dvals[span])
        )
    dse = jnp.concatenate(dses, axis=0)
    pe = pe_ref[...].reshape(slots * cols, width)
    dwk_s[...] += mm_tn(dse, q_all)
    dwv_s[...] += mm_tn(pe, da_all)
    dq = mm(dse, wk_ref[...])
    dq = jnp.concatenate(
        [fold_heads(dq[s * cols : (s + 1) * cols], own) for s in range(slots)], axis=0
    )
    dq_s[pl.ds(base, slots * HALF), :] = (dq * scale).astype(BF16)
    dr_s[pl.ds(base, slots * HALF), :] += jnp.concatenate(parts, axis=0)

    @pl.when(step == pl.num_programs(0) - 1)
    def _():
        if not end:
            for total, total_ref in enumerate((dwk_s, dwv_s, dwo_s)):
                sums_out[total] = total_ref[...]
            vec_out[...] = vec_s[...]
            dq_out[...] = dq_s[...]
            dr_out[...] = dr_s[...]
            pltpu.make_async_copy(packed_ref, packed_out_ref, packed_sem.at[0]).wait()
            return
        if not begin:
            pltpu.make_async_copy(packed_in, packed_ref, packed_sem.at[0]).wait()
        dq_all = dq_s[...]
        dwq = jnp.concatenate([mm_tn(c_ref[...], dq_all), vec_s[...]], axis=0)
        query_rest = put_matrix(packed_ref, places[0][0], dwq)
        key_rest = put_matrix(packed_ref, places[1][0], dwk_s[...] * scale)
        key_rest = jnp.concatenate([key_rest, jnp.zeros((4, key_rest.shape[1]), F32)], axis=0)
        put_tile(
            packed_ref, places[0][2][0], jnp.concatenate([query_rest, key_rest], axis=1)
        )
        value_rest = put_matrix(packed_ref, places[2][0], dwv_s[...])
        out_rest = put_matrix(packed_ref, places[3][0], dwo_s[...])
        put_tile(
            packed_ref, places[2][2][0], jnp.concatenate([value_rest, out_rest], axis=1)
        )
        copy = pltpu.make_async_copy(packed_ref, packed_out_ref, packed_sem.at[0])
        copy.start()
        size = sent_ref.shape[0]
        start = pl.multiple_of((1 - core_ref[0]) * size, size)
        copy_half = pltpu.make_async_copy(
            packed_ref.at[pl.ds(start, size)], sent_ref, packed_sem.at[1]
        )
        copy_half.start()
        cback_ref[...] = (dr_s[...] + mm_nt(dq_all, wq_ref[...])).astype(BF16)
        copy.wait()
        copy_half.wait()


def run_backward(
    core, x, p, pe, keys, lse, center, q, att, dc, params, consts, first, steps, micro, blocks, state,
    end, deps=(),
):
    groups, x_rows, pad = x.shape
    slots = groups // micro
    cols = p.shape[1]
    count, width = q.shape
    begin = state is None
    operands = [
        center, q, att, dc,
        params["query"], params["key"], params["value"], params["out"],
        params["gain1"], params["bias1"], params["up"], params["down_t"],
        params["gain2"], params["bias2"],
        consts[0],
    ]
    specs = [whole(o.shape) for o in operands]
    if not begin:
        for index in (2, 3, 7, 8, 9, 10, 11, 12, 13):
            specs[index] = ANY
    state = [] if begin else list(state)
    state_specs = [] if begin else [whole(o.shape) for o in state[:5]] + [ANY]
    packed = jax.ShapeDtypeStruct((blocks, 16, LANES), BF16)
    rows = jax.ShapeDtypeStruct((count, width), BF16)
    sums = jax.ShapeDtypeStruct((2, micro, slots, cols), F32)
    dvals = jax.ShapeDtypeStruct((groups, cols, width), BF16)
    kept = [
        (sums, pl.BlockSpec((2, 1, slots, cols), lambda i, core: (0, first + i, 0, 0))),
        (dvals, step_spec((slots, cols, width), first)),
        (packed, ANY),
    ]
    if end:
        half = jax.ShapeDtypeStruct((blocks // 2, 16, LANES), BF16)
        outs = [(rows, whole(rows.shape)), *kept, (half, ANY)]
    else:
        totals = [((3, width, width), F32), ((4, width), F32), ((count, width), BF16)]
        totals.append(((count, width), F32))
        outs = [(jax.ShapeDtypeStruct(shape, kind), whole(shape)) for shape, kind in totals] + kept
    if begin:
        outs.append((rows, whole(rows.shape)))
    if begin and end:
        dscores = jax.ShapeDtypeStruct((groups, cols, x_rows), BF16)
        outs.append((dscores, step_spec((slots, cols, x_rows))))
    inputs = [core, x, p, pe, keys, lse, *operands, *deps, *state]
    return pl.pallas_call(
        functools.partial(backward_kernel, width, len(deps), begin, end, first),
        grid_spec=pltpu.PrefetchScalarGridSpec(
            num_scalar_prefetch=1,
            grid=(steps,),
            in_specs=[
                step_spec((slots, x_rows, pad), first),
                step_spec((slots, cols, x_rows), first),
                step_spec((slots, cols, width), first),
                step_spec((slots, cols, width), first),
                step_spec((1, slots, cols), first),
            ]
            + specs
            + [ANY] * len(deps)
            + state_specs,
            out_specs=[spec for unused, spec in outs],
            scratch_shapes=[
                pltpu.VMEM((blocks, 16, LANES), BF16),
                pltpu.SemaphoreType.DMA((2,)),
                pltpu.VMEM((slots, cols, pad), BF16),
                pltpu.VMEM((width, width), F32),
                pltpu.VMEM((width, width), F32),
                pltpu.VMEM((width, width), F32),
                pltpu.VMEM((4, width), F32),
                pltpu.VMEM((count, width), BF16),
                pltpu.VMEM((count, width), F32),
                pltpu.VMEM((count, width), BF16),
            ],
        ),
        out_shape=[shape for shape, unused in outs],
        compiler_params=pltpu.CompilerParams(vmem_limit_bytes=VMEM),
        cost_estimate=cost(0.2e-6),
        name="layer_backward",
    )(*inputs)


def nothing(like):
    return tuple(
        pl.pallas_call(
            lambda *refs: None, out_specs=[ANY] * len(like), out_shape=list(like), name="nothing"
        )()
    )


def edge_forward_kernel(e_ref, w_ref, dep_ref, out_ref):
    unused, leaves, pairs, width = e_ref.shape
    rows = e_ref[0].reshape(leaves * pairs, width)
    out_ref[0] = mm(rows, w_ref[...]).astype(BF16).reshape(leaves, pairs, width)


def run_edge_forward(edges, weight, dep):
    micro, leaves, pairs, width = edges.shape
    cut = 2 if leaves % 2 == 0 else 1
    block = pl.BlockSpec((1, leaves // cut, pairs, width), lambda i: (i // cut, i % cut, 0, 0))
    return pl.pallas_call(
        edge_forward_kernel,
        grid=(micro * cut,),
        in_specs=[block, whole(weight.shape), pl.BlockSpec(memory_space=pl.ANY)],
        out_specs=block,
        out_shape=jax.ShapeDtypeStruct(edges.shape, BF16),
        compiler_params=pltpu.CompilerParams(vmem_limit_bytes=VMEM),
        cost_estimate=cost(13e-6),
        name="edge_forward",
    )(edges, weight, dep)


def edge_act_kernel(e_ref, w_ref, out_ref):
    unused, leaves, pairs, width = e_ref.shape
    act = mm(e_ref[0].reshape(leaves * pairs, width), w_ref[...])
    out_ref[0] = act.astype(BF16).reshape(leaves, pairs, width)


def run_edge_act(edges, weight, first, steps):
    micro, leaves, pairs, width = edges.shape
    per = pairs // HALF
    block = pl.BlockSpec(
        (1, leaves, HALF, width), lambda i: ((first + i) // per, 0, (first + i) % per, 0)
    )
    return pl.pallas_call(
        edge_act_kernel,
        grid=(steps,),
        in_specs=[block, whole(weight.shape)],
        out_specs=block,
        out_shape=jax.ShapeDtypeStruct(edges.shape, BF16),
        input_output_aliases={0: 0},
        compiler_params=pltpu.CompilerParams(vmem_limit_bytes=VMEM),
        cost_estimate=cost(2e-6 * steps),
        name="edge_act",
    )(edges, weight)


def edge_weight_kernel(
    width, e_ref, p_ref, ds_ref, keys_ref, dvals_ref, cross_ref, w0_ref, w1_ref, *rest
):
    early_ref, late_ref, out_ref = rest[-3:]
    slots, cols, unused = p_ref.shape
    leaves = e_ref.shape[1]
    edge_rows = leaves * GROUP

    @pl.when(pl.program_id(0) == 0)
    def _():
        out_ref[...] = jnp.zeros_like(out_ref)

    e_f32 = e_ref[0].astype(F32)
    dses, pes = [], []
    for slot in range(slots):
        part = e_f32[:, slot * GROUP : (slot + 1) * GROUP, :].reshape(edge_rows, width)
        part = part.astype(BF16)
        dses.append(mm(ds_ref[slot, :, 0:edge_rows], part).astype(BF16))
        pes.append(mm(p_ref[slot, :, 0:edge_rows], part).astype(BF16))
    flat = (slots * cols, width)
    out_ref[...] += mm_tn(jnp.concatenate(dses, axis=0), keys_ref[...].reshape(flat)) + mm_tn(
        jnp.concatenate(pes, axis=0), dvals_ref[...].reshape(flat)
    )

    @pl.when(pl.program_id(0) == pl.num_programs(0) - 1)
    def _():
        cross = cross_ref[...]
        early_ref[...] = (out_ref[...] + mm_nt(cross, w1_ref[...])).astype(BF16)
        late_ref[...] = mm_tn(w0_ref[...], cross).astype(BF16)


def run_edge_weight(edges, p, ds, keys, dvals, cross, w0, w1, *deps):
    micro, leaves, pairs, width = edges.shape
    groups, cols, x_rows = p.shape
    slots = groups // micro
    return pl.pallas_call(
        functools.partial(edge_weight_kernel, width),
        grid=(micro,),
        in_specs=[
            step_spec((1, leaves, pairs, width)),
            step_spec((slots, cols, x_rows)),
            step_spec((slots, cols, x_rows)),
            step_spec((slots, cols, width)),
            step_spec((slots, cols, width)),
        ]
        + [whole((width, width))] * 3
        + [ANY] * len(deps),
        out_specs=[whole((width, width))] * 2,
        out_shape=[jax.ShapeDtypeStruct((width, width), BF16)] * 2,
        scratch_shapes=[pltpu.VMEM((width, width), F32)],
        compiler_params=pltpu.CompilerParams(vmem_limit_bytes=VMEM),
        cost_estimate=cost(8e-6),
        name="edge_weight",
    )(edges, p, ds, keys, dvals, cross, w0, w1, *deps)


def edge_cross_kernel(e_ref, cot_ref, dep_ref, out_ref, total_ref):
    step = pl.program_id(0)
    unused, leaves, pairs, width = e_ref.shape
    flat = (leaves * pairs, width)

    @pl.when(step == 0)
    def _():
        total_ref[...] = jnp.zeros_like(total_ref)

    total_ref[...] += mm_tn(e_ref[0].reshape(flat), cot_ref[0].reshape(flat))

    @pl.when(step == pl.num_programs(0) - 1)
    def _():
        out_ref[...] = total_ref[...].astype(BF16)


def run_edge_cross(edges, cot, dep):
    micro, leaves, pairs, width = edges.shape
    cut = 2 if leaves % 2 == 0 else 1
    block = pl.BlockSpec((1, leaves // cut, pairs, width), lambda i: (i // cut, i % cut, 0, 0))
    return pl.pallas_call(
        edge_cross_kernel,
        grid=(micro * cut,),
        in_specs=[block, block, ANY],
        out_specs=whole((width, width)),
        out_shape=jax.ShapeDtypeStruct((width, width), BF16),
        scratch_shapes=[pltpu.VMEM((width, width), F32)],
        compiler_params=pltpu.CompilerParams(vmem_limit_bytes=VMEM),
        cost_estimate=cost(8e-6),
        name="edge_cross",
    )(edges, cot, dep)


def edge_backward_kernel(width, first, early, deps, *refs):
    if early:
        through_ref, x_ref, keys_ref, dvals_ref, own_sums_ref, *refs = refs
        c1_ref, rows1_ref, weights1_ref, sums_ref, w0_ref, own_ref, qbias_ref, *refs = refs
        out_ref, both_s, joint_s = refs[deps:]
    else:
        cot_ref, x_ref, keys_ref, dvals_ref, own_sums_ref, wc_ref, qbias_ref, *refs = refs
        out_ref, both_s = refs[deps:]
    step = pl.program_id(0)
    scale = 1.0 / math.sqrt(width // HEADS)
    last = (tiles_of(width) - 1) * LANES
    leaves = out_ref.shape[1]
    edge_rows = leaves * GROUP
    cols = HEADS * HALF

    @pl.when(step == 0)
    def _():
        for slot in range(2):
            for layer in range(2):
                both_s[slot, layer, :, last : last + LANES] = qbias_ref[...]
                both_s[slot, 2 + layer, :, last : last + LANES] = jnp.zeros((cols, LANES), BF16)

    base = pl.multiple_of((first + step) * HALF * 2, HALF * 2)
    half = ((first + step) % (own_sums_ref.shape[2] // 2)) * 2

    def attention_part(layers):
        parts = []
        count = layers * cols
        pad = both_s.shape[-1]
        for slot in range(2):
            x = x_ref[slot, 0:edge_rows, :]
            lse = own_sums_ref[0, 0, pl.ds(half + slot, 1), :]
            inner = own_sums_ref[1, 0, pl.ds(half + slot, 1), :]
            if layers == 2:
                lse = jnp.concatenate([lse, sums_ref[0, 0, pl.ds(half + slot, 1), :]], axis=1)
                inner = jnp.concatenate([inner, sums_ref[1, 0, pl.ds(half + slot, 1), :]], axis=1)
            if layers == 2:
                both = both_s[slot].reshape(2 * count, pad)
                product = mm_nt(x, both)
                probs = jnp.exp(product[:, 0:count] - lse)
                dscores = probs * (product[:, count:] - inner)
                part = mm(
                    jnp.concatenate([dscores.astype(BF16), probs.astype(BF16)], axis=1), both
                )
            else:
                keys, dvals = both_s[slot, 0], both_s[slot, 2]
                probs = jnp.exp(mm_nt(x, keys) - lse)
                dscores = probs * (mm_nt(x, dvals) - inner)
                part = mm(dscores.astype(BF16), keys) + mm(probs.astype(BF16), dvals)
            parts.append(part[:, 0:width])
        return parts

    def joined(parts):
        shaped = [part.reshape(leaves, GROUP, width) for part in parts]
        return jnp.concatenate(shaped, axis=1).reshape(leaves * HALF, width)

    for slot in range(2):
        both_s[slot, 0, :, 0:width] = keys_ref[slot]
        both_s[slot, 2, :, 0:width] = dvals_ref[slot]

    if not early:
        cot = cot_ref[0].reshape(leaves * HALF, width)
        grad = mm_nt(cot, wc_ref[...]) + joined(attention_part(1))
        out_ref[0] = grad.astype(BF16).reshape(leaves, HALF, width)
        return

    own = own_ref[...]
    stacked = weights1_ref.shape[0] // 4

    @pl.when(step == 0)
    def _():
        for index in range(2):
            at = (2 + index) * stacked
            other = weights1_ref[at : at + width, 0:width]
            joint_s[index] = mm(w0_ref[...], other).astype(BF16)

    def all_heads(rows):
        return jnp.concatenate([expand(rows[0:HALF], own), expand(rows[HALF:], own)], axis=0)

    w_query = weights1_ref[stacked : stacked + width, 0:width]
    q1 = mm(c1_ref[pl.ds(base, 2 * HALF), :], w_query).astype(BF16)
    da1 = rows1_ref[pl.ds(base, 2 * HALF), :]
    keys = (mm_nt(all_heads(q1), joint_s[0]) * scale).astype(BF16)
    dvals = mm_nt(all_heads(da1), joint_s[1]).astype(BF16)
    for slot in range(2):
        span = slice(slot * cols, (slot + 1) * cols)
        both_s[slot, 1, :, 0:width] = keys[span]
        both_s[slot, 3, :, 0:width] = dvals[span]
    through = through_ref[0].reshape(leaves * HALF, width)
    grad = through.astype(F32) + joined(attention_part(2))
    out_ref[0] = grad.astype(BF16).reshape(leaves, HALF, width)


def run_edge_backward(first, steps, so_far, early, grad, own, other, weights, consts, deps):
    micro, leaves, pairs, width = grad.shape
    per = pairs // HALF
    x, keys, dvals, sums = own
    groups, x_rows, pad = x.shape
    cols = HEADS * HALF
    slots = pairs // GROUP
    block = pl.BlockSpec(
        (1, leaves, HALF, width), lambda i: ((first + i) // per, 0, (first + i) % per, 0)
    )
    sums_spec = pl.BlockSpec((2, 1, slots, cols), lambda i: (0, (first + i) // per, 0, 0))
    operands = [*other[:3], *weights, consts[0], consts[1]] if early else [weights[0], consts[1]]
    specs = [whole(o.shape) for o in operands]
    scratch = [pltpu.VMEM((2, 4, cols, pad), BF16)]
    if early:
        operands.insert(3, other[3])
        specs.insert(3, sums_spec)
        scratch.append(pltpu.VMEM((2, width, width), BF16))
    extra = list(deps) + ([] if so_far is None else [so_far])
    inputs = [grad, x, keys, dvals, sums, *operands, *extra]
    return pl.pallas_call(
        functools.partial(edge_backward_kernel, width, first, early, len(extra)),
        grid=(steps,),
        in_specs=[
            block,
            step_spec((2, x_rows, pad), first),
            step_spec((2, cols, width), first),
            step_spec((2, cols, width), first),
            sums_spec,
        ]
        + specs
        + [ANY] * len(extra),
        out_specs=block,
        scratch_shapes=scratch,
        out_shape=jax.ShapeDtypeStruct(grad.shape, BF16),
        input_output_aliases={} if so_far is None else {len(inputs) - 1: 0},
        compiler_params=pltpu.CompilerParams(vmem_limit_bytes=VMEM),
        cost_estimate=cost(7e-6 * steps),
        name="edge_backward",
    )(*inputs)


def cost(seconds):
    return pl.CostEstimate(flops=int(seconds * 1e9), bytes_accessed=0, transcendentals=0)


def split_kernel(parts, recv_count, deps, edge_at, digit_ref, *refs):
    held_ref, *refs = refs
    recv_refs, refs = refs[:recv_count], refs[recv_count:]
    if edge_at is not None:
        edge_ref, edge_recv_ref, *refs = refs
    refs = refs[deps:]
    out_refs = refs
    size = held_ref.shape[0] // parts
    digit = digit_ref[0]
    for other, out_ref in enumerate(out_refs):
        span = pl.ds(pl.multiple_of((digit ^ other) * size, size), size)
        total = held_ref[span].astype(F32)
        for recv_ref in recv_refs:
            total = total + recv_ref[span].astype(F32)
        out_ref[...] = total.astype(BF16)
    if edge_at is not None:
        tiles = edge_ref.shape[0]
        for part in range(parts):
            low = max(edge_at, part * size)
            high = min(edge_at + tiles, (part + 1) * size)
            for other, out_ref in enumerate(out_refs):
                if low < high:

                    @pl.when((digit_ref[1] == 1) & ((digit ^ other) == part))
                    def _(low=low, high=high, part=part, out_ref=out_ref):
                        place = slice(low - part * size, high - part * size)
                        source = slice(low - edge_at, high - edge_at)
                        out_ref[place] = (
                            edge_ref[source].astype(F32) + edge_recv_ref[source].astype(F32)
                        ).astype(BF16)


def run_split(held, received, parts, digits, edges=(), edge_at=None, deps=()):
    count = held.shape[0] // 2 if edges else held.shape[0]
    size = count // parts
    inputs = [held, *received, *edges]

    def spec(array):
        return whole(array.shape)

    held_spec = pl.BlockSpec((count, 16, LANES), lambda i, digits: (digits[1], 0, 0))
    out_shape = [jax.ShapeDtypeStruct((size, 16, LANES), BF16)] * parts
    return pl.pallas_call(
        functools.partial(split_kernel, parts, len(received), len(deps), edge_at),
        grid_spec=pltpu.PrefetchScalarGridSpec(
            num_scalar_prefetch=1,
            grid=(1,),
            in_specs=[held_spec if edges else spec(held)]
            + [spec(array) for array in inputs[1:]]
            + [pl.BlockSpec(memory_space=pl.ANY)] * len(deps),
            out_specs=[spec(array) for array in out_shape],
        ),
        out_shape=out_shape,
        compiler_params=pltpu.CompilerParams(vmem_limit_bytes=VMEM),
        cost_estimate=cost(2e-6),
        name="split_gradients",
    )(digits, *inputs, *deps)


def join_kernel(count, deps, *refs):
    out_ref = refs[count + deps]
    size = refs[0].shape[0]
    for index in range(count):
        out_ref[index * size : (index + 1) * size] = refs[index][...]


def run_join(pieces, deps=()):
    size = pieces[0].shape[0]
    spec = pl.BlockSpec(memory_space=pltpu.VMEM)
    return pl.pallas_call(
        functools.partial(join_kernel, len(pieces), len(deps)),
        in_specs=[spec] * len(pieces) + [pl.BlockSpec(memory_space=pl.ANY)] * len(deps),
        out_specs=spec,
        out_shape=jax.ShapeDtypeStruct((size * len(pieces), 16, LANES), BF16),
        compiler_params=pltpu.CompilerParams(vmem_limit_bytes=VMEM),
        cost_estimate=cost(1e-6),
        name="join_gradients",
    )(*pieces, *deps)


def edge_tiles_kernel(late_ref, early_ref, late_edge_ref, sums_ref, dep_ref, out_ref):
    width = early_ref.shape[0]
    full = width // LANES
    edge = jnp.where(late_ref[0] == 1, late_edge_ref[...], early_ref[...]).astype(F32)
    over = put_matrix(out_ref, 0, edge)
    lane = lax.broadcasted_iota(jnp.int32, (LANES, width), 0) - SPOT - 4 * late_ref[1]
    table = jnp.zeros((LANES, width), F32)
    for index in range(2):
        row = sums_ref[index : index + 1, :]
        high = row.astype(BF16).astype(F32)
        table = jnp.where(lane == index, high, table)
        table = jnp.where(lane == 2 + index, row - high, table)
    columns = jnp.transpose(table)
    gap = jnp.zeros((width, LANES - over.shape[1]), F32)
    put_tile(out_ref, full, jnp.concatenate([over, gap], axis=1) + columns)


def run_edge_tiles(late_me, early_edge, late_edge, sums, dep):
    width = early_edge.shape[0]
    per = ROWS // 16
    vmem = pl.BlockSpec(memory_space=pltpu.VMEM)
    return pl.pallas_call(
        edge_tiles_kernel,
        in_specs=[pl.BlockSpec(memory_space=pltpu.SMEM), vmem, vmem, vmem, ANY],
        out_shape=jax.ShapeDtypeStruct((tiles_of(width) * per, 16, LANES), BF16),
        compiler_params=pltpu.CompilerParams(vmem_limit_bytes=VMEM),
        cost_estimate=cost(2e-6),
        name="edge_tiles",
    )(late_me, early_edge, late_edge, sums, dep)


def stack_kernel(*refs):
    *parts, dep_ref, out_ref = refs
    rows = out_ref.shape[0] // len(parts)
    for index, part in enumerate(parts):
        out_ref[index * rows : index * rows + part.shape[0], 0 : part.shape[1]] = part[...]


def run_stack(arrays, dep):
    rows, width = arrays[0].shape
    vmem = pl.BlockSpec(memory_space=pltpu.VMEM)
    shape = (len(arrays) * -(-rows // 16) * 16, tiles_of(width) * LANES)
    return pl.pallas_call(
        stack_kernel,
        in_specs=[vmem] * len(arrays) + [ANY],
        out_shape=jax.ShapeDtypeStruct(shape, BF16),
        compiler_params=pltpu.CompilerParams(vmem_limit_bytes=VMEM),
        cost_estimate=cost(1e-6),
        name="stack_weights",
    )(*arrays, dep)


def stages_of(devices):
    bits = devices.bit_length() - 1
    stages = [(0, 1)]
    if (bits - 1) % 2:
        stages.append((1, 1))
    at = sum(width for unused, width in stages)
    while at < bits:
        stages.append((at, 2))
        at += 2
    return stages


def unpack_kernel(width, ff, count, rows_summed, me_ref, *refs):
    sources, refs = refs[:count], refs[count:]
    total_ref = refs[-1]
    outs, vector_refs, stats_ref = refs[:7], refs[7:11], refs[11]
    me, at = me_ref[0], 0
    for source in sources:
        many, per = source.shape[0], source.shape[1]
        for index in range(many):
            start = pl.multiple_of((me ^ (at + index)) * per, per)
            total_ref[pl.ds(start, per)] = source[index]
        at += many
    rows = ROWS // 16

    def tile_at(tile):
        return total_ref[tile * rows : (tile + 1) * rows].reshape(ROWS, LANES).astype(F32)

    for (first, columns, (spot, lane)), ref in zip(placement(width, ff), outs):
        full = columns // LANES
        for tile in range(full):
            values = tile_at(first + tile)
            ref[:, 0, tile * LANES : (tile + 1) * LANES] = values[0:width]
            if first == 0:
                for row, vector_ref in enumerate(vector_refs):
                    vector_ref[:, tile * LANES : (tile + 1) * LANES] = values[
                        width + row : width + row + 1
                    ]
        values = tile_at(spot)[:, lane : lane + columns - full * LANES]
        ref[:, 0, full * LANES : columns] = values[0:width]
        if first == 0:
            for row, vector_ref in enumerate(vector_refs):
                vector_ref[:, full * LANES : columns] = values[width + row : width + row + 1]
    last = tile_at(placement(width, ff)[6][2][0])[0:width].astype(BF16)
    kind = lax.broadcasted_iota(jnp.int32, (16, LANES), 0)
    lane = lax.broadcasted_iota(jnp.int32, (16, LANES), 1)
    chosen = (lane >= SPOT) & (lane % 2 == kind)
    sums = mm_nt(chosen.astype(F32).astype(BF16), last) * (1.0 / rows_summed)
    stats_ref[0, 0:1, :] = sums[0:1]
    stats_ref[0, 1:2, :] = sums[1:2] - sums[0:1] * sums[0:1]


def run_unpack(me, pieces, width, ff, rows_summed):
    square = jax.ShapeDtypeStruct((width, 1, width), F32)
    wide = jax.ShapeDtypeStruct((width, 1, ff), F32)
    count = sum(piece.shape[0] * piece.shape[1] for piece in pieces)
    spec = pl.BlockSpec(memory_space=pltpu.VMEM)
    return pl.pallas_call(
        functools.partial(unpack_kernel, width, ff, len(pieces), rows_summed),
        in_specs=[pl.BlockSpec(memory_space=pltpu.SMEM)] + [spec] * len(pieces),
        out_shape=[square] * 4 + [wide] * 2 + [square]
        + [jax.ShapeDtypeStruct((1, width), F32)] * 4
        + [jax.ShapeDtypeStruct((1, 2, width), F32)],
        scratch_shapes=[pltpu.VMEM((count, 16, LANES), BF16)],
        compiler_params=pltpu.CompilerParams(vmem_limit_bytes=VMEM),
        name="unpack_gradients",
    )(me, *pieces)


def swapped(array, axis, bit):
    devices = lax.axis_size(axis)
    return lax.ppermute(array, axis, [(i, i ^ bit) for i in range(devices)])


def sum_small(array, axis):
    devices = lax.axis_size(axis)
    for k in range(devices.bit_length() - 1):
        array = array + swapped(array, axis, 1 << k)
    return array


def shards(
    center_input,
    edge_input,
    leaf_count,
    leaf_mask,
    w_query,
    w_key,
    w_value,
    w_out,
    gain_attn,
    bias_attn,
    w_up,
    w_down,
    gain_ffn,
    bias_ffn,
    w_edge,
    center_cot,
    edge_cot,
):
    micro, pairs, leaves, width = edge_input.shape
    ff = w_up.shape[-1]
    section = lax.axis_index("section")
    at_first = section == 0
    late = jnp.where(at_first, 0, 1).astype(jnp.int32).reshape(1)
    early = 1 - late
    consts = constants(width)
    params = {
        "query": w_query[0], "key": w_key[0], "value": w_value[0], "out": w_out[0],
        "gain1": gain_attn, "bias1": bias_attn,
        "up": w_up[0], "down_t": jnp.transpose(w_down[0]),
        "gain2": gain_ffn, "bias2": bias_ffn,
    }
    edges0 = jnp.transpose(edge_input, (0, 2, 1, 3))
    cot = jnp.transpose(edge_cot, (0, 2, 1, 3))
    center0 = center_input.reshape(micro * pairs * 2, width)

    slots = jnp.arange(leaves, dtype=jnp.int32)
    dead = jnp.where((slots < leaf_count[..., None]) & (leaf_mask == 1), 0.0, 1.0)
    dead = dead.reshape(micro * pairs // GROUP, HALF, leaves)

    def pick(at_first_section, at_second_section):
        return jnp.where(at_first, at_first_section, at_second_section)

    def back_to_first(array):
        return lax.ppermute(array, "section", [(1, 0)])

    def branch(on_first, on_second, *operands):
        def unwritten(run):
            return lambda *o: nothing(jax.eval_shape(run, *o))

        return lax.cond(
            at_first, on_first or unwritten(on_second), on_second or unwritten(on_first), *operands
        )

    edge_first = lax.ppermute(w_edge[0], "section", [(0, 1)])
    late_query, center0, dead = lax.optimization_barrier((w_query[0], center0, dead))
    (weights1,) = branch(
        None, lambda *o: (run_stack(o[:4], o[4]),), w_edge[0], late_query, w_key[0], w_value[0],
        edge_first,
    )
    weights1 = back_to_first(weights1)
    edge0 = pick(w_edge[0], edge_first)
    devices = lax.axis_size("dp")
    blocks = blocks_for(devices, width, ff)
    me = lax.axis_index("dp")
    core = (me & 1).astype(jnp.int32).reshape(1)

    def forward(edges, dead, center, dep):
        return tuple(run_forward(edges, dead, center, 0, params, consts, 0, micro, dep))

    def backward(*operands):
        return tuple(
            run_backward(*operands, params, consts, 0, micro, micro, blocks, None, True)
        )

    layer0 = branch(forward, None, edges0, dead, center0, ())
    new0, x0, p0, pe0, att0, q0, keys0, lse0, stat0 = layer0
    center1 = lax.ppermute(new0, "section", [(0, 1)])
    edges1 = run_edge_forward(edges0, edge0, new0)
    (cross,) = branch(lambda *o: (run_edge_cross(*o),), None, edges0, cot, edges1)
    weights1, cross = lax.optimization_barrier((weights1, cross))
    edge1 = pick(weights1[:width, :width], w_edge[0])
    joint = pick(mm(edge0, edge1).astype(BF16), edge1)
    cross_other = lax.ppermute(cross, "section", [(0, 1)])
    center_cot_rows, edges1 = lax.optimization_barrier(
        (center_cot.reshape(micro * pairs * 2, width), edges1)
    )

    layer1 = branch(
        None, lambda edges, dead, center, *deps: forward(edges, dead, center, deps),
        edges1, dead, center1, cross, weights1,
    )
    new1, x1, p1, pe1, att1, q1, keys1, lse1, stat1 = layer1
    new, stat = pick(new0, new1), pick(stat0, stat1)
    back1, sums1, dvals1, packed1, sent1, da1, ds1 = branch(
        None, backward, core, x1, p1, pe1, keys1, lse1, center1, q1, att1, center_cot_rows
    )
    back1_other, da1_other = back_to_first(back1), back_to_first(da1)
    sums1_other = back_to_first(sums1)

    (through,) = branch(lambda *o: (run_edge_forward(*o),), None, cot, joint.T, back1)
    early_edge, late_edge = branch(
        None, lambda *o: tuple(run_edge_weight(*o)), edges0, p1, ds1, keys1, dvals1, cross_other,
        edge0, edge1, through,
    )
    cut = micro - 1 if micro > 1 and pairs == 2 * HALF else micro

    def first_part(*operands):
        operands, deps = operands[:10], operands[10:]
        return tuple(
            run_backward(
                *operands, params, consts, 0, cut, micro, blocks, None, cut == micro, deps
            )
        )

    def last_part(*operands):
        operands, state, deps = operands[:10], operands[10:16], operands[16:-3]
        back, own_sums, dvals, packed, sent = run_backward(
            *operands, params, consts, cut, micro - cut, micro, blocks, state, True, deps
        )
        return back, packed, sent, own_sums, dvals

    def kept(*operands):
        like = jax.eval_shape(last_part, *operands)
        return (*operands[-3:], *nothing(like[3:]))

    own0 = (core, x0, p0, pe0, keys0, lse0, center0, q0, att0, back1_other)
    partial = branch(first_part, None, *own0, through, early_edge)
    early_other = back_to_first(early_edge)
    fits = sums_fit(devices, width)
    spot_of_sums = me if fits else jnp.full((), 2 * devices)
    late_me = jnp.concatenate([late, spot_of_sums.astype(jnp.int32).reshape(1)])
    edge_tiles = run_edge_tiles(late_me, early_other, late_edge, stat, partial[0])
    old = (back1, packed1, sent1)
    if cut == micro:
        back0, sums0, dvals0, packed0, sent0, da0 = partial[:6]
        back, packed, sent = branch(
            lambda *o: o[:3], lambda *o: o[3:], back0, packed0, sent0, *old
        )
        early_parts = [(sums0, dvals0)] * micro
    else:
        totals, vec, dq, dr, sums0, dvals0, packed0, da0 = partial
        back, packed, sent, last_sums, last_dvals = branch(
            last_part, kept, *own0, totals, vec, dq, dr, da0, packed0, da1_other, sums1_other,
            edge_tiles, *old,
        )
        early_parts = [(sums0, dvals0)] * cut + [(last_sums, last_dvals)]
    back, sent = lax.optimization_barrier((back, sent))
    edge_out = edges1
    edge_back = None
    steps, done = micro * pairs // HALF, 0

    def edge_piece(count, *deps):
        nonlocal edge_back, edge_out, done
        count = min(count, steps - done)
        if count:
            early_sums, early_dvals = early_parts[done * HALF // pairs]
            other = (new0, da1_other, weights1, sums1_other)
            tail = (*deps, edge_back) if done else deps

            def piece(early, grad, weights, edges, own, other, tail):
                so_far = tail[len(deps)] if done else None
                back = run_edge_backward(
                    done, count, so_far, early, grad, own, other, weights, consts,
                    tail[: len(deps)],
                )
                return back, edges if early else run_edge_act(edges, weights[1], done, count)

            edge_back, edge_out = lax.cond(
                at_first,
                lambda cot, through, edges, edge0, edge1, own0, own1, other, tail: piece(
                    True, through, [edge0], edges, own0, other, tail
                ),
                lambda cot, through, edges, edge0, edge1, own0, own1, other, tail: piece(
                    False, cot, [edge1, edge1], edges, own1, other, tail
                ),
                cot, through, edge_out, edge0, edge1, (x0, keys0, early_dvals, early_sums),
                (x1, keys1, dvals1, sums1), other, tail,
            )
            done += count

    stages = stages_of(devices)
    digits = [((me >> at) & ((1 << width_) - 1)).astype(jnp.int32) for at, width_ in stages]
    spot = jnp.zeros((), jnp.int32)
    for digit, (at, width_) in zip(digits, stages):
        spot = (spot << width_) | digit
    received = [swapped(sent, "dp", 1)]
    edges = (edge_tiles, swapped(edge_tiles, "dp", 1))
    edge_at = packed_tiles(width, ff) * (ROWS // 16) - blocks // 2
    held, hidden = packed, ()
    for (at, width_), digit in list(zip(stages, digits))[1:]:
        held, *sent = run_split(
            held, received, 1 << width_, jnp.stack([digit, digits[0]]), edges, edge_at, hidden
        )
        received = [swapped(part, "dp", (k + 1) << at) for k, part in enumerate(sent)]
        edge_piece(2, *sent)
        edges, edge_at, hidden = (), None, (edge_back,)
    (piece,) = run_split(held, received, 1, jnp.zeros((2,), jnp.int32), deps=hidden)
    for at, width_ in stages[:1:-1]:
        received = [swapped(piece, "dp", (k + 1) << at) for k in range((1 << width_) - 1)]
        edge_piece(2, piece)
        piece = run_join([piece, *received], (edge_back,))
    at, width_ = stages[1]
    own = [piece] + [swapped(piece, "dp", (k + 1) << at) for k in range((1 << width_) - 1)]
    other = [swapped(piece, "dp", 1)]
    edge_piece(steps, piece)
    *rest, edge_back, back, new = lax.optimization_barrier((*own[1:], edge_back, back, new))
    other += [swapped(part, "dp", 1) for part in rest]
    per = blocks // devices
    pieces = [part.reshape(-1, per, 16, LANES) for part in own + other]
    total = micro * pairs * 2 * devices
    *squares, up, down_t, edge_grad, dgain1, dbias1, dgain2, dbias2, stats = run_unpack(
        spot.reshape(1), pieces, width, ff, total
    )
    if not fits:
        means, squared = sum_small(stat, "dp") / total
        stats = jnp.stack([means, squared - means * means])[None]

    def matrix(array):
        return jnp.transpose(array, (1, 0, 2))

    shape = (1, micro, pairs, 2, width)

    return (
        new.reshape(shape),
        jnp.transpose(edge_out, (0, 2, 1, 3))[None],
        back.reshape(shape),
        jnp.transpose(edge_back, (0, 2, 1, 3))[None],
        *[matrix(square) for square in squares],
        dgain1,
        dbias1,
        matrix(up),
        jnp.transpose(down_t, (1, 2, 0)),
        dgain2,
        dbias2,
        matrix(edge_grad),
        stats,
    )


def solution(mesh):
    data4 = P(None, "dp", None, None)
    square = P("section", None, None)
    row = P("section", None)
    acts = P("section", None, "dp", None, None)
    return jax.shard_map(
        shards,
        mesh=mesh,
        in_specs=(
            data4, data4, P(None, "dp", None), data4,
            square, square, square, square, row, row, square, square, row, row, square,
            data4, data4,
        ),
        out_specs=(
            acts, acts, acts, acts,
            square, square, square, square, row, row, square, square, row, row, square,
            square,
        ),
        check_vma=False,
    )
```

```python
import functools
import math

import jax
import jax.numpy as jnp
import numpy as np
from jax import lax
from jax.experimental import pallas as pl
from jax.experimental.pallas import tpu as pltpu
from jax.sharding import PartitionSpec as P

HEADS = 12
EPS = 1e-05
BIG = 1e30
GROUP = 8
HALF = 2 * GROUP
LANES = 128
ROWS = 304
VMEM = 56 * 1024 * 1024

F32 = jnp.float32
BF16 = jnp.bfloat16


def mm(a, b):
    return lax.dot_general(a, b, (((1,), (0,)), ((), ())), preferred_element_type=F32)


def mm_nt(a, b):
    return lax.dot_general(a, b, (((1,), (1,)), ((), ())), preferred_element_type=F32)


def mm_tn(a, b):
    return lax.dot_general(a, b, (((0,), (0,)), ((), ())), preferred_element_type=F32)


def tiles_of(width):
    return -(-width // LANES)


def dead_lane(width):
    base = width - (tiles_of(width) - 1) * LANES
    return -(-(base + GROUP) // 8) * 8


def constants(width):
    rows = HEADS * HALF
    head = np.arange(rows) // HALF
    pair = (np.arange(rows) % HALF) // 2
    slot = np.arange(rows) % HALF
    head_width = width // HEADS
    own = (np.arange(width)[None, :] // head_width == head[:, None]).astype(np.float32)
    base = width - (tiles_of(width) - 1) * LANES
    dead = dead_lane(width)
    bias = np.zeros((rows, LANES), np.float32)
    for p in range(GROUP):
        bias[:, base + p] = np.where(pair == p, 0.0, -BIG)
    for s in range(HALF):
        bias[:, dead + s] = np.where(slot == s, -BIG, 0.0)
    one_hot = np.zeros((GROUP, LANES), np.float32)
    for p in range(GROUP):
        one_hot[p, base + p] = 1.0
    center = np.zeros((HALF, LANES), np.float32)
    for r in range(HALF):
        center[r, base + r // 2] = 1.0
        for s in range(HALF):
            center[r, dead + s] = float(s % 2 != r % 2)
    return (
        jnp.asarray(own, BF16),
        jnp.asarray(bias, BF16),
        jnp.asarray(one_hot, F32),
        jnp.asarray(center, BF16),
    )


def normalize(values):
    centred = values - jnp.mean(values, axis=-1, keepdims=True)
    inverse = lax.rsqrt(jnp.mean(centred * centred, axis=-1, keepdims=True) + EPS)
    return centred * inverse, inverse


def norm_back(grad, normed, inverse):
    return inverse * (
        grad
        - jnp.mean(grad, axis=-1, keepdims=True)
        - normed * jnp.mean(grad * normed, axis=-1, keepdims=True)
    )


GELU_C = math.sqrt(2.0 / math.pi)


def gelu_parts(x):
    square = x * x
    t = jnp.tanh(GELU_C * x * (1.0 + 0.044715 * square))
    return square, t


def expand(rows16, own):
    return jnp.concatenate([rows16] * HEADS, axis=0) * own


def fold_heads(values, own):
    masked = values * own.astype(F32)
    return jnp.sum(masked.reshape(HEADS, HALF, values.shape[-1]), axis=0)


def build_x(x_ref, slot, e_f32, dead_ref, one_hot_ref, featc_ref, c_rows, width):
    leaves = e_f32.shape[0]
    edge_rows = leaves * GROUP
    last = (tiles_of(width) - 1) * LANES
    place = dead_lane(width)
    rows = [jnp.zeros((place, LANES), F32)]
    rows.append(jnp.concatenate([dead_ref[slot], jnp.zeros((HALF, LANES - leaves), F32)], axis=1))
    rows.append(jnp.zeros((LANES - place - HALF, LANES), F32))
    dead = jnp.transpose(jnp.concatenate(rows, axis=0))[0:leaves]
    feature = dead[:, None, :] + one_hot_ref[...][None, :, :]
    x_ref[slot, 0:edge_rows, last : last + LANES] = feature.reshape(edge_rows, LANES).astype(BF16)
    part = e_f32[:, slot * GROUP : (slot + 1) * GROUP, :].reshape(edge_rows, width)
    x_ref[slot, 0:edge_rows, 0:width] = part.astype(BF16)
    x_ref[slot, edge_rows : edge_rows + HALF, last : last + LANES] = featc_ref[...]
    x_ref[slot, edge_rows : edge_rows + HALF, 0:width] = c_rows


def column_rows(columns):
    rows = columns[0].shape[0]
    lane = lax.broadcasted_iota(jnp.int32, (rows, LANES), 1)
    tile = jnp.zeros((rows, LANES), F32)
    for index, column in enumerate(columns):
        tile = jnp.where(lane == index, column, tile)
    return jnp.transpose(tile)[0 : len(columns)]


def forward_kernel(
    width,
    deps,
    e_ref,
    dead_ref,
    c_ref,
    wq_ref,
    wk_ref,
    wv_ref,
    wo_ref,
    gain1_ref,
    bias1_ref,
    wup_ref,
    wdt_ref,
    gain2_ref,
    bias2_ref,
    own_ref,
    qbias_ref,
    one_hot_ref,
    featc_ref,
    *rest,
):
    newc_ref, x_ref, p_ref, pe_ref, att_ref, q_ref, keys_ref, lse_ref, stat_ref, keys_s = rest[deps:]
    step = pl.program_id(0)
    scale = 1.0 / math.sqrt(width // HEADS)
    last = (tiles_of(width) - 1) * LANES
    slots = x_ref.shape[0]
    cols = HEADS * HALF

    @pl.when(step == 0)
    def _():
        q_ref[...] = mm(c_ref[...], wq_ref[...]).astype(BF16)
        for slot in range(slots):
            keys_s[slot, :, last : last + LANES] = qbias_ref[...]

    own = own_ref[...]
    base = pl.multiple_of(step * slots * HALF, slots * HALF)
    q_rows = q_ref[pl.ds(base, slots * HALF), :]
    q_all = jnp.concatenate(
        [expand(q_rows[s * HALF : (s + 1) * HALF], own) for s in range(slots)], axis=0
    )
    keys = (mm_nt(q_all, wk_ref[...]) * scale).astype(BF16)
    c_rows = c_ref[pl.ds(base, slots * HALF), :]
    e_f32 = e_ref[0].astype(F32)
    for slot in range(slots):
        keys_s[slot, :, 0:width] = keys[slot * cols : (slot + 1) * cols]
        keys_ref[slot] = keys[slot * cols : (slot + 1) * cols]
        build_x(
            x_ref, slot, e_f32, dead_ref, one_hot_ref, featc_ref,
            c_rows[slot * HALF : (slot + 1) * HALF], width,
        )
    scores = [mm_nt(keys_s[slot], x_ref[slot]) for slot in range(slots)]
    probs, logs = [], []
    for slot in range(slots):
        top = jnp.max(scores[slot], axis=1, keepdims=True)
        weights = jnp.exp(scores[slot] - top)
        total = jnp.sum(weights, axis=1, keepdims=True)
        probs.append((weights * (1.0 / total)).astype(BF16))
        logs.append(top + jnp.log(total))
    pes = []
    for slot in range(slots):
        p_ref[slot] = probs[slot]
        pe = mm(probs[slot], x_ref[slot])[:, 0:width].astype(BF16)
        pe_ref[slot] = pe
        pes.append(pe)
    lse_ref[0] = column_rows(logs)
    att = mm(jnp.concatenate(pes, axis=0), wv_ref[...])
    att = jnp.concatenate(
        [fold_heads(att[s * cols : (s + 1) * cols], own) for s in range(slots)], axis=0
    )
    att_ref[pl.ds(base, slots * HALF), :] = att.astype(BF16)

    @pl.when(step == pl.num_programs(0) - 1)
    def _():
        residual = c_ref[...].astype(F32) + mm(att_ref[...], wo_ref[...])
        z1, unused = normalize(residual)
        first = z1 * gain1_ref[...] + bias1_ref[...]
        hidden = mm(first.astype(BF16), wup_ref[...])
        unused, t = gelu_parts(hidden)
        gelu = (0.5 * hidden * (1.0 + t)).astype(BF16)
        z2, unused = normalize(first + mm_nt(gelu, wdt_ref[...]))
        new = (z2 * gain2_ref[...] + bias2_ref[...]).astype(BF16)
        newc_ref[...] = new
        new = new.astype(F32)
        stat_ref[0:1, :] = jnp.sum(new, axis=0, keepdims=True)
        stat_ref[1:2, :] = jnp.sum(new * new, axis=0, keepdims=True)


def whole(shape):
    zeros = (0,) * len(shape)
    return pl.BlockSpec(shape, lambda i, *unused: zeros)


def step_spec(shape, first=0):
    rest = (0,) * (len(shape) - 1)
    return pl.BlockSpec(shape, lambda i, *unused: (first + i,) + rest)


def part_spec(shape, part):
    return pl.BlockSpec(shape, lambda i, *unused: (part, 0))


ANY = pl.BlockSpec(memory_space=pl.ANY)


def run_forward(edges, dead, center, part, params, consts, first, micro, deps=()):
    unused, leaves, pairs, width = edges.shape
    slots = pairs // GROUP
    groups = micro * slots
    x_rows = leaves * GROUP + HALF
    pad = tiles_of(width) * LANES
    cols = HEADS * HALF
    count = groups * HALF
    operands = [
        params["query"], params["key"], params["value"], params["out"],
        params["gain1"], params["bias1"], params["up"], params["down_t"],
        params["gain2"], params["bias2"],
        *consts,
    ]
    return pl.pallas_call(
        functools.partial(forward_kernel, width, len(deps)),
        grid=(micro,),
        in_specs=[
            step_spec((1, leaves, pairs, width), first),
            step_spec((slots, HALF, leaves), first),
            part_spec((count, width), part),
        ]
        + [whole(o.shape) for o in operands]
        + [ANY] * len(deps),
        out_specs=[
            whole((count, width)),
            step_spec((slots, x_rows, pad)),
            step_spec((slots, cols, x_rows)),
            step_spec((slots, cols, width)),
            whole((count, width)),
            whole((count, width)),
            step_spec((slots, cols, width)),
            step_spec((1, slots, cols)),
            whole((2, width)),
        ],
        scratch_shapes=[pltpu.VMEM((slots, cols, pad), BF16)],
        out_shape=[
            jax.ShapeDtypeStruct((count, width), BF16),
            jax.ShapeDtypeStruct((groups, x_rows, pad), BF16),
            jax.ShapeDtypeStruct((groups, cols, x_rows), BF16),
            jax.ShapeDtypeStruct((groups, cols, width), BF16),
            jax.ShapeDtypeStruct((count, width), BF16),
            jax.ShapeDtypeStruct((count, width), BF16),
            jax.ShapeDtypeStruct((groups, cols, width), BF16),
            jax.ShapeDtypeStruct((micro, slots, cols), F32),
            jax.ShapeDtypeStruct((2, width), F32),
        ],
        compiler_params=pltpu.CompilerParams(vmem_limit_bytes=VMEM),
        cost_estimate=cost(10e-6),
        name="layer_forward",
    )(edges, dead, center, *operands, *deps)


def blocks_for(devices, width, ff):
    count = (packed_tiles(width, ff) + tiles_of(width)) * (ROWS // 16)
    return -(-count // devices) * devices


def packed_tiles(width, ff):
    return 4 * (width // LANES) + 2 * (ff // LANES) + 3


def placement(width, ff):
    full, wide = width // LANES, ff // LANES
    rest = 4 * full + 2 * wide
    narrow, broad = width - full * LANES, ff - wide * LANES
    return (
        (0, width, (rest, 0)),
        (full, width, (rest, narrow)),
        (2 * full, width, (rest + 1, 0)),
        (3 * full, width, (rest + 1, narrow)),
        (4 * full, ff, (rest + 2, 0)),
        (4 * full + wide, ff, (rest + 2, broad)),
        (rest + 3, width, (rest + 3 + full, 0)),
    )


SPOT = 64


def sums_fit(devices, width):
    return width % LANES <= SPOT and 4 * devices <= LANES - SPOT


def put_tile(packed_ref, tile, matrix):
    rows, lanes = matrix.shape
    full = matrix
    if rows < ROWS:
        full = jnp.concatenate([matrix, jnp.zeros((ROWS - rows, lanes), F32)], axis=0)
    if lanes < LANES:
        full = jnp.concatenate([full, jnp.zeros((ROWS, LANES - lanes), F32)], axis=1)
    per = ROWS // 16
    packed_ref[tile * per : (tile + 1) * per] = full.astype(BF16).reshape(per, 16, LANES)


def put_matrix(packed_ref, first_tile, matrix):
    full = matrix.shape[1] // LANES
    for tile in range(full):
        put_tile(packed_ref, first_tile + tile, matrix[:, tile * LANES : (tile + 1) * LANES])
    return matrix[:, full * LANES :]


def backward_kernel(
    width,
    deps,
    begin,
    end,
    first,
    core_ref,
    x_ref,
    p_ref,
    pe_ref,
    keys_ref,
    lse_ref,
    c_ref,
    q_ref,
    att_ref,
    dc_ref,
    wq_ref,
    wk_ref,
    wv_ref,
    wo_ref,
    gain1_ref,
    bias1_ref,
    wup_ref,
    wdt_ref,
    gain2_ref,
    bias2_ref,
    own_ref,
    *rest,
):
    rest = rest[deps:]
    if not begin:
        sums_in, vec_in, dq_in, dr_in, da_in, packed_in, *rest = rest
    if end:
        cback_ref, inner_ref, dvals_ref, packed_out_ref, sent_ref, *rest = rest
    else:
        sums_out, vec_out, dq_out, dr_out, inner_ref, dvals_ref, packed_out_ref, *rest = rest
    if begin:
        da_out, *rest = rest
    if begin and end:
        ds_ref, *rest = rest
    packed_ref, packed_sem, dvals_s, dwk_s, dwv_s, dwo_s, vec_s, dq_s, dr_s, da_s = rest
    count = c_ref.shape[0]
    step = pl.program_id(0)
    scale = 1.0 / math.sqrt(width // HEADS)
    last = (tiles_of(width) - 1) * LANES
    places = placement(width, wup_ref.shape[1])
    slots, x_rows, pad = x_ref.shape
    edge_rows = x_rows - HALF
    cols = HEADS * HALF

    @pl.when(step == 0)
    def _():
        for slot in range(slots):
            dvals_s[slot, :, last : last + LANES] = jnp.zeros((cols, LANES), BF16)
        if not begin:
            pltpu.make_async_copy(packed_in, packed_ref, packed_sem.at[0]).start()
            for total_ref, total in zip((dwk_s, dwv_s, dwo_s), (0, 1, 2)):
                total_ref[...] = sums_in[total]
            vec_s[...] = vec_in[...]
            dq_s[...] = dq_in[...]
            dr_s[...] = dr_in[...]
            da_s[...] = da_in[...]
            return
        dwk_s[...] = jnp.zeros_like(dwk_s)
        dwv_s[...] = jnp.zeros_like(dwv_s)
        att = att_ref[...]
        z1, inverse1 = normalize(c_ref[...].astype(F32) + mm(att, wo_ref[...]))
        first = z1 * gain1_ref[...] + bias1_ref[...]
        first_low = first.astype(BF16)
        hidden = mm(first_low, wup_ref[...])
        square, t = gelu_parts(hidden)
        gelu = (0.5 * hidden * (1.0 + t)).astype(BF16)
        z2, inverse2 = normalize(first + mm_nt(gelu, wdt_ref[...]))
        dc = dc_ref[0:count, :].astype(F32)
        dgain2 = jnp.sum(dc * z2, axis=0, keepdims=True)
        dbias2 = jnp.sum(dc, axis=0, keepdims=True)
        dr2 = norm_back(dc * gain2_ref[...], z2, inverse2)
        df = dr2.astype(BF16)
        down_rest = put_matrix(packed_ref, places[5][0], mm_tn(df, gelu))
        slope = 0.5 * (1.0 + t) + 0.5 * hidden * (1.0 - t * t) * GELU_C * (
            1.0 + 3.0 * 0.044715 * square
        )
        dh = (mm(df, wdt_ref[...]) * slope).astype(BF16)
        up_rest = put_matrix(packed_ref, places[4][0], mm_tn(first_low, dh))
        put_tile(packed_ref, places[4][2][0], jnp.concatenate([up_rest, down_rest], axis=1))
        dfirst = dr2 + mm_nt(dh, wup_ref[...])
        dgain1 = jnp.sum(dfirst * z1, axis=0, keepdims=True)
        dbias1 = jnp.sum(dfirst, axis=0, keepdims=True)
        dr1 = norm_back(dfirst * gain1_ref[...], z1, inverse1)
        dr_s[...] = dr1
        do = dr1.astype(BF16)
        dwo_s[...] = mm_tn(att, do)
        da_s[...] = mm_nt(do, wo_ref[...]).astype(BF16)
        da_out[...] = da_s[...]
        for index, vector in enumerate((dgain1, dbias1, dgain2, dbias2)):
            vec_s[index : index + 1, :] = vector
        if not end:
            pltpu.make_async_copy(packed_ref, packed_out_ref, packed_sem.at[0]).start()

    own = own_ref[...]
    base = pl.multiple_of((first + step) * slots * HALF, slots * HALF)

    def all_heads(ref):
        rows = ref[pl.ds(base, slots * HALF), :]
        return jnp.concatenate(
            [expand(rows[s * HALF : (s + 1) * HALF], own) for s in range(slots)], axis=0
        )

    q_all, da_all = all_heads(q_ref), all_heads(da_s)
    dvals = mm_nt(da_all, wv_ref[...]).astype(BF16)
    for slot in range(slots):
        dvals_s[slot, :, 0:width] = dvals[slot * cols : (slot + 1) * cols]
        dvals_ref[slot] = dvals[slot * cols : (slot + 1) * cols]
    dprobs = [mm_nt(dvals_s[slot], x_ref[slot]) for slot in range(slots)]
    dscores, inners = [], []
    for slot in range(slots):
        probs = p_ref[slot].astype(F32)
        inner = jnp.sum(probs * dprobs[slot], axis=1, keepdims=True)
        dscores.append((probs * (dprobs[slot] - inner)).astype(BF16))
        if begin and end:
            ds_ref[slot] = dscores[slot]
        inners.append(inner)
    inner_ref[0, 0] = lse_ref[0]
    inner_ref[1, 0] = column_rows(inners)
    dses, parts = [], []
    for slot in range(slots):
        dses.append(mm(dscores[slot], x_ref[slot])[:, 0:width].astype(BF16))
        span = slice(slot * cols, (slot + 1) * cols)
        parts.append(
            mm_tn(dscores[slot][:, edge_rows:], keys_ref[slot])
            + mm_tn(p_ref[slot, :, edge_rows:], dvals[span])
        )
    dse = jnp.concatenate(dses, axis=0)
    pe = pe_ref[...].reshape(slots * cols, width)
    dwk_s[...] += mm_tn(dse, q_all)
    dwv_s[...] += mm_tn(pe, da_all)
    dq = mm(dse, wk_ref[...])
    dq = jnp.concatenate(
        [fold_heads(dq[s * cols : (s + 1) * cols], own) for s in range(slots)], axis=0
    )
    dq_s[pl.ds(base, slots * HALF), :] = (dq * scale).astype(BF16)
    dr_s[pl.ds(base, slots * HALF), :] += jnp.concatenate(parts, axis=0)

    @pl.when(step == pl.num_programs(0) - 1)
    def _():
        if not end:
            for total, total_ref in enumerate((dwk_s, dwv_s, dwo_s)):
                sums_out[total] = total_ref[...]
            vec_out[...] = vec_s[...]
            dq_out[...] = dq_s[...]
            dr_out[...] = dr_s[...]
            pltpu.make_async_copy(packed_ref, packed_out_ref, packed_sem.at[0]).wait()
            return
        if not begin:
            pltpu.make_async_copy(packed_in, packed_ref, packed_sem.at[0]).wait()
        dq_all = dq_s[...]
        dwq = jnp.concatenate([mm_tn(c_ref[...], dq_all), vec_s[...]], axis=0)
        query_rest = put_matrix(packed_ref, places[0][0], dwq)
        key_rest = put_matrix(packed_ref, places[1][0], dwk_s[...] * scale)
        key_rest = jnp.concatenate([key_rest, jnp.zeros((4, key_rest.shape[1]), F32)], axis=0)
        put_tile(
            packed_ref, places[0][2][0], jnp.concatenate([query_rest, key_rest], axis=1)
        )
        value_rest = put_matrix(packed_ref, places[2][0], dwv_s[...])
        out_rest = put_matrix(packed_ref, places[3][0], dwo_s[...])
        put_tile(
            packed_ref, places[2][2][0], jnp.concatenate([value_rest, out_rest], axis=1)
        )
        copy = pltpu.make_async_copy(packed_ref, packed_out_ref, packed_sem.at[0])
        copy.start()
        size = sent_ref.shape[0]
        start = pl.multiple_of((1 - core_ref[0]) * size, size)
        copy_half = pltpu.make_async_copy(
            packed_ref.at[pl.ds(start, size)], sent_ref, packed_sem.at[1]
        )
        copy_half.start()
        cback_ref[...] = (dr_s[...] + mm_nt(dq_all, wq_ref[...])).astype(BF16)
        copy.wait()
        copy_half.wait()


def run_backward(
    core, x, p, pe, keys, lse, center, q, att, dc, params, consts, first, steps, micro, blocks, state,
    end, deps=(),
):
    groups, x_rows, pad = x.shape
    slots = groups // micro
    cols = p.shape[1]
    count, width = q.shape
    begin = state is None
    operands = [
        center, q, att, dc,
        params["query"], params["key"], params["value"], params["out"],
        params["gain1"], params["bias1"], params["up"], params["down_t"],
        params["gain2"], params["bias2"],
        consts[0],
    ]
    specs = [whole(o.shape) for o in operands]
    if not begin:
        for index in (2, 3, 7, 8, 9, 10, 11, 12, 13):
            specs[index] = ANY
    state = [] if begin else list(state)
    state_specs = [] if begin else [whole(o.shape) for o in state[:5]] + [ANY]
    packed = jax.ShapeDtypeStruct((blocks, 16, LANES), BF16)
    rows = jax.ShapeDtypeStruct((count, width), BF16)
    sums = jax.ShapeDtypeStruct((2, micro, slots, cols), F32)
    dvals = jax.ShapeDtypeStruct((groups, cols, width), BF16)
    kept = [
        (sums, pl.BlockSpec((2, 1, slots, cols), lambda i, core: (0, first + i, 0, 0))),
        (dvals, step_spec((slots, cols, width), first)),
        (packed, ANY),
    ]
    if end:
        half = jax.ShapeDtypeStruct((blocks // 2, 16, LANES), BF16)
        outs = [(rows, whole(rows.shape)), *kept, (half, ANY)]
    else:
        totals = [((3, width, width), F32), ((4, width), F32), ((count, width), BF16)]
        totals.append(((count, width), F32))
        outs = [(jax.ShapeDtypeStruct(shape, kind), whole(shape)) for shape, kind in totals] + kept
    if begin:
        outs.append((rows, whole(rows.shape)))
    if begin and end:
        dscores = jax.ShapeDtypeStruct((groups, cols, x_rows), BF16)
        outs.append((dscores, step_spec((slots, cols, x_rows))))
    inputs = [core, x, p, pe, keys, lse, *operands, *deps, *state]
    return pl.pallas_call(
        functools.partial(backward_kernel, width, len(deps), begin, end, first),
        grid_spec=pltpu.PrefetchScalarGridSpec(
            num_scalar_prefetch=1,
            grid=(steps,),
            in_specs=[
                step_spec((slots, x_rows, pad), first),
                step_spec((slots, cols, x_rows), first),
                step_spec((slots, cols, width), first),
                step_spec((slots, cols, width), first),
                step_spec((1, slots, cols), first),
            ]
            + specs
            + [ANY] * len(deps)
            + state_specs,
            out_specs=[spec for unused, spec in outs],
            scratch_shapes=[
                pltpu.VMEM((blocks, 16, LANES), BF16),
                pltpu.SemaphoreType.DMA((2,)),
                pltpu.VMEM((slots, cols, pad), BF16),
                pltpu.VMEM((width, width), F32),
                pltpu.VMEM((width, width), F32),
                pltpu.VMEM((width, width), F32),
                pltpu.VMEM((4, width), F32),
                pltpu.VMEM((count, width), BF16),
                pltpu.VMEM((count, width), F32),
                pltpu.VMEM((count, width), BF16),
            ],
        ),
        out_shape=[shape for shape, unused in outs],
        compiler_params=pltpu.CompilerParams(vmem_limit_bytes=VMEM),
        cost_estimate=cost(0.2e-6),
        name="layer_backward",
    )(*inputs)


def nothing(like):
    return tuple(
        pl.pallas_call(
            lambda *refs: None, out_specs=[ANY] * len(like), out_shape=list(like), name="nothing"
        )()
    )


def edge_forward_kernel(e_ref, w_ref, dep_ref, out_ref):
    unused, leaves, pairs, width = e_ref.shape
    rows = e_ref[0].reshape(leaves * pairs, width)
    out_ref[0] = mm(rows, w_ref[...]).astype(BF16).reshape(leaves, pairs, width)


def run_edge_forward(edges, weight, dep):
    micro, leaves, pairs, width = edges.shape
    cut = 2 if leaves % 2 == 0 else 1
    block = pl.BlockSpec((1, leaves // cut, pairs, width), lambda i: (i // cut, i % cut, 0, 0))
    return pl.pallas_call(
        edge_forward_kernel,
        grid=(micro * cut,),
        in_specs=[block, whole(weight.shape), pl.BlockSpec(memory_space=pl.ANY)],
        out_specs=block,
        out_shape=jax.ShapeDtypeStruct(edges.shape, BF16),
        compiler_params=pltpu.CompilerParams(vmem_limit_bytes=VMEM),
        cost_estimate=cost(13e-6),
        name="edge_forward",
    )(edges, weight, dep)


def edge_act_kernel(e_ref, w_ref, out_ref):
    unused, leaves, pairs, width = e_ref.shape
    act = mm(e_ref[0].reshape(leaves * pairs, width), w_ref[...])
    out_ref[0] = act.astype(BF16).reshape(leaves, pairs, width)


def run_edge_act(edges, weight, first, steps):
    micro, leaves, pairs, width = edges.shape
    per = pairs // HALF
    block = pl.BlockSpec(
        (1, leaves, HALF, width), lambda i: ((first + i) // per, 0, (first + i) % per, 0)
    )
    return pl.pallas_call(
        edge_act_kernel,
        grid=(steps,),
        in_specs=[block, whole(weight.shape)],
        out_specs=block,
        out_shape=jax.ShapeDtypeStruct(edges.shape, BF16),
        input_output_aliases={0: 0},
        compiler_params=pltpu.CompilerParams(vmem_limit_bytes=VMEM),
        cost_estimate=cost(2e-6 * steps),
        name="edge_act",
    )(edges, weight)


def edge_weight_kernel(
    width, e_ref, p_ref, ds_ref, keys_ref, dvals_ref, cross_ref, w0_ref, w1_ref, *rest
):
    early_ref, late_ref, out_ref = rest[-3:]
    slots, cols, unused = p_ref.shape
    leaves = e_ref.shape[1]
    edge_rows = leaves * GROUP

    @pl.when(pl.program_id(0) == 0)
    def _():
        out_ref[...] = jnp.zeros_like(out_ref)

    e_f32 = e_ref[0].astype(F32)
    dses, pes = [], []
    for slot in range(slots):
        part = e_f32[:, slot * GROUP : (slot + 1) * GROUP, :].reshape(edge_rows, width)
        part = part.astype(BF16)
        dses.append(mm(ds_ref[slot, :, 0:edge_rows], part).astype(BF16))
        pes.append(mm(p_ref[slot, :, 0:edge_rows], part).astype(BF16))
    flat = (slots * cols, width)
    out_ref[...] += mm_tn(jnp.concatenate(dses, axis=0), keys_ref[...].reshape(flat)) + mm_tn(
        jnp.concatenate(pes, axis=0), dvals_ref[...].reshape(flat)
    )

    @pl.when(pl.program_id(0) == pl.num_programs(0) - 1)
    def _():
        cross = cross_ref[...]
        early_ref[...] = (out_ref[...] + mm_nt(cross, w1_ref[...])).astype(BF16)
        late_ref[...] = mm_tn(w0_ref[...], cross).astype(BF16)


def run_edge_weight(edges, p, ds, keys, dvals, cross, w0, w1, *deps):
    micro, leaves, pairs, width = edges.shape
    groups, cols, x_rows = p.shape
    slots = groups // micro
    return pl.pallas_call(
        functools.partial(edge_weight_kernel, width),
        grid=(micro,),
        in_specs=[
            step_spec((1, leaves, pairs, width)),
            step_spec((slots, cols, x_rows)),
            step_spec((slots, cols, x_rows)),
            step_spec((slots, cols, width)),
            step_spec((slots, cols, width)),
        ]
        + [whole((width, width))] * 3
        + [ANY] * len(deps),
        out_specs=[whole((width, width))] * 2,
        out_shape=[jax.ShapeDtypeStruct((width, width), BF16)] * 2,
        scratch_shapes=[pltpu.VMEM((width, width), F32)],
        compiler_params=pltpu.CompilerParams(vmem_limit_bytes=VMEM),
        cost_estimate=cost(8e-6),
        name="edge_weight",
    )(edges, p, ds, keys, dvals, cross, w0, w1, *deps)


def edge_cross_kernel(e_ref, cot_ref, dep_ref, out_ref, total_ref):
    step = pl.program_id(0)
    unused, leaves, pairs, width = e_ref.shape
    flat = (leaves * pairs, width)

    @pl.when(step == 0)
    def _():
        total_ref[...] = jnp.zeros_like(total_ref)

    total_ref[...] += mm_tn(e_ref[0].reshape(flat), cot_ref[0].reshape(flat))

    @pl.when(step == pl.num_programs(0) - 1)
    def _():
        out_ref[...] = total_ref[...].astype(BF16)


def run_edge_cross(edges, cot, dep):
    micro, leaves, pairs, width = edges.shape
    cut = 2 if leaves % 2 == 0 else 1
    block = pl.BlockSpec((1, leaves // cut, pairs, width), lambda i: (i // cut, i % cut, 0, 0))
    return pl.pallas_call(
        edge_cross_kernel,
        grid=(micro * cut,),
        in_specs=[block, block, ANY],
        out_specs=whole((width, width)),
        out_shape=jax.ShapeDtypeStruct((width, width), BF16),
        scratch_shapes=[pltpu.VMEM((width, width), F32)],
        compiler_params=pltpu.CompilerParams(vmem_limit_bytes=VMEM),
        cost_estimate=cost(8e-6),
        name="edge_cross",
    )(edges, cot, dep)


def edge_backward_kernel(width, first, early, deps, *refs):
    if early:
        through_ref, x_ref, keys_ref, dvals_ref, own_sums_ref, *refs = refs
        c1_ref, rows1_ref, weights1_ref, sums_ref, w0_ref, own_ref, qbias_ref, *refs = refs
        out_ref, both_s, joint_s = refs[deps:]
    else:
        cot_ref, x_ref, keys_ref, dvals_ref, own_sums_ref, wc_ref, qbias_ref, *refs = refs
        out_ref, both_s = refs[deps:]
    step = pl.program_id(0)
    scale = 1.0 / math.sqrt(width // HEADS)
    last = (tiles_of(width) - 1) * LANES
    leaves = out_ref.shape[1]
    edge_rows = leaves * GROUP
    cols = HEADS * HALF

    @pl.when(step == 0)
    def _():
        for slot in range(2):
            for layer in range(2):
                both_s[slot, layer, :, last : last + LANES] = qbias_ref[...]
                both_s[slot, 2 + layer, :, last : last + LANES] = jnp.zeros((cols, LANES), BF16)

    base = pl.multiple_of((first + step) * HALF * 2, HALF * 2)
    half = ((first + step) % (own_sums_ref.shape[2] // 2)) * 2

    def attention_part(layers):
        parts = []
        count = layers * cols
        pad = both_s.shape[-1]
        for slot in range(2):
            x = x_ref[slot, 0:edge_rows, :]
            lse = own_sums_ref[0, 0, pl.ds(half + slot, 1), :]
            inner = own_sums_ref[1, 0, pl.ds(half + slot, 1), :]
            if layers == 2:
                lse = jnp.concatenate([lse, sums_ref[0, 0, pl.ds(half + slot, 1), :]], axis=1)
                inner = jnp.concatenate([inner, sums_ref[1, 0, pl.ds(half + slot, 1), :]], axis=1)
            if layers == 2:
                both = both_s[slot].reshape(2 * count, pad)
                product = mm_nt(x, both)
                probs = jnp.exp(jnp.minimum(product[:, 0:count] - lse, 0.0))
                dscores = probs * (product[:, count:] - inner)
                part = mm(
                    jnp.concatenate([dscores.astype(BF16), probs.astype(BF16)], axis=1), both
                )
            else:
                keys, dvals = both_s[slot, 0], both_s[slot, 2]
                probs = jnp.exp(jnp.minimum(mm_nt(x, keys) - lse, 0.0))
                dscores = probs * (mm_nt(x, dvals) - inner)
                part = mm(dscores.astype(BF16), keys) + mm(probs.astype(BF16), dvals)
            parts.append(part[:, 0:width])
        return parts

    def joined(parts):
        shaped = [part.reshape(leaves, GROUP, width) for part in parts]
        return jnp.concatenate(shaped, axis=1).reshape(leaves * HALF, width)

    for slot in range(2):
        both_s[slot, 0, :, 0:width] = keys_ref[slot]
        both_s[slot, 2, :, 0:width] = dvals_ref[slot]

    if not early:
        cot = cot_ref[0].reshape(leaves * HALF, width)
        grad = mm_nt(cot, wc_ref[...]) + joined(attention_part(1))
        out_ref[0] = grad.astype(BF16).reshape(leaves, HALF, width)
        return

    own = own_ref[...]
    stacked = weights1_ref.shape[0] // 4

    @pl.when(step == 0)
    def _():
        for index in range(2):
            at = (2 + index) * stacked
            other = weights1_ref[at : at + width, 0:width]
            joint_s[index] = mm(w0_ref[...], other).astype(BF16)

    def all_heads(rows):
        return jnp.concatenate([expand(rows[0:HALF], own), expand(rows[HALF:], own)], axis=0)

    w_query = weights1_ref[stacked : stacked + width, 0:width]
    q1 = mm(c1_ref[pl.ds(base, 2 * HALF), :], w_query).astype(BF16)
    da1 = rows1_ref[pl.ds(base, 2 * HALF), :]
    keys = (mm_nt(all_heads(q1), joint_s[0]) * scale).astype(BF16)
    dvals = mm_nt(all_heads(da1), joint_s[1]).astype(BF16)
    for slot in range(2):
        span = slice(slot * cols, (slot + 1) * cols)
        both_s[slot, 1, :, 0:width] = keys[span]
        both_s[slot, 3, :, 0:width] = dvals[span]
    through = through_ref[0].reshape(leaves * HALF, width)
    grad = through.astype(F32) + joined(attention_part(2))
    out_ref[0] = grad.astype(BF16).reshape(leaves, HALF, width)


def run_edge_backward(first, steps, so_far, early, grad, own, other, weights, consts, deps):
    micro, leaves, pairs, width = grad.shape
    per = pairs // HALF
    x, keys, dvals, sums = own
    groups, x_rows, pad = x.shape
    cols = HEADS * HALF
    slots = pairs // GROUP
    block = pl.BlockSpec(
        (1, leaves, HALF, width), lambda i: ((first + i) // per, 0, (first + i) % per, 0)
    )
    sums_spec = pl.BlockSpec((2, 1, slots, cols), lambda i: (0, (first + i) // per, 0, 0))
    operands = [*other[:3], *weights, consts[0], consts[1]] if early else [weights[0], consts[1]]
    specs = [whole(o.shape) for o in operands]
    scratch = [pltpu.VMEM((2, 4, cols, pad), BF16)]
    if early:
        operands.insert(3, other[3])
        specs.insert(3, sums_spec)
        scratch.append(pltpu.VMEM((2, width, width), BF16))
    extra = list(deps) + ([] if so_far is None else [so_far])
    inputs = [grad, x, keys, dvals, sums, *operands, *extra]
    return pl.pallas_call(
        functools.partial(edge_backward_kernel, width, first, early, len(extra)),
        grid=(steps,),
        in_specs=[
            block,
            step_spec((2, x_rows, pad), first),
            step_spec((2, cols, width), first),
            step_spec((2, cols, width), first),
            sums_spec,
        ]
        + specs
        + [ANY] * len(extra),
        out_specs=block,
        scratch_shapes=scratch,
        out_shape=jax.ShapeDtypeStruct(grad.shape, BF16),
        input_output_aliases={} if so_far is None else {len(inputs) - 1: 0},
        compiler_params=pltpu.CompilerParams(vmem_limit_bytes=VMEM),
        cost_estimate=cost(7e-6 * steps),
        name="edge_backward",
    )(*inputs)


def cost(seconds):
    return pl.CostEstimate(flops=int(seconds * 1e9), bytes_accessed=0, transcendentals=0)


def split_kernel(parts, recv_count, deps, edge_at, digit_ref, *refs):
    held_ref, *refs = refs
    recv_refs, refs = refs[:recv_count], refs[recv_count:]
    if edge_at is not None:
        edge_ref, edge_recv_ref, *refs = refs
    refs = refs[deps:]
    out_refs = refs
    size = held_ref.shape[0] // parts
    digit = digit_ref[0]
    for other, out_ref in enumerate(out_refs):
        span = pl.ds(pl.multiple_of((digit ^ other) * size, size), size)
        total = held_ref[span].astype(F32)
        for recv_ref in recv_refs:
            total = total + recv_ref[span].astype(F32)
        out_ref[...] = total.astype(BF16)
    if edge_at is not None:
        tiles = edge_ref.shape[0]
        for part in range(parts):
            low = max(edge_at, part * size)
            high = min(edge_at + tiles, (part + 1) * size)
            for other, out_ref in enumerate(out_refs):
                if low < high:

                    @pl.when((digit_ref[1] == 1) & ((digit ^ other) == part))
                    def _(low=low, high=high, part=part, out_ref=out_ref):
                        place = slice(low - part * size, high - part * size)
                        source = slice(low - edge_at, high - edge_at)
                        out_ref[place] = (
                            edge_ref[source].astype(F32) + edge_recv_ref[source].astype(F32)
                        ).astype(BF16)


def run_split(held, received, parts, digits, edges=(), edge_at=None, deps=()):
    count = held.shape[0] // 2 if edges else held.shape[0]
    size = count // parts
    inputs = [held, *received, *edges]

    def spec(array):
        return whole(array.shape)

    held_spec = pl.BlockSpec((count, 16, LANES), lambda i, digits: (digits[1], 0, 0))
    out_shape = [jax.ShapeDtypeStruct((size, 16, LANES), BF16)] * parts
    return pl.pallas_call(
        functools.partial(split_kernel, parts, len(received), len(deps), edge_at),
        grid_spec=pltpu.PrefetchScalarGridSpec(
            num_scalar_prefetch=1,
            grid=(1,),
            in_specs=[held_spec if edges else spec(held)]
            + [spec(array) for array in inputs[1:]]
            + [pl.BlockSpec(memory_space=pl.ANY)] * len(deps),
            out_specs=[spec(array) for array in out_shape],
        ),
        out_shape=out_shape,
        compiler_params=pltpu.CompilerParams(vmem_limit_bytes=VMEM),
        cost_estimate=cost(2e-6),
        name="split_gradients",
    )(digits, *inputs, *deps)


def join_kernel(count, deps, *refs):
    out_ref = refs[count + deps]
    size = refs[0].shape[0]
    for index in range(count):
        out_ref[index * size : (index + 1) * size] = refs[index][...]


def run_join(pieces, deps=()):
    size = pieces[0].shape[0]
    spec = pl.BlockSpec(memory_space=pltpu.VMEM)
    return pl.pallas_call(
        functools.partial(join_kernel, len(pieces), len(deps)),
        in_specs=[spec] * len(pieces) + [pl.BlockSpec(memory_space=pl.ANY)] * len(deps),
        out_specs=spec,
        out_shape=jax.ShapeDtypeStruct((size * len(pieces), 16, LANES), BF16),
        compiler_params=pltpu.CompilerParams(vmem_limit_bytes=VMEM),
        cost_estimate=cost(1e-6),
        name="join_gradients",
    )(*pieces, *deps)


def edge_tiles_kernel(late_ref, early_ref, late_edge_ref, sums_ref, dep_ref, out_ref):
    width = early_ref.shape[0]
    full = width // LANES
    edge = jnp.where(late_ref[0] == 1, late_edge_ref[...], early_ref[...]).astype(F32)
    over = put_matrix(out_ref, 0, edge)
    lane = lax.broadcasted_iota(jnp.int32, (LANES, width), 0) - SPOT - 4 * late_ref[1]
    table = jnp.zeros((LANES, width), F32)
    for index in range(2):
        row = sums_ref[index : index + 1, :]
        high = row.astype(BF16).astype(F32)
        table = jnp.where(lane == index, high, table)
        table = jnp.where(lane == 2 + index, row - high, table)
    columns = jnp.transpose(table)
    gap = jnp.zeros((width, LANES - over.shape[1]), F32)
    put_tile(out_ref, full, jnp.concatenate([over, gap], axis=1) + columns)


def run_edge_tiles(late_me, early_edge, late_edge, sums, dep):
    width = early_edge.shape[0]
    per = ROWS // 16
    vmem = pl.BlockSpec(memory_space=pltpu.VMEM)
    return pl.pallas_call(
        edge_tiles_kernel,
        in_specs=[pl.BlockSpec(memory_space=pltpu.SMEM), vmem, vmem, vmem, ANY],
        out_shape=jax.ShapeDtypeStruct((tiles_of(width) * per, 16, LANES), BF16),
        compiler_params=pltpu.CompilerParams(vmem_limit_bytes=VMEM),
        cost_estimate=cost(2e-6),
        name="edge_tiles",
    )(late_me, early_edge, late_edge, sums, dep)


def stack_kernel(*refs):
    *parts, dep_ref, out_ref = refs
    rows = out_ref.shape[0] // len(parts)
    for index, part in enumerate(parts):
        out_ref[index * rows : index * rows + part.shape[0], 0 : part.shape[1]] = part[...]


def run_stack(arrays, dep):
    rows, width = arrays[0].shape
    vmem = pl.BlockSpec(memory_space=pltpu.VMEM)
    shape = (len(arrays) * -(-rows // 16) * 16, tiles_of(width) * LANES)
    return pl.pallas_call(
        stack_kernel,
        in_specs=[vmem] * len(arrays) + [ANY],
        out_shape=jax.ShapeDtypeStruct(shape, BF16),
        compiler_params=pltpu.CompilerParams(vmem_limit_bytes=VMEM),
        cost_estimate=cost(1e-6),
        name="stack_weights",
    )(*arrays, dep)


def stages_of(devices):
    bits = devices.bit_length() - 1
    stages = [(0, 1)]
    if (bits - 1) % 2:
        stages.append((1, 1))
    at = sum(width for unused, width in stages)
    while at < bits:
        stages.append((at, 2))
        at += 2
    return stages


def unpack_kernel(width, ff, count, rows_summed, me_ref, *refs):
    sources, refs = refs[:count], refs[count:]
    total_ref = refs[-1]
    outs, vector_refs, stats_ref = refs[:7], refs[7:11], refs[11]
    me, at = me_ref[0], 0
    for source in sources:
        many, per = source.shape[0], source.shape[1]
        for index in range(many):
            start = pl.multiple_of((me ^ (at + index)) * per, per)
            total_ref[pl.ds(start, per)] = source[index]
        at += many
    rows = ROWS // 16

    def tile_at(tile):
        return total_ref[tile * rows : (tile + 1) * rows].reshape(ROWS, LANES).astype(F32)

    for (first, columns, (spot, lane)), ref in zip(placement(width, ff), outs):
        full = columns // LANES
        for tile in range(full):
            values = tile_at(first + tile)
            ref[:, 0, tile * LANES : (tile + 1) * LANES] = values[0:width]
            if first == 0:
                for row, vector_ref in enumerate(vector_refs):
                    vector_ref[:, tile * LANES : (tile + 1) * LANES] = values[
                        width + row : width + row + 1
                    ]
        values = tile_at(spot)[:, lane : lane + columns - full * LANES]
        ref[:, 0, full * LANES : columns] = values[0:width]
        if first == 0:
            for row, vector_ref in enumerate(vector_refs):
                vector_ref[:, full * LANES : columns] = values[width + row : width + row + 1]
    last = tile_at(placement(width, ff)[6][2][0])[0:width].astype(BF16)
    kind = lax.broadcasted_iota(jnp.int32, (16, LANES), 0)
    lane = lax.broadcasted_iota(jnp.int32, (16, LANES), 1)
    chosen = (lane >= SPOT) & (lane % 2 == kind)
    sums = mm_nt(chosen.astype(F32).astype(BF16), last) * (1.0 / rows_summed)
    stats_ref[0, 0:1, :] = sums[0:1]
    stats_ref[0, 1:2, :] = sums[1:2] - sums[0:1] * sums[0:1]


def run_unpack(me, pieces, width, ff, rows_summed):
    square = jax.ShapeDtypeStruct((width, 1, width), F32)
    wide = jax.ShapeDtypeStruct((width, 1, ff), F32)
    count = sum(piece.shape[0] * piece.shape[1] for piece in pieces)
    spec = pl.BlockSpec(memory_space=pltpu.VMEM)
    return pl.pallas_call(
        functools.partial(unpack_kernel, width, ff, len(pieces), rows_summed),
        in_specs=[pl.BlockSpec(memory_space=pltpu.SMEM)] + [spec] * len(pieces),
        out_shape=[square] * 4 + [wide] * 2 + [square]
        + [jax.ShapeDtypeStruct((1, width), F32)] * 4
        + [jax.ShapeDtypeStruct((1, 2, width), F32)],
        scratch_shapes=[pltpu.VMEM((count, 16, LANES), BF16)],
        compiler_params=pltpu.CompilerParams(vmem_limit_bytes=VMEM),
        name="unpack_gradients",
    )(me, *pieces)


def swapped(array, axis, bit):
    devices = lax.axis_size(axis)
    return lax.ppermute(array, axis, [(i, i ^ bit) for i in range(devices)])


def sum_small(array, axis):
    devices = lax.axis_size(axis)
    for k in range(devices.bit_length() - 1):
        array = array + swapped(array, axis, 1 << k)
    return array


def shards(
    center_input,
    edge_input,
    leaf_count,
    leaf_mask,
    w_query,
    w_key,
    w_value,
    w_out,
    gain_attn,
    bias_attn,
    w_up,
    w_down,
    gain_ffn,
    bias_ffn,
    w_edge,
    center_cot,
    edge_cot,
):
    micro, pairs, leaves, width = edge_input.shape
    ff = w_up.shape[-1]
    section = lax.axis_index("section")
    at_first = section == 0
    late = jnp.where(at_first, 0, 1).astype(jnp.int32).reshape(1)
    early = 1 - late
    consts = constants(width)
    params = {
        "query": w_query[0], "key": w_key[0], "value": w_value[0], "out": w_out[0],
        "gain1": gain_attn, "bias1": bias_attn,
        "up": w_up[0], "down_t": jnp.transpose(w_down[0]),
        "gain2": gain_ffn, "bias2": bias_ffn,
    }
    edges0 = jnp.transpose(edge_input, (0, 2, 1, 3))
    cot = jnp.transpose(edge_cot, (0, 2, 1, 3))
    center0 = center_input.reshape(micro * pairs * 2, width)

    slots = jnp.arange(leaves, dtype=jnp.int32)
    dead = jnp.where((slots < leaf_count[..., None]) & (leaf_mask == 1), 0.0, 1.0)
    dead = dead.reshape(micro * pairs // GROUP, HALF, leaves)

    def pick(at_first_section, at_second_section):
        return jnp.where(at_first, at_first_section, at_second_section)

    def back_to_first(array):
        return lax.ppermute(array, "section", [(1, 0)])

    def branch(on_first, on_second, *operands):
        def unwritten(run):
            return lambda *o: nothing(jax.eval_shape(run, *o))

        return lax.cond(
            at_first, on_first or unwritten(on_second), on_second or unwritten(on_first), *operands
        )

    edge_first = lax.ppermute(w_edge[0], "section", [(0, 1)])
    late_query, center0, dead = lax.optimization_barrier((w_query[0], center0, dead))
    (weights1,) = branch(
        None, lambda *o: (run_stack(o[:4], o[4]),), w_edge[0], late_query, w_key[0], w_value[0],
        edge_first,
    )
    weights1 = back_to_first(weights1)
    edge0 = pick(w_edge[0], edge_first)
    devices = lax.axis_size("dp")
    blocks = blocks_for(devices, width, ff)
    me = lax.axis_index("dp")
    core = (me & 1).astype(jnp.int32).reshape(1)

    def forward(edges, dead, center, dep):
        return tuple(run_forward(edges, dead, center, 0, params, consts, 0, micro, dep))

    def backward(*operands):
        return tuple(
            run_backward(*operands, params, consts, 0, micro, micro, blocks, None, True)
        )

    layer0 = branch(forward, None, edges0, dead, center0, ())
    new0, x0, p0, pe0, att0, q0, keys0, lse0, stat0 = layer0
    center1 = lax.ppermute(new0, "section", [(0, 1)])
    edges1 = run_edge_forward(edges0, edge0, new0)
    (cross,) = branch(lambda *o: (run_edge_cross(*o),), None, edges0, cot, edges1)
    weights1, cross = lax.optimization_barrier((weights1, cross))
    edge1 = pick(weights1[:width, :width], w_edge[0])
    joint = pick(mm(edge0, edge1).astype(BF16), edge1)
    cross_other = lax.ppermute(cross, "section", [(0, 1)])
    center_cot_rows, edges1 = lax.optimization_barrier(
        (center_cot.reshape(micro * pairs * 2, width), edges1)
    )

    layer1 = branch(
        None, lambda edges, dead, center, *deps: forward(edges, dead, center, deps),
        edges1, dead, center1, cross, weights1,
    )
    new1, x1, p1, pe1, att1, q1, keys1, lse1, stat1 = layer1
    new, stat = pick(new0, new1), pick(stat0, stat1)
    back1, sums1, dvals1, packed1, sent1, da1, ds1 = branch(
        None, backward, core, x1, p1, pe1, keys1, lse1, center1, q1, att1, center_cot_rows
    )
    back1_other, da1_other = back_to_first(back1), back_to_first(da1)
    sums1_other = back_to_first(sums1)

    (through,) = branch(lambda *o: (run_edge_forward(*o),), None, cot, joint.T, back1)
    early_edge, late_edge = branch(
        None, lambda *o: tuple(run_edge_weight(*o)), edges0, p1, ds1, keys1, dvals1, cross_other,
        edge0, edge1, through,
    )
    cut = micro - 1 if micro > 1 and pairs == 2 * HALF else micro

    def first_part(*operands):
        operands, deps = operands[:10], operands[10:]
        return tuple(
            run_backward(
                *operands, params, consts, 0, cut, micro, blocks, None, cut == micro, deps
            )
        )

    def last_part(*operands):
        operands, state, deps = operands[:10], operands[10:16], operands[16:-3]
        back, own_sums, dvals, packed, sent = run_backward(
            *operands, params, consts, cut, micro - cut, micro, blocks, state, True, deps
        )
        return back, packed, sent, own_sums, dvals

    def kept(*operands):
        like = jax.eval_shape(last_part, *operands)
        return (*operands[-3:], *nothing(like[3:]))

    own0 = (core, x0, p0, pe0, keys0, lse0, center0, q0, att0, back1_other)
    partial = branch(first_part, None, *own0, through, early_edge)
    early_other = back_to_first(early_edge)
    fits = sums_fit(devices, width)
    spot_of_sums = me if fits else jnp.full((), 2 * devices)
    late_me = jnp.concatenate([late, spot_of_sums.astype(jnp.int32).reshape(1)])
    edge_tiles = run_edge_tiles(late_me, early_other, late_edge, stat, partial[0])
    old = (back1, packed1, sent1)
    if cut == micro:
        back0, sums0, dvals0, packed0, sent0, da0 = partial[:6]
        back, packed, sent = branch(
            lambda *o: o[:3], lambda *o: o[3:], back0, packed0, sent0, *old
        )
        early_parts = [(sums0, dvals0)] * micro
    else:
        totals, vec, dq, dr, sums0, dvals0, packed0, da0 = partial
        back, packed, sent, last_sums, last_dvals = branch(
            last_part, kept, *own0, totals, vec, dq, dr, da0, packed0, da1_other, sums1_other,
            edge_tiles, *old,
        )
        early_parts = [(sums0, dvals0)] * cut + [(last_sums, last_dvals)]
    back, sent = lax.optimization_barrier((back, sent))
    edge_out = edges1
    edge_back = None
    steps, done = micro * pairs // HALF, 0

    def edge_piece(count, *deps):
        nonlocal edge_back, edge_out, done
        count = min(count, steps - done)
        if count:
            early_sums, early_dvals = early_parts[done * HALF // pairs]
            other = (new0, da1_other, weights1, sums1_other)
            tail = (*deps, edge_back) if done else deps

            def piece(early, grad, weights, edges, own, other, tail):
                so_far = tail[len(deps)] if done else None
                back = run_edge_backward(
                    done, count, so_far, early, grad, own, other, weights, consts,
                    tail[: len(deps)],
                )
                return back, edges if early else run_edge_act(edges, weights[1], done, count)

            edge_back, edge_out = lax.cond(
                at_first,
                lambda cot, through, edges, edge0, edge1, own0, own1, other, tail: piece(
                    True, through, [edge0], edges, own0, other, tail
                ),
                lambda cot, through, edges, edge0, edge1, own0, own1, other, tail: piece(
                    False, cot, [edge1, edge1], edges, own1, other, tail
                ),
                cot, through, edge_out, edge0, edge1, (x0, keys0, early_dvals, early_sums),
                (x1, keys1, dvals1, sums1), other, tail,
            )
            done += count

    stages = stages_of(devices)
    digits = [((me >> at) & ((1 << width_) - 1)).astype(jnp.int32) for at, width_ in stages]
    spot = jnp.zeros((), jnp.int32)
    for digit, (at, width_) in zip(digits, stages):
        spot = (spot << width_) | digit
    received = [swapped(sent, "dp", 1)]
    edges = (edge_tiles, swapped(edge_tiles, "dp", 1))
    edge_at = packed_tiles(width, ff) * (ROWS // 16) - blocks // 2
    held, hidden = packed, ()
    for (at, width_), digit in list(zip(stages, digits))[1:]:
        held, *sent = run_split(
            held, received, 1 << width_, jnp.stack([digit, digits[0]]), edges, edge_at, hidden
        )
        received = [swapped(part, "dp", (k + 1) << at) for k, part in enumerate(sent)]
        edge_piece(2, *sent)
        edges, edge_at, hidden = (), None, (edge_back,)
    (piece,) = run_split(held, received, 1, jnp.zeros((2,), jnp.int32), deps=hidden)
    for at, width_ in stages[:1:-1]:
        received = [swapped(piece, "dp", (k + 1) << at) for k in range((1 << width_) - 1)]
        edge_piece(2, piece)
        piece = run_join([piece, *received], (edge_back,))
    at, width_ = stages[1]
    own = [piece] + [swapped(piece, "dp", (k + 1) << at) for k in range((1 << width_) - 1)]
    other = [swapped(piece, "dp", 1)]
    edge_piece(steps, piece)
    *rest, edge_back, back, new = lax.optimization_barrier((*own[1:], edge_back, back, new))
    other += [swapped(part, "dp", 1) for part in rest]
    per = blocks // devices
    pieces = [part.reshape(-1, per, 16, LANES) for part in own + other]
    total = micro * pairs * 2 * devices
    *squares, up, down_t, edge_grad, dgain1, dbias1, dgain2, dbias2, stats = run_unpack(
        spot.reshape(1), pieces, width, ff, total
    )
    if not fits:
        means, squared = sum_small(stat, "dp") / total
        stats = jnp.stack([means, squared - means * means])[None]

    def matrix(array):
        return jnp.transpose(array, (1, 0, 2))

    shape = (1, micro, pairs, 2, width)

    return (
        new.reshape(shape),
        jnp.transpose(edge_out, (0, 2, 1, 3))[None],
        back.reshape(shape),
        jnp.transpose(edge_back, (0, 2, 1, 3))[None],
        *[matrix(square) for square in squares],
        dgain1,
        dbias1,
        matrix(up),
        jnp.transpose(down_t, (1, 2, 0)),
        dgain2,
        dbias2,
        matrix(edge_grad),
        stats,
    )


def solution(mesh):
    data4 = P(None, "dp", None, None)
    square = P("section", None, None)
    row = P("section", None)
    acts = P("section", None, "dp", None, None)
    return jax.shard_map(
        shards,
        mesh=mesh,
        in_specs=(
            data4, data4, P(None, "dp", None), data4,
            square, square, square, square, row, row, square, square, row, row, square,
            data4, data4,
        ),
        out_specs=(
            acts, acts, acts, acts,
            square, square, square, square, row, row, square, square, row, row, square,
            square,
        ),
        check_vma=False,
    )
```

```python
import functools
import math

import jax
import jax.numpy as jnp
import numpy as np
from jax import lax
from jax.experimental import pallas as pl
from jax.experimental.pallas import tpu as pltpu
from jax.sharding import PartitionSpec as P

HEADS = 12
EPS = 1e-05
BIG = 1e30
GROUP = 8
HALF = 2 * GROUP
LANES = 128
ROWS = 304
VMEM = 56 * 1024 * 1024

F32 = jnp.float32
BF16 = jnp.bfloat16


def mm(a, b):
    return lax.dot_general(a, b, (((1,), (0,)), ((), ())), preferred_element_type=F32)


def mm_nt(a, b):
    return lax.dot_general(a, b, (((1,), (1,)), ((), ())), preferred_element_type=F32)


def mm_tn(a, b):
    return lax.dot_general(a, b, (((0,), (0,)), ((), ())), preferred_element_type=F32)


def tiles_of(width):
    return -(-width // LANES)


def dead_lane(width):
    base = width - (tiles_of(width) - 1) * LANES
    return -(-(base + GROUP) // 8) * 8


def constants(width):
    rows = HEADS * HALF
    head = np.arange(rows) // HALF
    pair = (np.arange(rows) % HALF) // 2
    slot = np.arange(rows) % HALF
    head_width = width // HEADS
    own = (np.arange(width)[None, :] // head_width == head[:, None]).astype(np.float32)
    base = width - (tiles_of(width) - 1) * LANES
    dead = dead_lane(width)
    bias = np.zeros((rows, LANES), np.float32)
    for p in range(GROUP):
        bias[:, base + p] = np.where(pair == p, 0.0, -BIG)
    for s in range(HALF):
        bias[:, dead + s] = np.where(slot == s, -BIG, 0.0)
    one_hot = np.zeros((GROUP, LANES), np.float32)
    for p in range(GROUP):
        one_hot[p, base + p] = 1.0
    center = np.zeros((HALF, LANES), np.float32)
    for r in range(HALF):
        center[r, base + r // 2] = 1.0
        for s in range(HALF):
            center[r, dead + s] = float(s % 2 != r % 2)
    return (
        jnp.asarray(own, BF16),
        jnp.asarray(bias, BF16),
        jnp.asarray(one_hot, F32),
        jnp.asarray(center, BF16),
    )


def normalize(values):
    centred = values - jnp.mean(values, axis=-1, keepdims=True)
    inverse = lax.rsqrt(jnp.mean(centred * centred, axis=-1, keepdims=True) + EPS)
    return centred * inverse, inverse


def norm_back(grad, normed, inverse):
    return inverse * (
        grad
        - jnp.mean(grad, axis=-1, keepdims=True)
        - normed * jnp.mean(grad * normed, axis=-1, keepdims=True)
    )


GELU_C = math.sqrt(2.0 / math.pi)


def gelu_parts(x):
    square = x * x
    t = jnp.tanh(GELU_C * x * (1.0 + 0.044715 * square))
    return square, t


def expand(rows16, own):
    return jnp.concatenate([rows16] * HEADS, axis=0) * own


def fold_heads(values, own):
    masked = values * own.astype(F32)
    return jnp.sum(masked.reshape(HEADS, HALF, values.shape[-1]), axis=0)


def build_x(x_ref, slot, e_f32, dead_ref, one_hot_ref, featc_ref, c_rows, width):
    leaves = e_f32.shape[0]
    edge_rows = leaves * GROUP
    last = (tiles_of(width) - 1) * LANES
    place = dead_lane(width)
    rows = [jnp.zeros((place, LANES), F32)]
    rows.append(jnp.concatenate([dead_ref[slot], jnp.zeros((HALF, LANES - leaves), F32)], axis=1))
    rows.append(jnp.zeros((LANES - place - HALF, LANES), F32))
    dead = jnp.transpose(jnp.concatenate(rows, axis=0))[0:leaves]
    feature = dead[:, None, :] + one_hot_ref[...][None, :, :]
    x_ref[slot, 0:edge_rows, last : last + LANES] = feature.reshape(edge_rows, LANES).astype(BF16)
    part = e_f32[:, slot * GROUP : (slot + 1) * GROUP, :].reshape(edge_rows, width)
    x_ref[slot, 0:edge_rows, 0:width] = part.astype(BF16)
    x_ref[slot, edge_rows : edge_rows + HALF, last : last + LANES] = featc_ref[...]
    x_ref[slot, edge_rows : edge_rows + HALF, 0:width] = c_rows


def column_rows(columns):
    rows = columns[0].shape[0]
    lane = lax.broadcasted_iota(jnp.int32, (rows, LANES), 1)
    tile = jnp.zeros((rows, LANES), F32)
    for index, column in enumerate(columns):
        tile = jnp.where(lane == index, column, tile)
    return jnp.transpose(tile)[0 : len(columns)]


def forward_kernel(
    width,
    deps,
    e_ref,
    dead_ref,
    c_ref,
    wq_ref,
    wk_ref,
    wv_ref,
    wo_ref,
    gain1_ref,
    bias1_ref,
    wup_ref,
    wdt_ref,
    gain2_ref,
    bias2_ref,
    own_ref,
    qbias_ref,
    one_hot_ref,
    featc_ref,
    *rest,
):
    newc_ref, x_ref, p_ref, pe_ref, att_ref, q_ref, keys_ref, lse_ref, stat_ref, keys_s = rest[deps:]
    step = pl.program_id(0)
    scale = 1.0 / math.sqrt(width // HEADS)
    last = (tiles_of(width) - 1) * LANES
    slots = x_ref.shape[0]
    cols = HEADS * HALF

    @pl.when(step == 0)
    def _():
        q_ref[...] = mm(c_ref[...], wq_ref[...]).astype(BF16)
        for slot in range(slots):
            keys_s[slot, :, last : last + LANES] = qbias_ref[...]

    own = own_ref[...]
    base = pl.multiple_of(step * slots * HALF, slots * HALF)
    q_rows = q_ref[pl.ds(base, slots * HALF), :]
    q_all = jnp.concatenate(
        [expand(q_rows[s * HALF : (s + 1) * HALF], own) for s in range(slots)], axis=0
    )
    keys = (mm_nt(q_all, wk_ref[...]) * scale).astype(BF16)
    c_rows = c_ref[pl.ds(base, slots * HALF), :]
    e_f32 = e_ref[0].astype(F32)
    for slot in range(slots):
        keys_s[slot, :, 0:width] = keys[slot * cols : (slot + 1) * cols]
        keys_ref[slot] = keys[slot * cols : (slot + 1) * cols]
        build_x(
            x_ref, slot, e_f32, dead_ref, one_hot_ref, featc_ref,
            c_rows[slot * HALF : (slot + 1) * HALF], width,
        )
    scores = [mm_nt(keys_s[slot], x_ref[slot]) for slot in range(slots)]
    probs, logs = [], []
    for slot in range(slots):
        top = jnp.max(scores[slot], axis=1, keepdims=True)
        weights = jnp.exp(scores[slot] - top)
        total = jnp.sum(weights, axis=1, keepdims=True)
        probs.append((weights * (1.0 / total)).astype(BF16))
        logs.append(top + jnp.log(total))
    pes = []
    for slot in range(slots):
        p_ref[slot] = probs[slot]
        pe = mm(probs[slot], x_ref[slot])[:, 0:width].astype(BF16)
        pe_ref[slot] = pe
        pes.append(pe)
    lse_ref[0] = column_rows(logs)
    att = mm(jnp.concatenate(pes, axis=0), wv_ref[...])
    att = jnp.concatenate(
        [fold_heads(att[s * cols : (s + 1) * cols], own) for s in range(slots)], axis=0
    )
    att_ref[pl.ds(base, slots * HALF), :] = att.astype(BF16)

    @pl.when(step == pl.num_programs(0) - 1)
    def _():
        residual = c_ref[...].astype(F32) + mm(att_ref[...], wo_ref[...])
        z1, unused = normalize(residual)
        first = z1 * gain1_ref[...] + bias1_ref[...]
        hidden = mm(first.astype(BF16), wup_ref[...])
        unused, t = gelu_parts(hidden)
        gelu = (0.5 * hidden * (1.0 + t)).astype(BF16)
        z2, unused = normalize(first + mm_nt(gelu, wdt_ref[...]))
        new = (z2 * gain2_ref[...] + bias2_ref[...]).astype(BF16)
        newc_ref[...] = new
        new = new.astype(F32)
        stat_ref[0:1, :] = jnp.sum(new, axis=0, keepdims=True)
        stat_ref[1:2, :] = jnp.sum(new * new, axis=0, keepdims=True)


def whole(shape):
    zeros = (0,) * len(shape)
    return pl.BlockSpec(shape, lambda i, *unused: zeros)


def step_spec(shape, first=0):
    rest = (0,) * (len(shape) - 1)
    return pl.BlockSpec(shape, lambda i, *unused: (first + i,) + rest)


def part_spec(shape, part):
    return pl.BlockSpec(shape, lambda i, *unused: (part, 0))


ANY = pl.BlockSpec(memory_space=pl.ANY)


def run_forward(edges, dead, center, part, params, consts, first, micro, deps=()):
    unused, leaves, pairs, width = edges.shape
    slots = pairs // GROUP
    groups = micro * slots
    x_rows = leaves * GROUP + HALF
    pad = tiles_of(width) * LANES
    cols = HEADS * HALF
    count = groups * HALF
    operands = [
        params["query"], params["key"], params["value"], params["out"],
        params["gain1"], params["bias1"], params["up"], params["down_t"],
        params["gain2"], params["bias2"],
        *consts,
    ]
    return pl.pallas_call(
        functools.partial(forward_kernel, width, len(deps)),
        grid=(micro,),
        in_specs=[
            step_spec((1, leaves, pairs, width), first),
            step_spec((slots, HALF, leaves), first),
            part_spec((count, width), part),
        ]
        + [whole(o.shape) for o in operands]
        + [ANY] * len(deps),
        out_specs=[
            whole((count, width)),
            step_spec((slots, x_rows, pad)),
            step_spec((slots, cols, x_rows)),
            step_spec((slots, cols, width)),
            whole((count, width)),
            whole((count, width)),
            step_spec((slots, cols, width)),
            step_spec((1, slots, cols)),
            whole((2, width)),
        ],
        scratch_shapes=[pltpu.VMEM((slots, cols, pad), BF16)],
        out_shape=[
            jax.ShapeDtypeStruct((count, width), BF16),
            jax.ShapeDtypeStruct((groups, x_rows, pad), BF16),
            jax.ShapeDtypeStruct((groups, cols, x_rows), BF16),
            jax.ShapeDtypeStruct((groups, cols, width), BF16),
            jax.ShapeDtypeStruct((count, width), BF16),
            jax.ShapeDtypeStruct((count, width), BF16),
            jax.ShapeDtypeStruct((groups, cols, width), BF16),
            jax.ShapeDtypeStruct((micro, slots, cols), F32),
            jax.ShapeDtypeStruct((2, width), F32),
        ],
        compiler_params=pltpu.CompilerParams(vmem_limit_bytes=VMEM),
        cost_estimate=cost(10e-6),
        name="layer_forward",
    )(edges, dead, center, *operands, *deps)


def blocks_for(devices, width, ff):
    count = (packed_tiles(width, ff) + tiles_of(width)) * (ROWS // 16)
    return -(-count // devices) * devices


def packed_tiles(width, ff):
    return 4 * (width // LANES) + 2 * (ff // LANES) + 3


def placement(width, ff):
    full, wide = width // LANES, ff // LANES
    rest = 4 * full + 2 * wide
    narrow, broad = width - full * LANES, ff - wide * LANES
    return (
        (0, width, (rest, 0)),
        (full, width, (rest, narrow)),
        (2 * full, width, (rest + 1, 0)),
        (3 * full, width, (rest + 1, narrow)),
        (4 * full, ff, (rest + 2, 0)),
        (4 * full + wide, ff, (rest + 2, broad)),
        (rest + 3, width, (rest + 3 + full, 0)),
    )


SPOT = 64


def sums_fit(devices, width):
    return width % LANES <= SPOT and 4 * devices <= LANES - SPOT


def put_tile(packed_ref, tile, matrix):
    rows, lanes = matrix.shape
    full = matrix
    if rows < ROWS:
        full = jnp.concatenate([matrix, jnp.zeros((ROWS - rows, lanes), F32)], axis=0)
    if lanes < LANES:
        full = jnp.concatenate([full, jnp.zeros((ROWS, LANES - lanes), F32)], axis=1)
    per = ROWS // 16
    packed_ref[tile * per : (tile + 1) * per] = full.astype(BF16).reshape(per, 16, LANES)


def put_matrix(packed_ref, first_tile, matrix):
    full = matrix.shape[1] // LANES
    for tile in range(full):
        put_tile(packed_ref, first_tile + tile, matrix[:, tile * LANES : (tile + 1) * LANES])
    return matrix[:, full * LANES :]


def backward_kernel(
    width,
    deps,
    begin,
    end,
    first,
    core_ref,
    x_ref,
    p_ref,
    pe_ref,
    keys_ref,
    lse_ref,
    c_ref,
    q_ref,
    att_ref,
    dc_ref,
    wq_ref,
    wk_ref,
    wv_ref,
    wo_ref,
    gain1_ref,
    bias1_ref,
    wup_ref,
    wdt_ref,
    gain2_ref,
    bias2_ref,
    own_ref,
    *rest,
):
    rest = rest[deps:]
    if not begin:
        sums_in, vec_in, dq_in, dr_in, da_in, packed_in, *rest = rest
    if end:
        cback_ref, inner_ref, dvals_ref, packed_out_ref, sent_ref, *rest = rest
    else:
        sums_out, vec_out, dq_out, dr_out, inner_ref, dvals_ref, packed_out_ref, *rest = rest
    if begin:
        da_out, *rest = rest
    if begin and end:
        ds_ref, *rest = rest
    packed_ref, packed_sem, dvals_s, dwk_s, dwv_s, dwo_s, vec_s, dq_s, dr_s, da_s = rest
    count = c_ref.shape[0]
    step = pl.program_id(0)
    scale = 1.0 / math.sqrt(width // HEADS)
    last = (tiles_of(width) - 1) * LANES
    places = placement(width, wup_ref.shape[1])
    slots, x_rows, pad = x_ref.shape
    edge_rows = x_rows - HALF
    cols = HEADS * HALF

    @pl.when(step == 0)
    def _():
        for slot in range(slots):
            dvals_s[slot, :, last : last + LANES] = jnp.zeros((cols, LANES), BF16)
        if not begin:
            pltpu.make_async_copy(packed_in, packed_ref, packed_sem.at[0]).start()
            for total_ref, total in zip((dwk_s, dwv_s, dwo_s), (0, 1, 2)):
                total_ref[...] = sums_in[total]
            vec_s[...] = vec_in[...]
            dq_s[...] = dq_in[...]
            dr_s[...] = dr_in[...]
            da_s[...] = da_in[...]
            return
        dwk_s[...] = jnp.zeros_like(dwk_s)
        dwv_s[...] = jnp.zeros_like(dwv_s)
        att = att_ref[...]
        z1, inverse1 = normalize(c_ref[...].astype(F32) + mm(att, wo_ref[...]))
        first = z1 * gain1_ref[...] + bias1_ref[...]
        first_low = first.astype(BF16)
        hidden = mm(first_low, wup_ref[...])
        square, t = gelu_parts(hidden)
        gelu = (0.5 * hidden * (1.0 + t)).astype(BF16)
        z2, inverse2 = normalize(first + mm_nt(gelu, wdt_ref[...]))
        dc = dc_ref[0:count, :].astype(F32)
        dgain2 = jnp.sum(dc * z2, axis=0, keepdims=True)
        dbias2 = jnp.sum(dc, axis=0, keepdims=True)
        dr2 = norm_back(dc * gain2_ref[...], z2, inverse2)
        df = dr2.astype(BF16)
        down_rest = put_matrix(packed_ref, places[5][0], mm_tn(df, gelu))
        slope = 0.5 * (1.0 + t) + 0.5 * hidden * (1.0 - t * t) * GELU_C * (
            1.0 + 3.0 * 0.044715 * square
        )
        dh = (mm(df, wdt_ref[...]) * slope).astype(BF16)
        up_rest = put_matrix(packed_ref, places[4][0], mm_tn(first_low, dh))
        put_tile(packed_ref, places[4][2][0], jnp.concatenate([up_rest, down_rest], axis=1))
        dfirst = dr2 + mm_nt(dh, wup_ref[...])
        dgain1 = jnp.sum(dfirst * z1, axis=0, keepdims=True)
        dbias1 = jnp.sum(dfirst, axis=0, keepdims=True)
        dr1 = norm_back(dfirst * gain1_ref[...], z1, inverse1)
        dr_s[...] = dr1
        do = dr1.astype(BF16)
        dwo_s[...] = mm_tn(att, do)
        da_s[...] = mm_nt(do, wo_ref[...]).astype(BF16)
        da_out[...] = da_s[...]
        for index, vector in enumerate((dgain1, dbias1, dgain2, dbias2)):
            vec_s[index : index + 1, :] = vector
        if not end:
            pltpu.make_async_copy(packed_ref, packed_out_ref, packed_sem.at[0]).start()

    own = own_ref[...]
    base = pl.multiple_of((first + step) * slots * HALF, slots * HALF)

    def all_heads(ref):
        rows = ref[pl.ds(base, slots * HALF), :]
        return jnp.concatenate(
            [expand(rows[s * HALF : (s + 1) * HALF], own) for s in range(slots)], axis=0
        )

    q_all, da_all = all_heads(q_ref), all_heads(da_s)
    dvals = mm_nt(da_all, wv_ref[...]).astype(BF16)
    for slot in range(slots):
        dvals_s[slot, :, 0:width] = dvals[slot * cols : (slot + 1) * cols]
        dvals_ref[slot] = dvals[slot * cols : (slot + 1) * cols]
    dprobs = [mm_nt(dvals_s[slot], x_ref[slot]) for slot in range(slots)]
    dscores, inners = [], []
    for slot in range(slots):
        probs = p_ref[slot].astype(F32)
        inner = jnp.sum(probs * dprobs[slot], axis=1, keepdims=True)
        dscores.append((probs * (dprobs[slot] - inner)).astype(BF16))
        if begin and end:
            ds_ref[slot] = dscores[slot]
        inners.append(inner)
    inner_ref[0, 0] = lse_ref[0]
    inner_ref[1, 0] = column_rows(inners)
    dses, parts = [], []
    for slot in range(slots):
        dses.append(mm(dscores[slot], x_ref[slot])[:, 0:width].astype(BF16))
        span = slice(slot * cols, (slot + 1) * cols)
        parts.append(
            mm_tn(dscores[slot][:, edge_rows:], keys_ref[slot])
            + mm_tn(p_ref[slot, :, edge_rows:], dvals[span])
        )
    dse = jnp.concatenate(dses, axis=0)
    pe = pe_ref[...].reshape(slots * cols, width)
    dwk_s[...] += mm_tn(dse, q_all)
    dwv_s[...] += mm_tn(pe, da_all)
    dq = mm(dse, wk_ref[...])
    dq = jnp.concatenate(
        [fold_heads(dq[s * cols : (s + 1) * cols], own) for s in range(slots)], axis=0
    )
    dq_s[pl.ds(base, slots * HALF), :] = (dq * scale).astype(BF16)
    dr_s[pl.ds(base, slots * HALF), :] += jnp.concatenate(parts, axis=0)

    @pl.when(step == pl.num_programs(0) - 1)
    def _():
        if not end:
            for total, total_ref in enumerate((dwk_s, dwv_s, dwo_s)):
                sums_out[total] = total_ref[...]
            vec_out[...] = vec_s[...]
            dq_out[...] = dq_s[...]
            dr_out[...] = dr_s[...]
            pltpu.make_async_copy(packed_ref, packed_out_ref, packed_sem.at[0]).wait()
            return
        if not begin:
            pltpu.make_async_copy(packed_in, packed_ref, packed_sem.at[0]).wait()
        dq_all = dq_s[...]
        dwq = jnp.concatenate([mm_tn(c_ref[...], dq_all), vec_s[...]], axis=0)
        query_rest = put_matrix(packed_ref, places[0][0], dwq)
        key_rest = put_matrix(packed_ref, places[1][0], dwk_s[...] * scale)
        key_rest = jnp.concatenate([key_rest, jnp.zeros((4, key_rest.shape[1]), F32)], axis=0)
        put_tile(
            packed_ref, places[0][2][0], jnp.concatenate([query_rest, key_rest], axis=1)
        )
        value_rest = put_matrix(packed_ref, places[2][0], dwv_s[...])
        out_rest = put_matrix(packed_ref, places[3][0], dwo_s[...])
        put_tile(
            packed_ref, places[2][2][0], jnp.concatenate([value_rest, out_rest], axis=1)
        )
        copy = pltpu.make_async_copy(packed_ref, packed_out_ref, packed_sem.at[0])
        copy.start()
        size = sent_ref.shape[0]
        start = pl.multiple_of((1 - core_ref[0]) * size, size)
        copy_half = pltpu.make_async_copy(
            packed_ref.at[pl.ds(start, size)], sent_ref, packed_sem.at[1]
        )
        copy_half.start()
        cback_ref[...] = (dr_s[...] + mm_nt(dq_all, wq_ref[...])).astype(BF16)
        copy.wait()
        copy_half.wait()


def run_backward(
    core, x, p, pe, keys, lse, center, q, att, dc, params, consts, first, steps, micro, blocks, state,
    end, deps=(),
):
    groups, x_rows, pad = x.shape
    slots = groups // micro
    cols = p.shape[1]
    count, width = q.shape
    begin = state is None
    operands = [
        center, q, att, dc,
        params["query"], params["key"], params["value"], params["out"],
        params["gain1"], params["bias1"], params["up"], params["down_t"],
        params["gain2"], params["bias2"],
        consts[0],
    ]
    specs = [whole(o.shape) for o in operands]
    if not begin:
        for index in (2, 3, 7, 8, 9, 10, 11, 12, 13):
            specs[index] = ANY
    state = [] if begin else list(state)
    state_specs = [] if begin else [whole(o.shape) for o in state[:5]] + [ANY]
    packed = jax.ShapeDtypeStruct((blocks, 16, LANES), BF16)
    rows = jax.ShapeDtypeStruct((count, width), BF16)
    sums = jax.ShapeDtypeStruct((2, micro, slots, cols), F32)
    dvals = jax.ShapeDtypeStruct((groups, cols, width), BF16)
    kept = [
        (sums, pl.BlockSpec((2, 1, slots, cols), lambda i, core: (0, first + i, 0, 0))),
        (dvals, step_spec((slots, cols, width), first)),
        (packed, ANY),
    ]
    if end:
        half = jax.ShapeDtypeStruct((blocks // 2, 16, LANES), BF16)
        outs = [(rows, whole(rows.shape)), *kept, (half, ANY)]
    else:
        totals = [((3, width, width), F32), ((4, width), F32), ((count, width), BF16)]
        totals.append(((count, width), F32))
        outs = [(jax.ShapeDtypeStruct(shape, kind), whole(shape)) for shape, kind in totals] + kept
    if begin:
        outs.append((rows, whole(rows.shape)))
    if begin and end:
        dscores = jax.ShapeDtypeStruct((groups, cols, x_rows), BF16)
        outs.append((dscores, step_spec((slots, cols, x_rows))))
    inputs = [core, x, p, pe, keys, lse, *operands, *deps, *state]
    return pl.pallas_call(
        functools.partial(backward_kernel, width, len(deps), begin, end, first),
        grid_spec=pltpu.PrefetchScalarGridSpec(
            num_scalar_prefetch=1,
            grid=(steps,),
            in_specs=[
                step_spec((slots, x_rows, pad), first),
                step_spec((slots, cols, x_rows), first),
                step_spec((slots, cols, width), first),
                step_spec((slots, cols, width), first),
                step_spec((1, slots, cols), first),
            ]
            + specs
            + [ANY] * len(deps)
            + state_specs,
            out_specs=[spec for unused, spec in outs],
            scratch_shapes=[
                pltpu.VMEM((blocks, 16, LANES), BF16),
                pltpu.SemaphoreType.DMA((2,)),
                pltpu.VMEM((slots, cols, pad), BF16),
                pltpu.VMEM((width, width), F32),
                pltpu.VMEM((width, width), F32),
                pltpu.VMEM((width, width), F32),
                pltpu.VMEM((4, width), F32),
                pltpu.VMEM((count, width), BF16),
                pltpu.VMEM((count, width), F32),
                pltpu.VMEM((count, width), BF16),
            ],
        ),
        out_shape=[shape for shape, unused in outs],
        compiler_params=pltpu.CompilerParams(vmem_limit_bytes=VMEM),
        cost_estimate=cost(0.2e-6),
        name="layer_backward",
    )(*inputs)


def nothing(like):
    return tuple(
        pl.pallas_call(
            lambda *refs: None, out_specs=[ANY] * len(like), out_shape=list(like), name="nothing"
        )()
    )


def edge_forward_kernel(e_ref, w_ref, dep_ref, out_ref):
    unused, leaves, pairs, width = e_ref.shape
    rows = e_ref[0].reshape(leaves * pairs, width)
    out_ref[0] = mm(rows, w_ref[...]).astype(BF16).reshape(leaves, pairs, width)


def run_edge_forward(edges, weight, dep):
    micro, leaves, pairs, width = edges.shape
    cut = 2 if leaves % 2 == 0 else 1
    block = pl.BlockSpec((1, leaves // cut, pairs, width), lambda i: (i // cut, i % cut, 0, 0))
    return pl.pallas_call(
        edge_forward_kernel,
        grid=(micro * cut,),
        in_specs=[block, whole(weight.shape), pl.BlockSpec(memory_space=pl.ANY)],
        out_specs=block,
        out_shape=jax.ShapeDtypeStruct(edges.shape, BF16),
        compiler_params=pltpu.CompilerParams(vmem_limit_bytes=VMEM),
        cost_estimate=cost(13e-6),
        name="edge_forward",
    )(edges, weight, dep)


def edge_act_kernel(e_ref, w_ref, out_ref):
    unused, leaves, pairs, width = e_ref.shape
    act = mm(e_ref[0].reshape(leaves * pairs, width), w_ref[...])
    out_ref[0] = act.astype(BF16).reshape(leaves, pairs, width)


def run_edge_act(edges, weight, first, steps):
    micro, leaves, pairs, width = edges.shape
    per = pairs // HALF
    block = pl.BlockSpec(
        (1, leaves, HALF, width), lambda i: ((first + i) // per, 0, (first + i) % per, 0)
    )
    return pl.pallas_call(
        edge_act_kernel,
        grid=(steps,),
        in_specs=[block, whole(weight.shape)],
        out_specs=block,
        out_shape=jax.ShapeDtypeStruct(edges.shape, BF16),
        input_output_aliases={0: 0},
        compiler_params=pltpu.CompilerParams(vmem_limit_bytes=VMEM),
        cost_estimate=cost(2e-6 * steps),
        name="edge_act",
    )(edges, weight)


def edge_weight_kernel(
    width, e_ref, p_ref, ds_ref, keys_ref, dvals_ref, cross_ref, w0_ref, w1_ref, *rest
):
    early_ref, late_ref, out_ref = rest[-3:]
    slots, cols, unused = p_ref.shape
    leaves = e_ref.shape[1]
    edge_rows = leaves * GROUP

    @pl.when(pl.program_id(0) == 0)
    def _():
        out_ref[...] = jnp.zeros_like(out_ref)

    e_f32 = e_ref[0].astype(F32)
    dses, pes = [], []
    for slot in range(slots):
        part = e_f32[:, slot * GROUP : (slot + 1) * GROUP, :].reshape(edge_rows, width)
        part = part.astype(BF16)
        dses.append(mm(ds_ref[slot, :, 0:edge_rows], part).astype(BF16))
        pes.append(mm(p_ref[slot, :, 0:edge_rows], part).astype(BF16))
    flat = (slots * cols, width)
    out_ref[...] += mm_tn(jnp.concatenate(dses, axis=0), keys_ref[...].reshape(flat)) + mm_tn(
        jnp.concatenate(pes, axis=0), dvals_ref[...].reshape(flat)
    )

    @pl.when(pl.program_id(0) == pl.num_programs(0) - 1)
    def _():
        cross = cross_ref[...]
        early_ref[...] = (out_ref[...] + mm_nt(cross, w1_ref[...])).astype(BF16)
        late_ref[...] = mm_tn(w0_ref[...], cross).astype(BF16)


def run_edge_weight(edges, p, ds, keys, dvals, cross, w0, w1, *deps):
    micro, leaves, pairs, width = edges.shape
    groups, cols, x_rows = p.shape
    slots = groups // micro
    return pl.pallas_call(
        functools.partial(edge_weight_kernel, width),
        grid=(micro,),
        in_specs=[
            step_spec((1, leaves, pairs, width)),
            step_spec((slots, cols, x_rows)),
            step_spec((slots, cols, x_rows)),
            step_spec((slots, cols, width)),
            step_spec((slots, cols, width)),
        ]
        + [whole((width, width))] * 3
        + [ANY] * len(deps),
        out_specs=[whole((width, width))] * 2,
        out_shape=[jax.ShapeDtypeStruct((width, width), BF16)] * 2,
        scratch_shapes=[pltpu.VMEM((width, width), F32)],
        compiler_params=pltpu.CompilerParams(vmem_limit_bytes=VMEM),
        cost_estimate=cost(8e-6),
        name="edge_weight",
    )(edges, p, ds, keys, dvals, cross, w0, w1, *deps)


def edge_cross_kernel(e_ref, cot_ref, dep_ref, out_ref, total_ref):
    step = pl.program_id(0)
    unused, leaves, pairs, width = e_ref.shape
    flat = (leaves * pairs, width)

    @pl.when(step == 0)
    def _():
        total_ref[...] = jnp.zeros_like(total_ref)

    total_ref[...] += mm_tn(e_ref[0].reshape(flat), cot_ref[0].reshape(flat))

    @pl.when(step == pl.num_programs(0) - 1)
    def _():
        out_ref[...] = total_ref[...].astype(BF16)


def run_edge_cross(edges, cot, dep):
    micro, leaves, pairs, width = edges.shape
    cut = 2 if leaves % 2 == 0 else 1
    block = pl.BlockSpec((1, leaves // cut, pairs, width), lambda i: (i // cut, i % cut, 0, 0))
    return pl.pallas_call(
        edge_cross_kernel,
        grid=(micro * cut,),
        in_specs=[block, block, ANY],
        out_specs=whole((width, width)),
        out_shape=jax.ShapeDtypeStruct((width, width), BF16),
        scratch_shapes=[pltpu.VMEM((width, width), F32)],
        compiler_params=pltpu.CompilerParams(vmem_limit_bytes=VMEM),
        cost_estimate=cost(8e-6),
        name="edge_cross",
    )(edges, cot, dep)


def edge_backward_kernel(width, first, early, deps, *refs):
    if early:
        through_ref, x_ref, keys_ref, dvals_ref, own_sums_ref, *refs = refs
        c1_ref, rows1_ref, weights1_ref, sums_ref, w0_ref, own_ref, qbias_ref, *refs = refs
        out_ref, both_s, joint_s = refs[deps:]
    else:
        cot_ref, x_ref, keys_ref, dvals_ref, own_sums_ref, wc_ref, qbias_ref, *refs = refs
        out_ref, both_s = refs[deps:]
    step = pl.program_id(0)
    scale = 1.0 / math.sqrt(width // HEADS)
    last = (tiles_of(width) - 1) * LANES
    leaves = out_ref.shape[1]
    edge_rows = leaves * GROUP
    cols = HEADS * HALF

    @pl.when(step == 0)
    def _():
        for slot in range(2):
            for layer in range(2):
                both_s[slot, layer, :, last : last + LANES] = qbias_ref[...]
                both_s[slot, 2 + layer, :, last : last + LANES] = jnp.zeros((cols, LANES), BF16)

    base = pl.multiple_of((first + step) * HALF * 2, HALF * 2)
    half = ((first + step) % (own_sums_ref.shape[2] // 2)) * 2

    def attention_part(layers):
        parts = []
        count = layers * cols
        pad = both_s.shape[-1]
        for slot in range(2):
            x = x_ref[slot, 0:edge_rows, :]
            lse = own_sums_ref[0, 0, pl.ds(half + slot, 1), :]
            inner = own_sums_ref[1, 0, pl.ds(half + slot, 1), :]
            if layers == 2:
                lse = jnp.concatenate([lse, sums_ref[0, 0, pl.ds(half + slot, 1), :]], axis=1)
                inner = jnp.concatenate([inner, sums_ref[1, 0, pl.ds(half + slot, 1), :]], axis=1)
            if layers == 2:
                both = both_s[slot].reshape(2 * count, pad)
                product = mm_nt(x, both)
                probs = jnp.exp(jnp.minimum(product[:, 0:count] - lse, 0.0))
                dscores = probs * (product[:, count:] - inner)
                part = mm(
                    jnp.concatenate([dscores.astype(BF16), probs.astype(BF16)], axis=1), both
                )
            else:
                keys, dvals = both_s[slot, 0], both_s[slot, 2]
                probs = jnp.exp(jnp.minimum(mm_nt(x, keys) - lse, 0.0))
                dscores = probs * (mm_nt(x, dvals) - inner)
                part = mm(dscores.astype(BF16), keys) + mm(probs.astype(BF16), dvals)
            parts.append(part[:, 0:width])
        return parts

    def joined(parts):
        shaped = [part.reshape(leaves, GROUP, width) for part in parts]
        return jnp.concatenate(shaped, axis=1).reshape(leaves * HALF, width)

    for slot in range(2):
        both_s[slot, 0, :, 0:width] = keys_ref[slot]
        both_s[slot, 2, :, 0:width] = dvals_ref[slot]

    if not early:
        cot = cot_ref[0].reshape(leaves * HALF, width)
        grad = mm_nt(cot, wc_ref[...]) + joined(attention_part(1))
        out_ref[0] = grad.astype(BF16).reshape(leaves, HALF, width)
        return

    own = own_ref[...]
    stacked = weights1_ref.shape[0] // 4

    @pl.when(step == 0)
    def _():
        for index in range(2):
            at = (2 + index) * stacked
            other = weights1_ref[at : at + width, 0:width]
            joint_s[index] = mm(w0_ref[...], other).astype(BF16)

    def all_heads(rows):
        return jnp.concatenate([expand(rows[0:HALF], own), expand(rows[HALF:], own)], axis=0)

    w_query = weights1_ref[stacked : stacked + width, 0:width]
    q1 = mm(c1_ref[pl.ds(base, 2 * HALF), :], w_query).astype(BF16)
    da1 = rows1_ref[pl.ds(base, 2 * HALF), :]
    keys = (mm_nt(all_heads(q1), joint_s[0]) * scale).astype(BF16)
    dvals = mm_nt(all_heads(da1), joint_s[1]).astype(BF16)
    for slot in range(2):
        span = slice(slot * cols, (slot + 1) * cols)
        both_s[slot, 1, :, 0:width] = keys[span]
        both_s[slot, 3, :, 0:width] = dvals[span]
    through = through_ref[0].reshape(leaves * HALF, width)
    grad = through.astype(F32) + joined(attention_part(2))
    out_ref[0] = grad.astype(BF16).reshape(leaves, HALF, width)


def run_edge_backward(first, steps, so_far, early, grad, own, other, weights, consts, deps):
    micro, leaves, pairs, width = grad.shape
    per = pairs // HALF
    x, keys, dvals, sums = own
    groups, x_rows, pad = x.shape
    cols = HEADS * HALF
    slots = pairs // GROUP
    block = pl.BlockSpec(
        (1, leaves, HALF, width), lambda i: ((first + i) // per, 0, (first + i) % per, 0)
    )
    sums_spec = pl.BlockSpec((2, 1, slots, cols), lambda i: (0, (first + i) // per, 0, 0))
    operands = [*other[:3], *weights, consts[0], consts[1]] if early else [weights[0], consts[1]]
    specs = [whole(o.shape) for o in operands]
    scratch = [pltpu.VMEM((2, 4, cols, pad), BF16)]
    if early:
        operands.insert(3, other[3])
        specs.insert(3, sums_spec)
        scratch.append(pltpu.VMEM((2, width, width), BF16))
    extra = list(deps) + ([] if so_far is None else [so_far])
    inputs = [grad, x, keys, dvals, sums, *operands, *extra]
    return pl.pallas_call(
        functools.partial(edge_backward_kernel, width, first, early, len(extra)),
        grid=(steps,),
        in_specs=[
            block,
            step_spec((2, x_rows, pad), first),
            step_spec((2, cols, width), first),
            step_spec((2, cols, width), first),
            sums_spec,
        ]
        + specs
        + [ANY] * len(extra),
        out_specs=block,
        scratch_shapes=scratch,
        out_shape=jax.ShapeDtypeStruct(grad.shape, BF16),
        input_output_aliases={} if so_far is None else {len(inputs) - 1: 0},
        compiler_params=pltpu.CompilerParams(vmem_limit_bytes=VMEM),
        cost_estimate=cost(7e-6 * steps),
        name="edge_backward",
    )(*inputs)


def cost(seconds):
    return pl.CostEstimate(flops=int(seconds * 1e9), bytes_accessed=0, transcendentals=0)


def split_kernel(parts, recv_count, deps, edge_at, digit_ref, *refs):
    held_ref, *refs = refs
    recv_refs, refs = refs[:recv_count], refs[recv_count:]
    if edge_at is not None:
        edge_ref, edge_recv_ref, *refs = refs
    refs = refs[deps:]
    out_refs = refs
    size = held_ref.shape[0] // parts
    digit = digit_ref[0]
    for other, out_ref in enumerate(out_refs):
        span = pl.ds(pl.multiple_of((digit ^ other) * size, size), size)
        total = held_ref[span].astype(F32)
        for recv_ref in recv_refs:
            total = total + recv_ref[span].astype(F32)
        out_ref[...] = total.astype(BF16)
    if edge_at is not None:
        tiles = edge_ref.shape[0]
        for part in range(parts):
            low = max(edge_at, part * size)
            high = min(edge_at + tiles, (part + 1) * size)
            for other, out_ref in enumerate(out_refs):
                if low < high:

                    @pl.when((digit_ref[1] == 1) & ((digit ^ other) == part))
                    def _(low=low, high=high, part=part, out_ref=out_ref):
                        place = slice(low - part * size, high - part * size)
                        source = slice(low - edge_at, high - edge_at)
                        out_ref[place] = (
                            edge_ref[source].astype(F32) + edge_recv_ref[source].astype(F32)
                        ).astype(BF16)


def run_split(held, received, parts, digits, edges=(), edge_at=None, deps=()):
    count = held.shape[0] // 2 if edges else held.shape[0]
    size = count // parts
    inputs = [held, *received, *edges]

    def spec(array):
        return whole(array.shape)

    held_spec = pl.BlockSpec((count, 16, LANES), lambda i, digits: (digits[1], 0, 0))
    out_shape = [jax.ShapeDtypeStruct((size, 16, LANES), BF16)] * parts
    return pl.pallas_call(
        functools.partial(split_kernel, parts, len(received), len(deps), edge_at),
        grid_spec=pltpu.PrefetchScalarGridSpec(
            num_scalar_prefetch=1,
            grid=(1,),
            in_specs=[held_spec if edges else spec(held)]
            + [spec(array) for array in inputs[1:]]
            + [pl.BlockSpec(memory_space=pl.ANY)] * len(deps),
            out_specs=[spec(array) for array in out_shape],
        ),
        out_shape=out_shape,
        compiler_params=pltpu.CompilerParams(vmem_limit_bytes=VMEM),
        cost_estimate=cost(2e-6),
        name="split_gradients",
    )(digits, *inputs, *deps)


def join_kernel(count, deps, *refs):
    out_ref = refs[count + deps]
    size = refs[0].shape[0]
    for index in range(count):
        out_ref[index * size : (index + 1) * size] = refs[index][...]


def run_join(pieces, deps=()):
    size = pieces[0].shape[0]
    spec = pl.BlockSpec(memory_space=pltpu.VMEM)
    return pl.pallas_call(
        functools.partial(join_kernel, len(pieces), len(deps)),
        in_specs=[spec] * len(pieces) + [pl.BlockSpec(memory_space=pl.ANY)] * len(deps),
        out_specs=spec,
        out_shape=jax.ShapeDtypeStruct((size * len(pieces), 16, LANES), BF16),
        compiler_params=pltpu.CompilerParams(vmem_limit_bytes=VMEM),
        cost_estimate=cost(1e-6),
        name="join_gradients",
    )(*pieces, *deps)


def edge_tiles_kernel(late_ref, early_ref, late_edge_ref, sums_ref, dep_ref, out_ref):
    width = early_ref.shape[0]
    full = width // LANES
    edge = jnp.where(late_ref[0] == 1, late_edge_ref[...], early_ref[...]).astype(F32)
    over = put_matrix(out_ref, 0, edge)
    lane = lax.broadcasted_iota(jnp.int32, (LANES, width), 0) - SPOT - 4 * late_ref[1]
    table = jnp.zeros((LANES, width), F32)
    for index in range(2):
        row = sums_ref[index : index + 1, :]
        high = row.astype(BF16).astype(F32)
        table = jnp.where(lane == index, high, table)
        table = jnp.where(lane == 2 + index, row - high, table)
    columns = jnp.transpose(table)
    gap = jnp.zeros((width, LANES - over.shape[1]), F32)
    put_tile(out_ref, full, jnp.concatenate([over, gap], axis=1) + columns)


def run_edge_tiles(late_me, early_edge, late_edge, sums, dep):
    width = early_edge.shape[0]
    per = ROWS // 16
    vmem = pl.BlockSpec(memory_space=pltpu.VMEM)
    return pl.pallas_call(
        edge_tiles_kernel,
        in_specs=[pl.BlockSpec(memory_space=pltpu.SMEM), vmem, vmem, vmem, ANY],
        out_shape=jax.ShapeDtypeStruct((tiles_of(width) * per, 16, LANES), BF16),
        compiler_params=pltpu.CompilerParams(vmem_limit_bytes=VMEM),
        cost_estimate=cost(2e-6),
        name="edge_tiles",
    )(late_me, early_edge, late_edge, sums, dep)


def stack_kernel(*refs):
    *parts, dep_ref, out_ref = refs
    rows = out_ref.shape[0] // len(parts)
    for index, part in enumerate(parts):
        out_ref[index * rows : index * rows + part.shape[0], 0 : part.shape[1]] = part[...]


def run_stack(arrays, dep):
    rows, width = arrays[0].shape
    vmem = pl.BlockSpec(memory_space=pltpu.VMEM)
    shape = (len(arrays) * -(-rows // 16) * 16, tiles_of(width) * LANES)
    return pl.pallas_call(
        stack_kernel,
        in_specs=[vmem] * len(arrays) + [ANY],
        out_shape=jax.ShapeDtypeStruct(shape, BF16),
        compiler_params=pltpu.CompilerParams(vmem_limit_bytes=VMEM),
        cost_estimate=cost(1e-6),
        name="stack_weights",
    )(*arrays, dep)


def stages_of(devices):
    bits = devices.bit_length() - 1
    stages = [(0, 1)]
    if (bits - 1) % 2:
        stages.append((1, 1))
    at = sum(width for unused, width in stages)
    while at < bits:
        stages.append((at, 2))
        at += 2
    return stages


def unpack_kernel(width, ff, count, rows_summed, me_ref, *refs):
    sources, refs = refs[:count], refs[count:]
    total_ref = refs[-1]
    outs, vector_refs, stats_ref = refs[:7], refs[7:11], refs[11]
    me, at = me_ref[0], 0
    for source in sources:
        many, per = source.shape[0], source.shape[1]
        for index in range(many):
            start = pl.multiple_of((me ^ (at + index)) * per, per)
            total_ref[pl.ds(start, per)] = source[index]
        at += many
    rows = ROWS // 16

    def tile_at(tile):
        return total_ref[tile * rows : (tile + 1) * rows].reshape(ROWS, LANES).astype(F32)

    for (first, columns, (spot, lane)), ref in zip(placement(width, ff), outs):
        full = columns // LANES
        for tile in range(full):
            values = tile_at(first + tile)
            ref[:, 0, tile * LANES : (tile + 1) * LANES] = values[0:width]
            if first == 0:
                for row, vector_ref in enumerate(vector_refs):
                    vector_ref[:, tile * LANES : (tile + 1) * LANES] = values[
                        width + row : width + row + 1
                    ]
        values = tile_at(spot)[:, lane : lane + columns - full * LANES]
        ref[:, 0, full * LANES : columns] = values[0:width]
        if first == 0:
            for row, vector_ref in enumerate(vector_refs):
                vector_ref[:, full * LANES : columns] = values[width + row : width + row + 1]
    last = tile_at(placement(width, ff)[6][2][0])[0:width].astype(BF16)
    kind = lax.broadcasted_iota(jnp.int32, (16, LANES), 0)
    lane = lax.broadcasted_iota(jnp.int32, (16, LANES), 1)
    chosen = (lane >= SPOT) & (lane % 2 == kind)
    sums = mm_nt(chosen.astype(F32).astype(BF16), last) * (1.0 / rows_summed)
    stats_ref[0, 0:1, :] = sums[0:1]
    stats_ref[0, 1:2, :] = sums[1:2] - sums[0:1] * sums[0:1]


def run_unpack(me, pieces, width, ff, rows_summed):
    square = jax.ShapeDtypeStruct((width, 1, width), F32)
    wide = jax.ShapeDtypeStruct((width, 1, ff), F32)
    count = sum(piece.shape[0] * piece.shape[1] for piece in pieces)
    spec = pl.BlockSpec(memory_space=pltpu.VMEM)
    return pl.pallas_call(
        functools.partial(unpack_kernel, width, ff, len(pieces), rows_summed),
        in_specs=[pl.BlockSpec(memory_space=pltpu.SMEM)] + [spec] * len(pieces),
        out_shape=[square] * 4 + [wide] * 2 + [square]
        + [jax.ShapeDtypeStruct((1, width), F32)] * 4
        + [jax.ShapeDtypeStruct((1, 2, width), F32)],
        scratch_shapes=[pltpu.VMEM((count, 16, LANES), BF16)],
        compiler_params=pltpu.CompilerParams(vmem_limit_bytes=VMEM),
        name="unpack_gradients",
    )(me, *pieces)


def swapped(array, axis, bit):
    devices = lax.axis_size(axis)
    return lax.ppermute(array, axis, [(i, i ^ bit) for i in range(devices)])


def sum_small(array, axis):
    devices = lax.axis_size(axis)
    for k in range(devices.bit_length() - 1):
        array = array + swapped(array, axis, 1 << k)
    return array


def shards(
    center_input,
    edge_input,
    leaf_count,
    leaf_mask,
    w_query,
    w_key,
    w_value,
    w_out,
    gain_attn,
    bias_attn,
    w_up,
    w_down,
    gain_ffn,
    bias_ffn,
    w_edge,
    center_cot,
    edge_cot,
):
    micro, pairs, leaves, width = edge_input.shape
    ff = w_up.shape[-1]
    section = lax.axis_index("section")
    at_first = section == 0
    late = jnp.where(at_first, 0, 1).astype(jnp.int32).reshape(1)
    early = 1 - late
    consts = constants(width)
    params = {
        "query": w_query[0], "key": w_key[0], "value": w_value[0], "out": w_out[0],
        "gain1": gain_attn, "bias1": bias_attn,
        "up": w_up[0], "down_t": jnp.transpose(w_down[0]),
        "gain2": gain_ffn, "bias2": bias_ffn,
    }
    edges0 = jnp.transpose(edge_input, (0, 2, 1, 3))
    cot = jnp.transpose(edge_cot, (0, 2, 1, 3))
    center0 = center_input.reshape(micro * pairs * 2, width)

    slots = jnp.arange(leaves, dtype=jnp.int32)
    dead = jnp.where((slots < leaf_count[..., None]) & (leaf_mask == 1), 0.0, 1.0)
    dead = dead.reshape(micro * pairs // GROUP, HALF, leaves)

    def pick(at_first_section, at_second_section):
        return jnp.where(at_first, at_first_section, at_second_section)

    def back_to_first(array):
        return lax.ppermute(array, "section", [(1, 0)])

    def branch(on_first, on_second, *operands):
        def unwritten(run):
            return lambda *o: nothing(jax.eval_shape(run, *o))

        return lax.cond(
            at_first, on_first or unwritten(on_second), on_second or unwritten(on_first), *operands
        )

    edge_first = lax.ppermute(w_edge[0], "section", [(0, 1)])
    late_query, center0, dead = lax.optimization_barrier((w_query[0], center0, dead))
    (weights1,) = branch(
        None, lambda *o: (run_stack(o[:4], o[4]),), w_edge[0], late_query, w_key[0], w_value[0],
        edge_first,
    )
    weights1 = back_to_first(weights1)
    edge0 = pick(w_edge[0], edge_first)
    devices = lax.axis_size("dp")
    blocks = blocks_for(devices, width, ff)
    me = lax.axis_index("dp")
    core = (me & 1).astype(jnp.int32).reshape(1)

    def forward(edges, dead, center, dep):
        return tuple(run_forward(edges, dead, center, 0, params, consts, 0, micro, dep))

    def backward(*operands):
        return tuple(
            run_backward(*operands, params, consts, 0, micro, micro, blocks, None, True)
        )

    layer0 = branch(forward, None, edges0, dead, center0, ())
    new0, x0, p0, pe0, att0, q0, keys0, lse0, stat0 = layer0
    center1 = lax.ppermute(new0, "section", [(0, 1)])
    edges1 = run_edge_forward(edges0, edge0, new0)
    (cross,) = branch(lambda *o: (run_edge_cross(*o),), None, edges0, cot, edges1)
    weights1, cross = lax.optimization_barrier((weights1, cross))
    edge1 = pick(weights1[:width, :width], w_edge[0])
    joint = pick(mm(edge0, edge1).astype(BF16), edge1)
    cross_other = lax.ppermute(cross, "section", [(0, 1)])
    center_cot_rows, edges1 = lax.optimization_barrier(
        (center_cot.reshape(micro * pairs * 2, width), edges1)
    )

    layer1 = branch(
        None, lambda edges, dead, center, *deps: forward(edges, dead, center, deps),
        edges1, dead, center1, cross, weights1,
    )
    new1, x1, p1, pe1, att1, q1, keys1, lse1, stat1 = layer1
    new, stat = pick(new0, new1), pick(stat0, stat1)
    back1, sums1, dvals1, packed1, sent1, da1, ds1 = branch(
        None, backward, core, x1, p1, pe1, keys1, lse1, center1, q1, att1, center_cot_rows
    )
    back1_other = back_to_first(back1)

    (through,) = branch(lambda *o: (run_edge_forward(*o),), None, cot, joint.T, back1)
    early_edge, late_edge = branch(
        None, lambda *o: tuple(run_edge_weight(*o)), edges0, p1, ds1, keys1, dvals1, cross_other,
        edge0, edge1, through,
    )
    early_edge, sent_da1, sent_sums1 = lax.optimization_barrier((early_edge, da1, sums1))
    da1_other, sums1_other = back_to_first(sent_da1), back_to_first(sent_sums1)
    cut = micro - 1 if micro > 1 and pairs == 2 * HALF else micro

    def first_part(*operands):
        operands, deps = operands[:10], operands[10:]
        return tuple(
            run_backward(
                *operands, params, consts, 0, cut, micro, blocks, None, cut == micro, deps
            )
        )

    def last_part(*operands):
        operands, state, deps = operands[:10], operands[10:16], operands[16:-3]
        back, own_sums, dvals, packed, sent = run_backward(
            *operands, params, consts, cut, micro - cut, micro, blocks, state, True, deps
        )
        return back, packed, sent, own_sums, dvals

    def kept(*operands):
        like = jax.eval_shape(last_part, *operands)
        return (*operands[-3:], *nothing(like[3:]))

    own0 = (core, x0, p0, pe0, keys0, lse0, center0, q0, att0, back1_other)
    partial = branch(first_part, None, *own0, through, early_edge)
    early_other = back_to_first(early_edge)
    fits = sums_fit(devices, width)
    spot_of_sums = me if fits else jnp.full((), 2 * devices)
    late_me = jnp.concatenate([late, spot_of_sums.astype(jnp.int32).reshape(1)])
    edge_tiles = run_edge_tiles(late_me, early_other, late_edge, stat, partial[0])
    old = (back1, packed1, sent1)
    if cut == micro:
        back0, sums0, dvals0, packed0, sent0, da0 = partial[:6]
        back, packed, sent = branch(
            lambda *o: o[:3], lambda *o: o[3:], back0, packed0, sent0, *old
        )
        early_parts = [(sums0, dvals0)] * micro
    else:
        totals, vec, dq, dr, sums0, dvals0, packed0, da0 = partial
        back, packed, sent, last_sums, last_dvals = branch(
            last_part, kept, *own0, totals, vec, dq, dr, da0, packed0, da1_other, sums1_other,
            edge_tiles, *old,
        )
        early_parts = [(sums0, dvals0)] * cut + [(last_sums, last_dvals)]
    back, sent = lax.optimization_barrier((back, sent))
    edge_out = edges1
    edge_back = None
    steps, done = micro * pairs // HALF, 0

    def edge_piece(count, *deps):
        nonlocal edge_back, edge_out, done
        count = min(count, steps - done)
        if count:
            early_sums, early_dvals = early_parts[done * HALF // pairs]
            other = (new0, da1_other, weights1, sums1_other)
            tail = (*deps, edge_back) if done else deps

            def piece(early, grad, weights, edges, own, other, tail):
                so_far = tail[len(deps)] if done else None
                back = run_edge_backward(
                    done, count, so_far, early, grad, own, other, weights, consts,
                    tail[: len(deps)],
                )
                return back, edges if early else run_edge_act(edges, weights[1], done, count)

            edge_back, edge_out = lax.cond(
                at_first,
                lambda cot, through, edges, edge0, edge1, own0, own1, other, tail: piece(
                    True, through, [edge0], edges, own0, other, tail
                ),
                lambda cot, through, edges, edge0, edge1, own0, own1, other, tail: piece(
                    False, cot, [edge1, edge1], edges, own1, other, tail
                ),
                cot, through, edge_out, edge0, edge1, (x0, keys0, early_dvals, early_sums),
                (x1, keys1, dvals1, sums1), other, tail,
            )
            done += count

    stages = stages_of(devices)
    digits = [((me >> at) & ((1 << width_) - 1)).astype(jnp.int32) for at, width_ in stages]
    spot = jnp.zeros((), jnp.int32)
    for digit, (at, width_) in zip(digits, stages):
        spot = (spot << width_) | digit
    received = [swapped(sent, "dp", 1)]
    edges = (edge_tiles, swapped(edge_tiles, "dp", 1))
    edge_at = packed_tiles(width, ff) * (ROWS // 16) - blocks // 2
    held, hidden = packed, ()
    for (at, width_), digit in list(zip(stages, digits))[1:]:
        held, *sent = run_split(
            held, received, 1 << width_, jnp.stack([digit, digits[0]]), edges, edge_at, hidden
        )
        received = [swapped(part, "dp", (k + 1) << at) for k, part in enumerate(sent)]
        edge_piece(2, *sent)
        edges, edge_at, hidden = (), None, (edge_back,)
    (piece,) = run_split(held, received, 1, jnp.zeros((2,), jnp.int32), deps=hidden)
    for at, width_ in stages[:1:-1]:
        received = [swapped(piece, "dp", (k + 1) << at) for k in range((1 << width_) - 1)]
        edge_piece(2, piece)
        piece = run_join([piece, *received], (edge_back,))
    at, width_ = stages[1]
    own = [piece] + [swapped(piece, "dp", (k + 1) << at) for k in range((1 << width_) - 1)]
    other = [swapped(piece, "dp", 1)]
    edge_piece(steps, piece)
    *rest, edge_back, back, new = lax.optimization_barrier((*own[1:], edge_back, back, new))
    other += [swapped(part, "dp", 1) for part in rest]
    per = blocks // devices
    pieces = [part.reshape(-1, per, 16, LANES) for part in own + other]
    total = micro * pairs * 2 * devices
    *squares, up, down_t, edge_grad, dgain1, dbias1, dgain2, dbias2, stats = run_unpack(
        spot.reshape(1), pieces, width, ff, total
    )
    if not fits:
        means, squared = sum_small(stat, "dp") / total
        stats = jnp.stack([means, squared - means * means])[None]

    def matrix(array):
        return jnp.transpose(array, (1, 0, 2))

    shape = (1, micro, pairs, 2, width)

    return (
        new.reshape(shape),
        jnp.transpose(edge_out, (0, 2, 1, 3))[None],
        back.reshape(shape),
        jnp.transpose(edge_back, (0, 2, 1, 3))[None],
        *[matrix(square) for square in squares],
        dgain1,
        dbias1,
        matrix(up),
        jnp.transpose(down_t, (1, 2, 0)),
        dgain2,
        dbias2,
        matrix(edge_grad),
        stats,
    )


def solution(mesh):
    data4 = P(None, "dp", None, None)
    square = P("section", None, None)
    row = P("section", None)
    acts = P("section", None, "dp", None, None)
    return jax.shard_map(
        shards,
        mesh=mesh,
        in_specs=(
            data4, data4, P(None, "dp", None), data4,
            square, square, square, square, row, row, square, square, row, row, square,
            data4, data4,
        ),
        out_specs=(
            acts, acts, acts, acts,
            square, square, square, square, row, row, square, square, row, row, square,
            square,
        ),
        check_vma=False,
    )
```
